32 devices in a mesh: ctx: 8 (over y, x, core), fsdp: 4 (over z).
Axes of the slice: x: 2, y: 2, z: 4, core: 2. Of those that a mesh axis runs over, the one named last changes fastest.
Arguments:
- inputs: bfloat16 [4, 4096, 2560], P('fsdp', 'ctx'), may hold values from -6 to 6
- norm_gains: float32 [2, 2560], replicated, may hold values from 0.5 to 1.5
- q_weight: bfloat16 [2560, 2560], P('fsdp'), may hold values from -0.125 to 0.125
- kv_weight: bfloat16 [512, 2560], P('fsdp'), may hold values from -0.125 to 0.125
- o_weight: bfloat16 [2560, 2560], P('fsdp'), may hold values from -0.625 to 0.625
- gate_weight: bfloat16 [7680, 2560], P('fsdp'), may hold values from -0.125 to 0.125
- up_weight: bfloat16 [7680, 2560], P('fsdp'), may hold values from -0.125 to 0.125
- down_weight: bfloat16 [7680, 2560], P('fsdp'), may hold values from -0.0625 to 0.0625
- cotangent: bfloat16 [4, 4096, 2560], P('fsdp', 'ctx'), may hold values from -6 to 6
- doc_lengths: int32 [4, 4], P('fsdp'), may hold values from 1 to 3000, 4096 in all within a row
Outputs:
- output: bfloat16 [4, 4096, 2560], P('fsdp', 'ctx')
- input_grad: bfloat16 [4, 4096, 2560], P('fsdp', 'ctx')
- norm_gains_grad: float32 [2, 2560], P(None, 'ctx')
- q_grad: float32 [2560, 2560], P('fsdp', 'ctx')
- kv_grad: float32 [512, 2560], P('fsdp', 'ctx')
- o_grad: float32 [2560, 2560], P('fsdp', 'ctx')
- gate_grad: float32 [7680, 2560], P('fsdp', 'ctx')
- up_grad: float32 [7680, 2560], P('fsdp', 'ctx')
- down_grad: float32 [7680, 2560], P('fsdp', 'ctx')
The draws below stay inside these ranges and needn't reach their ends.
Inputs may be any that keep to these rules, and one draw needn't show every extreme that they name: `doc_lengths`: the lengths of each row sum to 4096; in each row the longest is exactly 3000.
All inputs are finite; a program needn't handle non-finite values.
Results may differ from the reference program's by a relative error of at most 0.02.
Values may be sent and summed in bfloat16 or wider, within the bound.
No kernel may reach another device: no remote copies, remote signals or barrier semaphores. Data moves between devices by JAX's collectives and lax.ppermute only.
A program may use at most 448 MiB of HBM per device.

```python
import math
import jax
import jax.numpy as jnp
import numpy as np
from jax import lax

D = 2560
HEADS = 10
HEAD = 256
FF = 7680
WINDOW = 2048
MAXDOC = 3000
LENGTH = 4096
SEQS = 4
DOCS = 4
HD = 2560


def shard_levels(rng, dims, shards, low, largest):
    factor_of = 1.0
    for dim, blocks in shards:
        draws = jax.random.uniform(jax.random.fold_in(jax.random.fold_in(rng, 6), dim), (blocks,), jnp.float32, low / len(shards), largest / len(shards))
        factor_of = factor_of * jnp.repeat(jnp.exp(draws), dims[dim] // blocks).reshape((-1,) + (1,) * (len(dims) - 1 - dim))
    return factor_of


def profile(amount, total, most, slope):
    portions = [(1 << 20) // math.isqrt(rank ** slope) + 1 for rank in range(2, amount + 1)]
    spare, given = total - most - (amount - 1), [1] * (amount - 1)
    while spare > 0:
        candidates = [i for i in range(amount - 1) if given[i] < most]
        whole, left = sum([portions[i] for i in candidates]), spare
        for i in candidates:
            addition = min(most - given[i], max(1, left * portions[i] // whole), spare)
            given[i] = given[i] + addition
            spare = spare - addition
    return np.array([most] + given)


def uneven(rng, count, total, most, lean):
    if count == 2:
        one = jax.random.randint(rng, (), max(1, total - most), min(most, total - 1) + 1)
        return jnp.stack([one, total - one])
    sizes = jnp.asarray(profile(count, total, most, lean), jnp.int32)
    twos = (count - 1) // 2
    giver, receiver = sizes[1:1 + 2 * twos:2], sizes[2:2 + 2 * twos:2]
    margin = jnp.minimum(giver - 1, most - receiver)
    moved = jax.random.randint(jax.random.fold_in(rng, 1), (twos,), 0, 1 << 20) % (margin + 1)
    sizes = sizes.at[1:1 + 2 * twos:2].set(giver - moved).at[2:2 + 2 * twos:2].set(receiver + moved)
    return sizes[jax.random.permutation(jax.random.fold_in(rng, 2), count)]


def normal_values(key, shape, width, limit, split=(), kind=jnp.bfloat16):
    gain = shard_levels(key, shape, split, -0.22, 0.18) if split else 1.0
    array = jax.random.normal(key, shape, jnp.float32) * width * gain
    return jnp.minimum(jnp.maximum(array, -limit), limit).astype(kind)


def setup_inputs(seed: int = 0) -> dict:
    key_of = jax.random.split(jax.random.key(seed), 11)
    return {
        "inputs": normal_values(key_of[0], (SEQS, LENGTH, D), 1.0, 6.0, ((0, 4), (1, 8))),
        "norm_gains": jnp.clip(1.0 + 0.1 * jax.random.normal(key_of[1], (2, D), jnp.float32), 0.5, 1.5),
        "q_weight": normal_values(key_of[2], (HD, D), D ** -0.5, 0.125, ((0, 4),)),
        "kv_weight": normal_values(key_of[3], (2 * HEAD, D), D ** -0.5, 0.125, ((0, 4),)),
        "o_weight": normal_values(key_of[4], (HD, D), (HD // 32) ** -0.5, 0.625, ((0, 4),)),
        "gate_weight": normal_values(key_of[5], (FF, D), D ** -0.5, 0.125, ((0, 4),)),
        "up_weight": normal_values(key_of[6], (FF, D), D ** -0.5, 0.125, ((0, 4),)),
        "down_weight": normal_values(key_of[7], (FF, D), FF ** -0.5, 0.0625, ((0, 4),)),
        "cotangent": normal_values(key_of[8], (SEQS, LENGTH, D), 1.0, 6.0, ((0, 4), (1, 8))),
        "doc_lengths": jax.vmap(lambda own: uneven(own, DOCS, LENGTH, MAXDOC, 1))(jax.random.split(key_of[9], SEQS)).reshape((SEQS, DOCS)).astype(jnp.int32),
    }


EPSILON = 1e-06
MASKED = -1e+30

@jax.custom_vjp
def low(v):
    return lax.optimization_barrier(v.astype(jnp.bfloat16)).astype(jnp.float32)

@jax.custom_vjp
def low_back(v):
    return v

def low_keep(v):
    return (low(v), None)

def low_pass(kept, grad):
    return (grad,)

def back_keep(v):
    return (v, None)

def back_low(kept, grad):
    return (low(grad),)
low.defvjp(low_keep, low_pass)
low_back.defvjp(back_keep, back_low)

def product_hi(left, right):
    return jnp.dot(left, right, precision=lax.Precision.HIGHEST, preferred_element_type=jnp.float32)

def doc_info(doc_lengths, first_token, token_count):
    doc_ends = jnp.cumsum(doc_lengths).astype(jnp.int32)
    doc_starts = doc_ends - doc_lengths
    token_ids = first_token + jnp.arange(token_count, dtype=jnp.int32)
    segment = lax.optimization_barrier(jnp.sum((doc_ends[None, :] <= token_ids[:, None]).astype(jnp.int32), 1)).astype(jnp.int32)
    begins = lax.optimization_barrier(jnp.max(jnp.where(doc_starts[None, :] <= token_ids[:, None], doc_starts[None, :], 0), 1))
    return (token_ids, segment, token_ids - begins)

def rope_angles(positions):
    half_width = HEAD // 2
    column = jnp.arange(half_width, dtype=jnp.float32)
    inverse = jnp.power(10000.0, -column / half_width)
    angles = positions.astype(jnp.float32)[:, None] * inverse[None, :]
    return (jnp.cos(angles), jnp.sin(angles))

def rotate(values, cosine, sine):
    half_width = values.shape[-1] // 2
    first_half = values[..., :half_width]
    second_half = values[..., half_width:]
    return jnp.concatenate([first_half * cosine - second_half * sine, second_half * cosine + first_half * sine], -1)

def attention(query_rot, key_rot, value_rows, segment):
    length = query_rot.shape[0]
    block_len = min(512, length)
    key_pad = jnp.concatenate([jnp.zeros((WINDOW, HEAD), jnp.float32), key_rot], 0)
    value_pad = jnp.concatenate([jnp.zeros((WINDOW, HEAD), jnp.float32), value_rows], 0)
    segment_pad = jnp.concatenate([jnp.full((WINDOW,), -1, jnp.int32), segment], 0)

    def one_block(block_index):
        first_row = block_index * block_len
        query_block = lax.dynamic_slice_in_dim(query_rot, first_row, block_len, 0)
        query_segment = lax.dynamic_slice_in_dim(segment, first_row, block_len, 0)
        key_block = lax.dynamic_slice_in_dim(key_pad, first_row, block_len + WINDOW, 0)
        value_block = lax.dynamic_slice_in_dim(value_pad, first_row, block_len + WINDOW, 0)
        key_segment = lax.dynamic_slice_in_dim(segment_pad, first_row, block_len + WINDOW, 0)
        query_ids = first_row + jnp.arange(block_len, dtype=jnp.int32)
        key_ids = first_row - WINDOW + jnp.arange(block_len + WINDOW, dtype=jnp.int32)
        offset = query_ids[:, None] - key_ids[None, :]
        allowed = (query_segment[:, None] == key_segment[None, :]) & (offset >= 0) & (offset < WINDOW)
        scores = low_back(jnp.einsum('qhd,kd->qhk', query_block, key_block, precision=lax.Precision.HIGHEST))
        masked = jnp.where(allowed[:, None, :], scores, MASKED)
        log_total = jax.nn.logsumexp(masked, -1, keepdims=True)
        probability = low(jnp.exp(masked - log_total))
        return jnp.einsum('qhk,kd->qhd', probability, value_block, precision=lax.Precision.HIGHEST)
    blocks = lax.map(jax.checkpoint(one_block), jnp.arange(length // block_len, dtype=jnp.int32))
    return blocks.reshape(length, HEADS, HEAD)

def forward(x_rows, norm_gains, q_weight, kv_weight, o_weight, gate_weight, up_weight, down_weight, segment, positions):
    length = x_rows.shape[0]
    scale_one = lax.rsqrt(lax.optimization_barrier(jnp.mean(x_rows * x_rows, -1, keepdims=True)) + EPSILON)
    normed_one = low(x_rows * scale_one * norm_gains[0])
    query_pre = low_back(product_hi(normed_one, q_weight.T))
    kv_pre = low_back(product_hi(normed_one, kv_weight.T))
    cosine, sine = rope_angles(positions)
    query_rot = low(rotate(query_pre.reshape(length, HEADS, HEAD), cosine[:, None, :], sine[:, None, :]) * HEAD ** (-0.5))
    key_rot = low(rotate(kv_pre[:, :HEAD], cosine, sine))
    value_rows = low(kv_pre[:, HEAD:])
    attended = attention(query_rot, key_rot, value_rows, segment)
    attn_rows = low_back(low(attended.reshape(length, HEADS * HEAD)))
    hidden_one = x_rows + low_back(product_hi(attn_rows, o_weight))
    scale_two = lax.rsqrt(lax.optimization_barrier(jnp.mean(hidden_one * hidden_one, -1, keepdims=True)) + EPSILON)
    normed_two = low(hidden_one * scale_two * norm_gains[1])
    gate_pre = low_back(product_hi(normed_two, gate_weight.T))
    up_pre = low_back(product_hi(normed_two, up_weight.T))
    mixed = low(jax.nn.gelu(gate_pre, approximate=True) * up_pre)
    return hidden_one + product_hi(mixed, down_weight)

def reference(inputs, norm_gains, q_weight, kv_weight, o_weight, gate_weight, up_weight, down_weight, cotangent, doc_lengths):
    weights = tuple((matrix.astype(jnp.float32) for matrix in (q_weight, kv_weight, o_weight, gate_weight, up_weight, down_weight)))

    def per_sequence(carried, sequence_item):
        rows_in, rows_cot, lengths_in = sequence_item
        token_ids, segment, positions = doc_info(lengths_in, jnp.int32(0), rows_in.shape[0])

        def local_forward(x_rows, gains, *matrices):
            return forward(x_rows, gains, *matrices, segment, positions)
        result, pull_back = jax.vjp(local_forward, rows_in.astype(jnp.float32), norm_gains, *weights)
        gradients = pull_back(rows_cot.astype(jnp.float32))
        updated = tuple((running + addend for running, addend in zip(carried, gradients[1:])))
        return (updated, (result.astype(jnp.bfloat16), gradients[0].astype(jnp.bfloat16)))
    initial = (jnp.zeros_like(norm_gains),) + tuple((jnp.zeros_like(matrix) for matrix in weights))
    totals, outputs = lax.scan(per_sequence, initial, (inputs, cotangent, doc_lengths))
    return (outputs[0], outputs[1], totals[0], totals[1], totals[2], totals[3], totals[4], totals[5], totals[6])
```

```python
import jax
import jax.numpy as jnp
from jax import lax
from jax.experimental import pallas as pl
from jax.experimental.pallas import tpu as pltpu
from jax.sharding import PartitionSpec as P

HEADS = 10
HEAD = 256
WINDOW = 2048


EPSILON = 1e-06
MASKED = -1e30
LOWEST = -1e29
VMEM = 56 * 1024 * 1024


def shifted(value, axis, steps):
    count = lax.axis_size(axis)
    initial, last = (max(0, -steps), min(count, count - steps))
    return lax.ppermute(value, axis, [(source, source + steps) for source in range(initial, last)])


def swap(value, axis, bit):
    return lax.ppermute(value, axis, [(i, i ^ bit) for i in range(lax.axis_size(axis))])


def add16(left, right):
    return (left.astype(jnp.float32) + right.astype(jnp.float32)).astype(jnp.bfloat16)


def times_rows(left, right):
    return lax.dot_general(
        left, right, (((1,), (1,)), ((), ())), preferred_element_type=jnp.float32
    )


def gram_rows(left, right):
    return lax.dot_general(
        left, right, (((0,), (0,)), ((), ())), preferred_element_type=jnp.float32
    )


def product(left, right):
    return jnp.dot(left, right, preferred_element_type=jnp.float32)


def doc_info(doc_lengths, first_token, token_count):
    doc_ends = jnp.cumsum(doc_lengths)
    doc_starts = doc_ends - doc_lengths
    token_ids = first_token + jnp.arange(token_count, dtype=jnp.int32)
    segment = jnp.sum((doc_ends[None, :] <= token_ids[:, None]).astype(jnp.int32), 1)
    begins = jnp.max(
        jnp.where(doc_starts[None, :] <= token_ids[:, None], doc_starts[None, :], 0), 1
    )
    return (token_ids, segment, token_ids - begins)


def rope_angles(positions):
    half_width = HEAD // 2
    column = jnp.arange(half_width, dtype=jnp.float32)
    inverse = jnp.power(10000.0, -column / half_width)
    angles = positions.astype(jnp.float32)[:, None] * inverse[None, :]
    return (jnp.cos(angles), jnp.sin(angles))


def rotate(values, cosine, sine):
    half_width = values.shape[-1] // 2
    first_half = values[..., :half_width]
    second_half = values[..., half_width:]
    return jnp.concatenate(
        [first_half * cosine - second_half * sine, second_half * cosine + first_half * sine], -1
    )


def rotate_back(grad_in, cosine, sine):
    half_width = grad_in.shape[-1] // 2
    first_half = grad_in[..., :half_width]
    second_half = grad_in[..., half_width:]
    return jnp.concatenate(
        [first_half * cosine + second_half * sine, second_half * cosine - first_half * sine], -1
    )


def norm_scale(values):
    return lax.rsqrt(jnp.mean(values * values, -1, keepdims=True) + EPSILON)


def norm_back(grad_in, values, scale, gain):
    weighted = grad_in * gain
    return scale * weighted - values * scale * scale * scale * jnp.mean(
        weighted * values, -1, keepdims=True
    )


def head_rows(block, count):
    return jnp.concatenate([block[:, h * HEAD : (h + 1) * HEAD] for h in range(count)], 0)


def row_bounds(low_ref, first_key, tokens, count):
    high = first_key + lax.broadcasted_iota(jnp.int32, (1, tokens), 1)
    low = low_ref[0]
    return jnp.concatenate([low] * count, 1), jnp.concatenate([high] * count, 1)


def seen(start, shape, low, high):
    key = start + lax.broadcasted_iota(jnp.int32, shape, 0)
    return (key >= low) & (key <= high)


def attend_kernel(
    span_ref, pre_ref, cos_ref, sin_ref, low_ref, key_ref, value_ref, out_ref, rot_ref, log_ref, acc, *, base, chunk
):
    tile = pl.program_id(0)
    tokens = pre_ref.shape[0]
    count = pre_ref.shape[1] // HEAD
    cosine, sine = cos_ref[...], sin_ref[...]
    half = HEAD // 2
    for h in range(count):
        first = pre_ref[:, h * HEAD : h * HEAD + half]
        second = pre_ref[:, h * HEAD + half : (h + 1) * HEAD]
        rot_ref[:, h * HEAD : h * HEAD + half] = (
            (first * cosine - second * sine) * HEAD ** (-0.5)
        ).astype(jnp.bfloat16)
        rot_ref[:, h * HEAD + half : (h + 1) * HEAD] = (
            (second * cosine + first * sine) * HEAD ** (-0.5)
        ).astype(jnp.bfloat16)
    query = head_rows(rot_ref[...], count)
    low, high = row_bounds(low_ref, base + tile * tokens, tokens, count)
    rows = count * tokens

    acc[...] = jnp.zeros_like(acc)

    def step(j, carry):
        top, total = carry
        start = pl.multiple_of(j * chunk, chunk)
        scores = lax.dot_general(
            key_ref[pl.ds(start, chunk), :], query, (((1,), (1,)), ((), ())),
            preferred_element_type=jnp.float32,
        )
        scores = jnp.where(seen(start, scores.shape, low, high), scores, MASKED)
        higher = jnp.maximum(top, jnp.max(scores, 0, keepdims=True))
        part = jnp.exp(scores - higher)
        shrink = jnp.exp(top - higher)
        acc[...] = acc[...] * shrink + lax.dot_general(
            value_ref[:, pl.ds(start, chunk)], part.astype(jnp.bfloat16), (((1,), (0,)), ((), ())),
            preferred_element_type=jnp.float32,
        )
        return higher, total * shrink + jnp.sum(part, 0, keepdims=True)

    top, total = lax.fori_loop(
        span_ref[0, tile], span_ref[1, tile], step,
        (jnp.full((1, rows), LOWEST, jnp.float32), jnp.zeros((1, rows), jnp.float32)),
    )
    log_ref[0, 0] = top + jnp.log(total)
    outs = (acc[...] * (1.0 / total)).T.astype(jnp.bfloat16)
    for h in range(count):
        out_ref[:, h * HEAD : (h + 1) * HEAD] = outs[h * tokens : (h + 1) * tokens]


def attend_back_kernel(
    span_ref, rot_ref, grad_ref, out_ref, log_ref, cos_ref, sin_ref, low_ref, key_ref, value_ref, key_t_ref,
    pre_ref, grad_key_ref, grad_value_ref, acc, *, base, chunk
):
    tile = pl.program_id(0)
    tokens = rot_ref.shape[0]
    count = rot_ref.shape[1] // HEAD

    @pl.when((tile == 0) & (pl.program_id(1) == 0))
    def _():
        grad_key_ref[...] = jnp.zeros_like(grad_key_ref)
        grad_value_ref[...] = jnp.zeros_like(grad_value_ref)

    query = head_rows(rot_ref[...], count)
    grad = head_rows(grad_ref[...], count)
    outs = head_rows(out_ref[...], count)
    delta = jnp.sum((grad.astype(jnp.float32) * outs.astype(jnp.float32)).T, 0, keepdims=True)
    log_total = log_ref[0, 0]
    low, high = row_bounds(low_ref, base + tile * tokens, tokens, count)
    acc[...] = jnp.zeros_like(acc)

    def step(j, carry):
        start = pl.multiple_of(j * chunk, chunk)
        here = pl.ds(start, chunk)
        scores = lax.dot_general(
            key_ref[here, :], query, (((1,), (1,)), ((), ())), preferred_element_type=jnp.float32
        )
        grad_probs = lax.dot_general(
            value_ref[here, :], grad, (((1,), (1,)), ((), ())), preferred_element_type=jnp.float32
        )
        probs = jnp.where(seen(start, scores.shape, low, high), jnp.exp(scores - log_total), 0.0)
        grad_scores = (probs * (grad_probs - delta)).astype(jnp.bfloat16)
        grad_value_ref[here, :] += jnp.dot(
            probs.astype(jnp.bfloat16), grad, preferred_element_type=jnp.float32
        )
        grad_key_ref[here, :] += jnp.dot(grad_scores, query, preferred_element_type=jnp.float32)
        acc[...] += lax.dot_general(
            key_t_ref[:, here], grad_scores, (((1,), (0,)), ((), ())),
            preferred_element_type=jnp.float32,
        )
        return carry

    lax.fori_loop(span_ref[0, tile], span_ref[1, tile], step, 0)
    grad_rot = acc[...].T * HEAD ** (-0.5)
    cosine, sine = cos_ref[...], sin_ref[...]
    half = HEAD // 2
    for h in range(count):
        own = grad_rot[h * tokens : (h + 1) * tokens]
        first, second = own[:, :half], own[:, half:]
        pre_ref[:, h * HEAD : h * HEAD + half] = (first * cosine + second * sine).astype(jnp.bfloat16)
        pre_ref[:, h * HEAD + half : (h + 1) * HEAD] = (second * cosine - first * sine).astype(
            jnp.bfloat16
        )


def attention_plan(tok_rows, key_count, low):
    tile = min(128, tok_rows)
    chunk = 256 if key_count % 256 == 0 else 128
    base = key_count - tok_rows
    tiles = tok_rows // tile
    begin = low[::tile] // chunk
    end = (base + (jnp.arange(tiles, dtype=jnp.int32) + 1) * tile + chunk - 1) // chunk
    return tile, chunk, base, jnp.stack([begin, end], 0).astype(jnp.int32)


GROUP = 10


def attend(query_pre, cosine, sine, low, keys, values_t):
    tok_rows = query_pre.shape[0]
    key_count = keys.shape[0]
    tile, chunk, base, span = attention_plan(tok_rows, key_count, low)
    tiles = tok_rows // tile
    groups = HEADS // GROUP
    wide = GROUP * HEAD
    block = pl.BlockSpec((tile, wide), lambda i, g, s: (i, g))
    angle = pl.BlockSpec((tile, HEAD // 2), lambda i, g, s: (i, 0))
    return pl.pallas_call(
        lambda *refs: attend_kernel(*refs, base=base, chunk=chunk),
        grid_spec=pltpu.PrefetchScalarGridSpec(
            num_scalar_prefetch=1,
            grid=(tiles, groups),
            in_specs=[
                block,
                angle,
                angle,
                pl.BlockSpec((1, 1, tile), lambda i, g, s: (i, 0, 0)),
                pl.BlockSpec((key_count, HEAD), lambda i, g, s: (0, 0)),
                pl.BlockSpec((HEAD, key_count), lambda i, g, s: (0, 0)),
            ],
            out_specs=[
                block,
                block,
                pl.BlockSpec((1, 1, 1, GROUP * tile), lambda i, g, s: (i, g, 0, 0)),
            ],
            scratch_shapes=[pltpu.VMEM((HEAD, GROUP * tile), jnp.float32)],
        ),
        out_shape=[
            jax.ShapeDtypeStruct(query_pre.shape, jnp.bfloat16),
            jax.ShapeDtypeStruct(query_pre.shape, jnp.bfloat16),
            jax.ShapeDtypeStruct((tiles, groups, 1, GROUP * tile), jnp.float32),
        ],
        compiler_params=pltpu.CompilerParams(vmem_limit_bytes=VMEM),
        name="attend",
    )(span, query_pre, cosine, sine, low.reshape(tiles, 1, tile), keys, values_t)


def attend_back(query_rot, grad_rows, attn_rows, log_total, cosine, sine, low, keys, values, keys_t):
    tok_rows = query_rot.shape[0]
    key_count = keys.shape[0]
    tile, chunk, base, span = attention_plan(tok_rows, key_count, low)
    tiles = tok_rows // tile
    groups = HEADS // GROUP
    wide = GROUP * HEAD
    block = pl.BlockSpec((tile, wide), lambda i, g, s: (i, g))
    angle = pl.BlockSpec((tile, HEAD // 2), lambda i, g, s: (i, 0))
    window = pl.BlockSpec((key_count, HEAD), lambda i, g, s: (0, 0))
    return pl.pallas_call(
        lambda *refs: attend_back_kernel(*refs, base=base, chunk=chunk),
        grid_spec=pltpu.PrefetchScalarGridSpec(
            num_scalar_prefetch=1,
            grid=(tiles, groups),
            in_specs=[
                block,
                block,
                block,
                pl.BlockSpec((1, 1, 1, GROUP * tile), lambda i, g, s: (i, g, 0, 0)),
                angle,
                angle,
                pl.BlockSpec((1, 1, tile), lambda i, g, s: (i, 0, 0)),
                window,
                window,
                pl.BlockSpec((HEAD, key_count), lambda i, g, s: (0, 0)),
            ],
            out_specs=[block, window, window],
            scratch_shapes=[pltpu.VMEM((HEAD, GROUP * tile), jnp.float32)],
        ),
        out_shape=[
            jax.ShapeDtypeStruct(query_rot.shape, jnp.bfloat16),
            jax.ShapeDtypeStruct((key_count, HEAD), jnp.float32),
            jax.ShapeDtypeStruct((key_count, HEAD), jnp.float32),
        ],
        compiler_params=pltpu.CompilerParams(vmem_limit_bytes=VMEM),
        name="attend_back",
    )(
        span, query_rot, grad_rows, attn_rows, log_total, cosine, sine, low.reshape(tiles, 1, tile),
        keys, values, keys_t,
    )


def nt(left, right):
    return lax.dot_general(
        left, right, (((1,), (1,)), ((), ())), preferred_element_type=jnp.float32
    )


def units_kernel(normed_ref, cot_ref, gate_ref, up_ref, down_ref, *refs):
    grad_gate_ref, grad_up_ref, mixed_ref = refs[-3:]
    gate = nt(gate_ref[...], normed_ref[...])
    up = nt(up_ref[...], normed_ref[...])
    grad_mixed = nt(down_ref[...], cot_ref[...])
    root = (2.0 / jnp.pi) ** 0.5
    square = gate * gate
    curve = jnp.tanh(root * (gate + 0.044715 * (square * gate)))
    upper = 0.5 * (1.0 + curve)
    activated = gate * upper
    slope = upper + 0.5 * gate * (1.0 - curve * curve) * (root * (1.0 + 0.134145 * square))
    mixed_ref[...] = (activated * up).astype(jnp.bfloat16)
    grad_up_ref[...] = (grad_mixed * activated).astype(jnp.bfloat16)
    grad_gate_ref[...] = (grad_mixed * up * slope).astype(jnp.bfloat16)


def units(normed, cot, weights, group, held):
    tokens, width = normed.shape
    hidden = weights[0].shape[0]
    cols = min(512, tokens)
    rows = hidden // 2
    first = group * (tokens // cols)
    token_block = pl.BlockSpec((cols, width), lambda i, j: (j, 0))
    weight_block = pl.BlockSpec((rows, width), lambda i, j: (i, 0))
    out_block = pl.BlockSpec((rows, cols), lambda i, j: (i, first + j))
    shape = jax.ShapeDtypeStruct((hidden, 2 * tokens), jnp.bfloat16)
    extra = () if held is None else tuple(held)
    return pl.pallas_call(
        units_kernel,
        grid=(hidden // rows, tokens // cols),
        in_specs=[token_block, token_block, weight_block, weight_block, weight_block]
        + [pl.BlockSpec(memory_space=pl.ANY)] * len(extra),
        out_specs=[out_block] * 3,
        out_shape=[shape] * 3,
        input_output_aliases={5 + i: i for i in range(len(extra))},
        compiler_params=pltpu.CompilerParams(vmem_limit_bytes=VMEM),
        name="units",
    )(normed, cot, *weights, *extra)


def grams_kernel(left_ref, near_ref, far_ref, out_ref):
    tokens = near_ref.shape[0]
    left = left_ref[...]
    out_ref[0] = (
        jnp.dot(left[:, :tokens], near_ref[...], preferred_element_type=jnp.float32)
        + jnp.dot(left[:, tokens:], far_ref[...], preferred_element_type=jnp.float32)
    ).astype(jnp.bfloat16)


def grams(left, near, far, pairs):
    rows, all_tokens = left.shape
    tokens, width = near.shape
    cols = width // pairs
    if cols % 128:
        whole = product(left[:, :tokens], near) + product(left[:, tokens:], far)
        return whole.astype(jnp.bfloat16).reshape(rows, pairs, cols).transpose(1, 0, 2)
    part = rows // 2
    token_block = pl.BlockSpec((tokens, cols), lambda i, j: (0, j))
    return pl.pallas_call(
        grams_kernel,
        grid=(2, pairs),
        in_specs=[pl.BlockSpec((part, all_tokens), lambda i, j: (i, 0)), token_block, token_block],
        out_specs=pl.BlockSpec((1, part, cols), lambda i, j: (j, i, 0)),
        out_shape=jax.ShapeDtypeStruct((pairs, rows, cols), jnp.bfloat16),
        compiler_params=pltpu.CompilerParams(vmem_limit_bytes=VMEM),
        name="grams",
    )(left, near, far)


def swap(value, axis, bit):
    return lax.ppermute(value, axis, [(i, i ^ bit) for i in range(lax.axis_size(axis))])


def same_core():
    count = lax.axis_size("ctx")
    return [list(range(0, count, 2)), list(range(1, count, 2))]


def swap_sum(value):
    for axis in ("ctx", "fsdp"):
        bit = 1
        while bit < lax.axis_size(axis):
            value = value + swap(value, axis, bit)
            bit = 2 * bit
    return value


def own_part(shard, place):
    part = shard.shape[0] // lax.axis_size("ctx")
    return lax.dynamic_slice_in_dim(shard, place * part, part, 0)


def in_order(gathered, first, part):
    mine = gathered[:, :, first : first + part].transpose(1, 0, 2, 3)
    return mine.reshape(-1, gathered.shape[-1])


def body(
    inputs,
    norm_gains,
    q_weight,
    kv_weight,
    o_weight,
    gate_weight,
    up_weight,
    down_weight,
    cotangent,
    doc_lengths,
):
    x_rows = inputs[0].astype(jnp.float32)
    grad_out = cotangent[0]
    tok_rows, width = x_rows.shape
    place = lax.axis_index("ctx")
    ctx_count = lax.axis_size("ctx")
    pairs = ctx_count // 2
    core = place % 2
    pair = place // 2
    fsdp_count = lax.axis_size("fsdp")
    reach = min(ctx_count - 1, (WINDOW + tok_rows - 2) // tok_rows)
    key_count = (reach + 1) * tok_rows
    first_token = place * tok_rows
    token_ids, segment, positions = doc_info(doc_lengths[0], first_token, tok_rows)
    low = jnp.maximum(token_ids - positions, token_ids - (WINDOW - 1)) - (
        first_token - reach * tok_rows
    )
    cosine, sine = rope_angles(positions)
    gain_attn = norm_gains[0]
    gain_mlp = norm_gains[1]

    q_part, kv_part, o_part = (own_part(w, place) for w in (q_weight, kv_weight, o_weight))
    q_rows, kv_rows = q_part.shape[0], kv_part.shape[0]
    over_z = lax.all_gather(jnp.concatenate([q_part, kv_part], 0), "fsdp", axis=0)
    over_all = lax.all_gather(over_z, "ctx", axis=0)
    q_full = in_order(over_all, 0, q_rows)
    kv_full = in_order(over_all, q_rows, kv_rows)
    o_z = lax.all_gather(o_part, "fsdp", axis=0)
    o_full = in_order(lax.all_gather(o_z, "ctx", axis=0), 0, o_part.shape[0])

    half_rows = gate_weight.shape[0] // 2
    part_rows = half_rows // pairs

    def own_half(weight):
        return lax.dynamic_slice_in_dim(weight, core * half_rows, half_rows, 0)

    def far_half(weight):
        mine = lax.dynamic_slice_in_dim(weight, core * half_rows + pair * part_rows, part_rows, 0)
        return lax.all_gather(
            swap(mine, "fsdp", 2), "ctx", axis=0, tiled=True, axis_index_groups=same_core()
        )

    weights = [
        tuple(own_half(w) for w in (gate_weight, up_weight, down_weight)),
        tuple(far_half(w) for w in (gate_weight, up_weight, down_weight)),
    ]

    def token_groups(rows):
        near = jnp.concatenate([rows, swap(rows, "ctx", 1)], 0)
        across = swap(rows, "fsdp", 1)
        far = jnp.concatenate([across, swap(across, "ctx", 1)], 0)
        return [near, far]

    cot_groups = token_groups(grad_out)

    scale_one = norm_scale(x_rows)
    normed_one = (x_rows * scale_one * gain_attn).astype(jnp.bfloat16)
    kv_pre = times_rows(normed_one, kv_full)
    key_rot = rotate(kv_pre[:, :HEAD], cosine, sine).astype(jnp.bfloat16)
    kv_local = jnp.concatenate([key_rot, kv_pre[:, HEAD:].astype(jnp.bfloat16)], 1)
    kv_window = jnp.concatenate(
        [shifted(kv_local, "ctx", hop) for hop in range(reach, 0, -1)] + [kv_local], 0
    )
    query_pre = times_rows(normed_one, q_full)
    keys, values = kv_window[:, :HEAD], kv_window[:, HEAD:]
    attn_rows, query_rot, log_total = attend(query_pre, cosine, sine, low, keys, values.T)
    hidden_one = x_rows + product(attn_rows, o_full)
    scale_two = norm_scale(hidden_one)
    normed_two = (hidden_one * scale_two * gain_mlp).astype(jnp.bfloat16)

    normed_groups = token_groups(normed_two)
    acts = []
    for h in (0, 1):
        held = None
        for g in (0, 1):
            held = units(normed_groups[g], cot_groups[g], weights[h], g, held)
        acts.append(held)

    def group_sum(g, which):
        total = 0.0
        for h in (0, 1):
            for act, weight in which:
                total = total + gram_rows(
                    acts[h][act][:, g * 2 * tok_rows : (g + 1) * 2 * tok_rows], weights[h][weight]
                )
        return total.astype(jnp.bfloat16)

    def groups_scatter(near, far):
        across = swap(add16(far[:tok_rows], swap(far[tok_rows:], "ctx", 1)), "fsdp", 1)
        return (
            near[:tok_rows].astype(jnp.float32)
            + swap(near[tok_rows:], "ctx", 1).astype(jnp.float32)
            + across.astype(jnp.float32)
        )

    back = ((0, 0), (1, 1))
    far_back = group_sum(1, back)
    near_back = group_sum(0, back)
    grad_normed_two = groups_scatter(near_back, far_back)
    mlp_out = groups_scatter(group_sum(0, ((2, 2),)), group_sum(1, ((2, 2),)))
    result = hidden_one + mlp_out

    pair_cols = width // pairs
    out_cols = width // ctx_count

    def over_pairs(blocks):
        return lax.psum_scatter(
            blocks, "ctx", scatter_dimension=0, tiled=False, axis_index_groups=same_core()
        )

    def both_halves(mine):
        rows = mine.shape[0]
        keep = lax.dynamic_slice_in_dim(mine, core * out_cols, out_cols, 1)
        give = lax.dynamic_slice_in_dim(mine, (1 - core) * out_cols, out_cols, 1)
        got = swap(give.astype(jnp.bfloat16), "ctx", 1).astype(jnp.float32)
        lower = jnp.where(core == 0, keep, got)
        upper = jnp.where(core == 0, got, keep)
        return jnp.concatenate([lower, upper], 0)

    mlp_grads = []
    for which, groups in ((0, normed_groups), (1, normed_groups), (2, cot_groups)):
        own = over_pairs(grams(acts[0][which], groups[0], groups[1], pairs))
        far = swap(over_pairs(grams(acts[1][which], groups[0], groups[1], pairs)), "fsdp", 2)
        mlp_grads.append(both_halves(own.astype(jnp.float32) + far.astype(jnp.float32)))

    grad_hidden = grad_out.astype(jnp.float32) + norm_back(
        grad_normed_two, hidden_one, scale_two, gain_mlp
    )
    gain_mlp_grad = jnp.sum(grad_normed_two * hidden_one * scale_two, 0)
    grad_branch = grad_hidden.astype(jnp.bfloat16)
    grad_attended = times_rows(grad_branch, o_full).astype(jnp.bfloat16)

    def attn_weight_grads(lefts, right):
        keeps, gives = [], []
        for left in lefts:
            rows = left.shape[1] // fsdp_count // 2
            whole = gram_rows(left, right).astype(jnp.bfloat16)
            whole = whole.reshape(fsdp_count, 2, rows, pairs, pair_cols)
            keeps.append(lax.dynamic_index_in_dim(whole, core, 1, keepdims=False))
            gives.append(lax.dynamic_index_in_dim(whole, 1 - core, 1, keepdims=False))
        keep, give = (
            jnp.concatenate(part, 1).transpose(2, 0, 1, 3) if len(part) > 1 else part[0].transpose(2, 0, 1, 3)
            for part in (keeps, gives)
        )
        mine = over_pairs(add16(keep, swap(give, "ctx", 1)))
        mine = lax.psum_scatter(mine, "fsdp", scatter_dimension=0, tiled=False)
        outs, first = [], 0
        for left in lefts:
            rows = left.shape[1] // fsdp_count // 2
            outs.append(both_halves(mine[first : first + rows].astype(jnp.float32)))
            first = first + rows
        return outs

    (o_grad,) = attn_weight_grads([attn_rows], grad_branch)

    grad_query_pre, grad_keys, grad_values = attend_back(
        query_rot, grad_attended, attn_rows, log_total, cosine, sine, low, keys, values, keys.T
    )
    grad_window = jnp.concatenate([grad_keys, grad_values], 1)
    grad_stack = grad_window.reshape(reach + 1, tok_rows, 2 * HEAD)
    own_kv_grad = grad_stack[reach]
    for hop in range(1, reach + 1):
        own_kv_grad = own_kv_grad + shifted(
            grad_stack[reach - hop].astype(jnp.bfloat16), "ctx", -hop
        ).astype(jnp.float32)
    grad_kv_pre = jnp.concatenate(
        [rotate_back(own_kv_grad[:, :HEAD], cosine, sine), own_kv_grad[:, HEAD:]], 1
    ).astype(jnp.bfloat16)
    q_grad, kv_grad = attn_weight_grads([grad_query_pre, grad_kv_pre], normed_one)
    grad_normed_one = product(grad_query_pre, q_full) + product(grad_kv_pre, kv_full)
    grad_inputs = grad_hidden + norm_back(grad_normed_one, x_rows, scale_one, gain_attn)
    gain_attn_grad = jnp.sum(grad_normed_one * x_rows * scale_one, 0)
    gains_grad = swap_sum(jnp.stack([gain_attn_grad, gain_mlp_grad], 0))
    gain_total = lax.dynamic_slice_in_dim(gains_grad, place * out_cols, out_cols, 1)
    return (
        result.astype(jnp.bfloat16)[None],
        grad_inputs.astype(jnp.bfloat16)[None],
        gain_total,
        q_grad,
        kv_grad,
        o_grad,
        mlp_grads[0],
        mlp_grads[1],
        mlp_grads[2],
    )


def solution(mesh):
    in_specs = (
        P("fsdp", "ctx", None),
        P(),
        P("fsdp", None),
        P("fsdp", None),
        P("fsdp", None),
        P("fsdp", None),
        P("fsdp", None),
        P("fsdp", None),
        P("fsdp", "ctx", None),
        P("fsdp", None),
    )
    out_specs = (
        P("fsdp", "ctx", None),
        P("fsdp", "ctx", None),
        P(None, "ctx"),
        P("fsdp", "ctx"),
        P("fsdp", "ctx"),
        P("fsdp", "ctx"),
        P("fsdp", "ctx"),
        P("fsdp", "ctx"),
        P("fsdp", "ctx"),
    )
    return jax.shard_map(body, mesh=mesh, in_specs=in_specs, out_specs=out_specs, check_vma=False)
```

```python
import jax
import jax.numpy as jnp
from jax import lax
from jax.experimental import pallas as pl
from jax.experimental.pallas import tpu as pltpu
from jax.sharding import PartitionSpec as P

HEADS = 10
HEAD = 256
WINDOW = 2048


EPSILON = 1e-06
MASKED = -1e30
LOWEST = -1e29
VMEM = 56 * 1024 * 1024
FREE = pl.CostEstimate(flops=0, bytes_accessed=0, transcendentals=0)


def shifted(value, axis, steps):
    count = lax.axis_size(axis)
    initial, last = (max(0, -steps), min(count, count - steps))
    return lax.ppermute(value, axis, [(source, source + steps) for source in range(initial, last)])


def swap(value, axis, bit):
    return lax.ppermute(value, axis, [(i, i ^ bit) for i in range(lax.axis_size(axis))])


def add16(left, right):
    return (left.astype(jnp.float32) + right.astype(jnp.float32)).astype(jnp.bfloat16)


def times_rows(left, right):
    return lax.dot_general(
        left, right, (((1,), (1,)), ((), ())), preferred_element_type=jnp.float32
    )


def gram_rows(left, right):
    return lax.dot_general(
        left, right, (((0,), (0,)), ((), ())), preferred_element_type=jnp.float32
    )


def product(left, right):
    return jnp.dot(left, right, preferred_element_type=jnp.float32)


def doc_info(doc_lengths, first_token, token_count):
    doc_ends = jnp.cumsum(doc_lengths)
    doc_starts = doc_ends - doc_lengths
    token_ids = first_token + jnp.arange(token_count, dtype=jnp.int32)
    segment = jnp.sum((doc_ends[None, :] <= token_ids[:, None]).astype(jnp.int32), 1)
    begins = jnp.max(
        jnp.where(doc_starts[None, :] <= token_ids[:, None], doc_starts[None, :], 0), 1
    )
    return (token_ids, segment, token_ids - begins)


def rope_angles(positions):
    half_width = HEAD // 2
    column = jnp.arange(half_width, dtype=jnp.float32)
    inverse = jnp.power(10000.0, -column / half_width)
    angles = positions.astype(jnp.float32)[:, None] * inverse[None, :]
    return (jnp.cos(angles), jnp.sin(angles))


def rotate(values, cosine, sine):
    half_width = values.shape[-1] // 2
    first_half = values[..., :half_width]
    second_half = values[..., half_width:]
    return jnp.concatenate(
        [first_half * cosine - second_half * sine, second_half * cosine + first_half * sine], -1
    )


def rotate_back(grad_in, cosine, sine):
    half_width = grad_in.shape[-1] // 2
    first_half = grad_in[..., :half_width]
    second_half = grad_in[..., half_width:]
    return jnp.concatenate(
        [first_half * cosine + second_half * sine, second_half * cosine - first_half * sine], -1
    )


def norm_scale(values):
    return lax.rsqrt(jnp.mean(values * values, -1, keepdims=True) + EPSILON)


def norm_back(grad_in, values, scale, gain):
    weighted = grad_in * gain
    return scale * weighted - values * scale * scale * scale * jnp.mean(
        weighted * values, -1, keepdims=True
    )


def head_rows(block, count):
    return jnp.concatenate([block[:, h * HEAD : (h + 1) * HEAD] for h in range(count)], 0)


def row_bounds(low_ref, first_key, tokens, count):
    high = first_key + lax.broadcasted_iota(jnp.int32, (1, tokens), 1)
    low = low_ref[0]
    return jnp.concatenate([low] * count, 1), jnp.concatenate([high] * count, 1)


def seen(start, shape, low, high):
    key = start + lax.broadcasted_iota(jnp.int32, shape, 0)
    return (key >= low) & (key <= high)


def attend_kernel(
    span_ref, pre_ref, cos_ref, sin_ref, low_ref, key_ref, value_ref, *refs, base, chunk
):
    out_ref, out_t_ref, rot_ref, log_ref, acc = refs[-5:]
    tile = pl.program_id(0)
    tokens = pre_ref.shape[0]
    count = pre_ref.shape[1] // HEAD
    cosine, sine = cos_ref[...], sin_ref[...]
    half = HEAD // 2
    for h in range(count):
        first = pre_ref[:, h * HEAD : h * HEAD + half]
        second = pre_ref[:, h * HEAD + half : (h + 1) * HEAD]
        rot_ref[:, h * HEAD : h * HEAD + half] = (
            (first * cosine - second * sine) * HEAD ** (-0.5)
        ).astype(jnp.bfloat16)
        rot_ref[:, h * HEAD + half : (h + 1) * HEAD] = (
            (second * cosine + first * sine) * HEAD ** (-0.5)
        ).astype(jnp.bfloat16)
    query = head_rows(rot_ref[...], count)
    low, high = row_bounds(low_ref, base + tile * tokens, tokens, count)
    rows = count * tokens

    acc[...] = jnp.zeros_like(acc)

    def step(j, carry):
        top, total = carry
        start = pl.multiple_of(j * chunk, chunk)
        scores = lax.dot_general(
            key_ref[pl.ds(start, chunk), :], query, (((1,), (1,)), ((), ())),
            preferred_element_type=jnp.float32,
        )
        scores = jnp.where(seen(start, scores.shape, low, high), scores, MASKED)
        higher = jnp.maximum(top, jnp.max(scores, 0, keepdims=True))
        part = jnp.exp(scores - higher)
        shrink = jnp.exp(top - higher)
        acc[...] = acc[...] * shrink + lax.dot_general(
            value_ref[:, pl.ds(start, chunk)], part.astype(jnp.bfloat16), (((1,), (0,)), ((), ())),
            preferred_element_type=jnp.float32,
        )
        return higher, total * shrink + jnp.sum(part, 0, keepdims=True)

    top, total = lax.fori_loop(
        span_ref[0, tile], span_ref[1, tile], step,
        (jnp.full((1, rows), LOWEST, jnp.float32), jnp.zeros((1, rows), jnp.float32)),
    )
    log_ref[0, 0] = top + jnp.log(total)
    outs_t = acc[...] * (1.0 / total)
    outs = outs_t.T.astype(jnp.bfloat16)
    outs_t = outs_t.astype(jnp.bfloat16)
    for h in range(count):
        out_t_ref[h * HEAD : (h + 1) * HEAD, :] = outs_t[:, h * tokens : (h + 1) * tokens]
        out_ref[:, h * HEAD : (h + 1) * HEAD] = outs[h * tokens : (h + 1) * tokens]


def attend_back_kernel(
    span_ref, rot_ref, grad_ref, out_ref, log_ref, cos_ref, sin_ref, low_ref, key_ref, value_ref, key_t_ref,
    *refs, base, chunk
):
    pre_ref, pre_t_ref, grad_kv_ref, grad_key_ref, grad_value_ref, acc = refs[-6:]
    tile = pl.program_id(0)
    tokens = rot_ref.shape[0]
    count = rot_ref.shape[1] // HEAD

    @pl.when((tile == 0) & (pl.program_id(1) == 0))
    def _():
        grad_key_ref[...] = jnp.zeros_like(grad_key_ref)
        grad_value_ref[...] = jnp.zeros_like(grad_value_ref)

    query = head_rows(rot_ref[...], count)
    grad = head_rows(grad_ref[...], count)
    outs = head_rows(out_ref[...], count)
    delta = jnp.sum((grad.astype(jnp.float32) * outs.astype(jnp.float32)).T, 0, keepdims=True)
    log_total = log_ref[0, 0]
    low, high = row_bounds(low_ref, base + tile * tokens, tokens, count)
    acc[...] = jnp.zeros_like(acc)

    def step(j, carry):
        start = pl.multiple_of(j * chunk, chunk)
        here = pl.ds(start, chunk)
        scores = lax.dot_general(
            key_ref[here, :], query, (((1,), (1,)), ((), ())), preferred_element_type=jnp.float32
        )
        grad_probs = lax.dot_general(
            value_ref[here, :], grad, (((1,), (1,)), ((), ())), preferred_element_type=jnp.float32
        )
        probs = jnp.where(seen(start, scores.shape, low, high), jnp.exp(scores - log_total), 0.0)
        grad_scores = (probs * (grad_probs - delta)).astype(jnp.bfloat16)
        grad_value_ref[here, :] += jnp.dot(
            probs.astype(jnp.bfloat16), grad, preferred_element_type=jnp.float32
        )
        grad_key_ref[here, :] += jnp.dot(grad_scores, query, preferred_element_type=jnp.float32)
        acc[...] += lax.dot_general(
            key_t_ref[:, here], grad_scores, (((1,), (0,)), ((), ())),
            preferred_element_type=jnp.float32,
        )
        return carry

    lax.fori_loop(span_ref[0, tile], span_ref[1, tile], step, 0)
    cosine, sine = cos_ref[...], sin_ref[...]
    half = HEAD // 2
    for h in range(count):
        own = acc[:, h * tokens : (h + 1) * tokens] * HEAD ** (-0.5)
        first, second = own[:half], own[half:]
        own = jnp.concatenate(
            [first * cosine + second * sine, second * cosine - first * sine], 0
        )
        pre_t_ref[h * HEAD : (h + 1) * HEAD, :] = own.astype(jnp.bfloat16)
        pre_ref[:, h * HEAD : (h + 1) * HEAD] = own.T.astype(jnp.bfloat16)

    @pl.when((tile == pl.num_programs(0) - 1) & (pl.program_id(1) == pl.num_programs(1) - 1))
    def _():
        grad_kv_ref[:, :HEAD] = grad_key_ref[...].astype(jnp.bfloat16)
        grad_kv_ref[:, HEAD:] = grad_value_ref[...].astype(jnp.bfloat16)


def attention_plan(tok_rows, key_count, low):
    tile = min(128, tok_rows)
    chunk = 256 if key_count % 256 == 0 else 128
    base = key_count - tok_rows
    tiles = tok_rows // tile
    begin = low[::tile] // chunk
    end = (base + (jnp.arange(tiles, dtype=jnp.int32) + 1) * tile + chunk - 1) // chunk
    return tile, chunk, base, jnp.stack([begin, end], 0).astype(jnp.int32)


GROUP = 10


def attend(query_pre, cosine, sine, low, keys, values_t, deps=()):
    tok_rows = query_pre.shape[0]
    key_count = keys.shape[0]
    tile, chunk, base, span = attention_plan(tok_rows, key_count, low)
    tiles = tok_rows // tile
    groups = HEADS // GROUP
    wide = GROUP * HEAD
    block = pl.BlockSpec((tile, wide), lambda i, g, s: (i, g))
    angle = pl.BlockSpec((tile, HEAD // 2), lambda i, g, s: (i, 0))
    return pl.pallas_call(
        lambda *refs: attend_kernel(*refs, base=base, chunk=chunk),
        grid_spec=pltpu.PrefetchScalarGridSpec(
            num_scalar_prefetch=1,
            grid=(tiles, groups),
            in_specs=[
                block,
                angle,
                angle,
                pl.BlockSpec((1, 1, tile), lambda i, g, s: (i, 0, 0)),
                pl.BlockSpec((key_count, HEAD), lambda i, g, s: (0, 0)),
                pl.BlockSpec((HEAD, key_count), lambda i, g, s: (0, 0)),
            ]
            + [pl.BlockSpec(memory_space=pl.ANY)] * len(deps),
            out_specs=[
                block,
                pl.BlockSpec((wide, tile), lambda i, g, s: (g, i)),
                block,
                pl.BlockSpec((1, 1, 1, GROUP * tile), lambda i, g, s: (i, g, 0, 0)),
            ],
            scratch_shapes=[pltpu.VMEM((HEAD, GROUP * tile), jnp.float32)],
        ),
        out_shape=[
            jax.ShapeDtypeStruct(query_pre.shape, jnp.bfloat16),
            jax.ShapeDtypeStruct(query_pre.shape[::-1], jnp.bfloat16),
            jax.ShapeDtypeStruct(query_pre.shape, jnp.bfloat16),
            jax.ShapeDtypeStruct((tiles, groups, 1, GROUP * tile), jnp.float32),
        ],
        compiler_params=pltpu.CompilerParams(vmem_limit_bytes=VMEM),
        cost_estimate=FREE,
        name="attend",
    )(span, query_pre, cosine, sine, low.reshape(tiles, 1, tile), keys, values_t, *deps)


def attend_back(query_rot, grad_rows, attn_rows, log_total, cosine_t, sine_t, low, keys, values, keys_t, deps):
    tok_rows = query_rot.shape[0]
    key_count = keys.shape[0]
    tile, chunk, base, span = attention_plan(tok_rows, key_count, low)
    tiles = tok_rows // tile
    groups = HEADS // GROUP
    wide = GROUP * HEAD
    block = pl.BlockSpec((tile, wide), lambda i, g, s: (i, g))
    angle = pl.BlockSpec((HEAD // 2, tile), lambda i, g, s: (0, i))
    window = pl.BlockSpec((key_count, HEAD), lambda i, g, s: (0, 0))
    return pl.pallas_call(
        lambda *refs: attend_back_kernel(*refs, base=base, chunk=chunk),
        grid_spec=pltpu.PrefetchScalarGridSpec(
            num_scalar_prefetch=1,
            grid=(tiles, groups),
            in_specs=[
                block,
                block,
                block,
                pl.BlockSpec((1, 1, 1, GROUP * tile), lambda i, g, s: (i, g, 0, 0)),
                angle,
                angle,
                pl.BlockSpec((1, 1, tile), lambda i, g, s: (i, 0, 0)),
                window,
                window,
                pl.BlockSpec((HEAD, key_count), lambda i, g, s: (0, 0)),
            ]
            + [pl.BlockSpec(memory_space=pl.ANY)] * len(deps),
            out_specs=[
                block,
                pl.BlockSpec((wide, tile), lambda i, g, s: (g, i)),
                pl.BlockSpec((key_count, 2 * HEAD), lambda i, g, s: (0, 0)),
            ],
            scratch_shapes=[
                pltpu.VMEM((key_count, HEAD), jnp.float32),
                pltpu.VMEM((key_count, HEAD), jnp.float32),
                pltpu.VMEM((HEAD, GROUP * tile), jnp.float32),
            ],
        ),
        out_shape=[
            jax.ShapeDtypeStruct(query_rot.shape, jnp.bfloat16),
            jax.ShapeDtypeStruct(query_rot.shape[::-1], jnp.bfloat16),
            jax.ShapeDtypeStruct((key_count, 2 * HEAD), jnp.bfloat16),
        ],
        compiler_params=pltpu.CompilerParams(vmem_limit_bytes=VMEM),
        cost_estimate=FREE,
        name="attend_back",
    )(
        span, query_rot, grad_rows, attn_rows, log_total, cosine_t, sine_t, low.reshape(tiles, 1, tile),
        keys, values, keys_t, *deps,
    )


def nt(left, right):
    return lax.dot_general(
        left, right, (((1,), (1,)), ((), ())), preferred_element_type=jnp.float32
    )


def tn(left, right):
    return lax.dot_general(
        left, right, (((0,), (0,)), ((), ())), preferred_element_type=jnp.float32
    )


def flat(ref):
    block = ref[...]
    return block.reshape(-1, block.shape[-1])


def units_kernel(core_ref, *refs):
    tokens, cots = refs[0:2], refs[2:4]
    gate_ref, up_ref, down_ref = refs[4:7]
    out_ref = refs[-1]
    gate_rows, up_rows, down_rows = flat(gate_ref), flat(up_ref), flat(down_ref)

    def one(token_ref, cot_ref):
        gate = nt(gate_rows, token_ref[...])
        up = nt(up_rows, token_ref[...])
        grad_mixed = nt(down_rows, cot_ref[...])
        root = (2.0 / jnp.pi) ** 0.5
        square = gate * gate
        curve = jnp.tanh(root * (gate + 0.044715 * (square * gate)))
        upper = 0.5 * (1.0 + curve)
        activated = gate * upper
        slope = upper + 0.5 * gate * (1.0 - curve * curve) * (root * (1.0 + 0.134145 * square))
        out_ref[0] = (grad_mixed * up * slope).astype(jnp.bfloat16)
        out_ref[1] = (grad_mixed * activated).astype(jnp.bfloat16)
        out_ref[2] = (activated * up).astype(jnp.bfloat16)

    for j in (0, 1):
        pl.when(pl.program_id(1) == j)(lambda j=j: one(tokens[j], cots[j]))


def units(tokens, cots, weights, core, group, held, deps=()):
    cols, width = tokens[0].shape
    hidden = weights.hidden
    token_block = pl.BlockSpec((cols, width), lambda i, j, s: (0, 0))
    extra = (() if held is None else (held,)) + tuple(deps)
    return pl.pallas_call(
        units_kernel,
        grid_spec=pltpu.PrefetchScalarGridSpec(
            num_scalar_prefetch=1,
            grid=(2, 2),
            in_specs=[token_block] * 4
            + weights.specs(2, lambda i, j, s: (i, 0), width)
            + [pl.BlockSpec(memory_space=pl.ANY)] * len(extra),
            out_specs=pl.BlockSpec(
                (3, hidden // 2, cols), lambda i, j, s: (0, i, 2 * group + j)
            ),
        ),
        out_shape=jax.ShapeDtypeStruct((3, hidden, 4 * cols), jnp.bfloat16),
        input_output_aliases={} if held is None else {8: 0},
        compiler_params=pltpu.CompilerParams(vmem_limit_bytes=VMEM),
        cost_estimate=FREE,
        name="units",
    )(core, *tokens, *cots, *weights.arrays, *extra)


class OwnWeights:
    def __init__(self, shards):
        self.arrays = tuple(shards)
        self.hidden = shards[0].shape[0] // 2

    def specs(self, cuts, place, width):
        def index(*grid):
            row, col = place(*grid)
            return (grid[-1][0] * cuts + row, col)

        return [pl.BlockSpec((self.hidden // cuts, width), index)] * len(self.arrays)


class FarWeights:
    def __init__(self, gathered):
        parts, count, rows, width = gathered.shape
        self.hidden = parts * rows
        if rows % 16:
            gathered = gathered.reshape(2, parts // 2, count, rows, width)
            gathered = gathered.transpose(0, 2, 1, 3, 4).reshape(2, count, -1, width)
        self.arrays = (gathered,) * count

    def specs(self, cuts, place, width):
        parts, count, rows, _ = self.arrays[0].shape

        def spec(which):
            def index(*grid):
                row, col = place(*grid)
                return (row, which, 0, col)

            return pl.BlockSpec((parts // cuts, 1, rows, width), index)

        return [spec(which) for which in range(count)]


def sums_kernel(core_ref, *refs, count):
    total = 0.0
    for act_ref, weight_ref in zip(refs[:count], refs[count : 2 * count], strict=True):
        total = total + tn(act_ref[0], flat(weight_ref))
    refs[-1][...] = total.astype(jnp.bfloat16)


def sums(acts, weights, core, group, which, block=None, deps=()):
    hidden, all_tokens = acts[0].shape[1:]
    width = weights[0].arrays[0].shape[-1]
    rows = all_tokens // 4
    blocks = 2 if block is None else 1
    cols = width // 2
    first = 2 * group + (block or 0)

    def act_spec(kind):
        return pl.BlockSpec((1, hidden, rows), lambda n, t, s: (kind, 0, first + t))

    act_specs, weight_specs, act_args, weight_args = [], [], [], []
    for act, weight in zip(acts, weights, strict=True):
        specs = weight.specs(1, lambda n, t, s: (0, n), cols)
        for kind in which:
            act_specs.append(act_spec(kind))
            act_args.append(act)
            weight_specs.append(specs[kind])
            weight_args.append(weight.arrays[kind])
    return pl.pallas_call(
        lambda *refs: sums_kernel(*refs, count=len(act_args)),
        grid_spec=pltpu.PrefetchScalarGridSpec(
            num_scalar_prefetch=1,
            grid=(2, blocks),
            in_specs=act_specs + weight_specs + [pl.BlockSpec(memory_space=pl.ANY)] * len(deps),
            out_specs=pl.BlockSpec((rows, cols), lambda n, t, s: (t, n)),
        ),
        out_shape=jax.ShapeDtypeStruct((blocks * rows, width), jnp.bfloat16),
        compiler_params=pltpu.CompilerParams(vmem_limit_bytes=VMEM),
        cost_estimate=FREE,
        name="sums",
    )(core, *act_args, *weight_args, *deps)


def grams_kernel(acts_ref, *refs, sets):
    out_ref = refs[-1]

    def one(rights):
        step = rights[0].shape[0]
        total = 0.0
        for i, right_ref in enumerate(rights):
            total = total + jnp.dot(
                acts_ref[0, :, i * step : (i + 1) * step], right_ref[...],
                preferred_element_type=jnp.float32,
            )
        out_ref[0] = total.astype(jnp.bfloat16)

    if sets == 1:
        one(refs[0:4])
    else:
        pl.when(pl.program_id(0) < 2)(lambda: one(refs[0:4]))
        pl.when(pl.program_id(0) == 2)(lambda: one(refs[4:8]))


def grams(acts, tokens, cots, pairs, kinds, deps=()):
    _, hidden, all_tokens = acts.shape
    step, width = tokens[0].shape
    cols = width // pairs
    first, count = kinds[0], len(kinds)
    if cols % 128:
        parts = []
        for kind in kinds:
            whole = sum(
                product(acts[kind, :, i * step : (i + 1) * step], right)
                for i, right in enumerate(cots if kind == 2 else tokens)
            )
            parts.append(whole.astype(jnp.bfloat16))
        return jnp.concatenate(parts, 0).reshape(count * hidden, pairs, cols).transpose(1, 0, 2)
    if count == 3:
        specs = [pl.BlockSpec((step, cols), lambda k, p: (0, jnp.where(k < 2, p, pairs - 1)))] * 4
        specs = specs + [pl.BlockSpec((step, cols), lambda k, p: (0, jnp.where(k < 2, 0, p)))] * 4
        rights = tuple(tokens) + tuple(cots)
    else:
        specs = [pl.BlockSpec((step, cols), lambda k, p: (0, p))] * 4
        rights = tuple(cots) if first == 2 else tuple(tokens)
    return pl.pallas_call(
        lambda *refs: grams_kernel(*refs, sets=len(rights) // 4),
        grid=(count, pairs),
        in_specs=[pl.BlockSpec((1, hidden, all_tokens), lambda k, p: (first + k, 0, 0))]
        + specs
        + [pl.BlockSpec(memory_space=pl.ANY)] * len(deps),
        out_specs=pl.BlockSpec((1, hidden, cols), lambda k, p: (p, k, 0)),
        out_shape=jax.ShapeDtypeStruct((pairs, count * hidden, cols), jnp.bfloat16),
        compiler_params=pltpu.CompilerParams(vmem_limit_bytes=VMEM),
        cost_estimate=FREE,
        name="grams",
    )(acts, *rights, *deps)


def spread_kernel(left_ref, weight_ref, *refs):
    out_ref = refs[-1]
    out_ref[...] = nt(left_ref[...], flat(weight_ref)).astype(out_ref.dtype)


def pieces(gathered):
    count, shards, rows, width = gathered.shape
    if rows % 16:
        return gathered.transpose(1, 0, 2, 3).reshape(1, shards, count * rows, width)
    return gathered


def spread(left, weight, dtype, deps=()):
    count, shards, rows, width = weight.shape
    tokens = left.shape[0]
    return pl.pallas_call(
        spread_kernel,
        grid=(shards,),
        in_specs=[
            pl.BlockSpec((tokens, width), lambda z: (0, 0)),
            pl.BlockSpec((count, 1, rows, width), lambda z: (0, z, 0, 0)),
        ]
        + [pl.BlockSpec(memory_space=pl.ANY)] * len(deps),
        out_specs=pl.BlockSpec((tokens, count * rows), lambda z: (0, z)),
        out_shape=jax.ShapeDtypeStruct((tokens, shards * count * rows), dtype),
        compiler_params=pltpu.CompilerParams(vmem_limit_bytes=VMEM),
        cost_estimate=FREE,
        name="spread",
    )(left, weight, *deps)


def collect_kernel(left_ref, weight_ref, start_ref, gain_ref, *refs, normed):
    shard = pl.program_id(0)
    total_ref = refs[0]

    @pl.when(shard == 0)
    def _():
        total_ref[...] = start_ref[...].astype(jnp.float32)

    total_ref[...] += jnp.dot(left_ref[...], flat(weight_ref), preferred_element_type=jnp.float32)
    if normed:

        @pl.when(shard == pl.num_programs(0) - 1)
        def _():
            rows = min(128, total_ref.shape[0])

            def norm(i, carry):
                here = pl.ds(pl.multiple_of(i * rows, rows), rows)
                total = total_ref[here, :]
                scale = norm_scale(total)
                refs[1][here, :] = (total * scale * gain_ref[...]).astype(jnp.bfloat16)
                refs[2][here, :] = jnp.broadcast_to(scale, (rows, 128))
                return carry

            lax.fori_loop(0, total_ref.shape[0] // rows, norm, 0)


def collect(left, weight, start, gain=None):
    count, shards, rows, width = weight.shape
    tokens = left.shape[0]
    whole = pl.BlockSpec((tokens, width), lambda z: (0, 0))
    shapes, specs = [jax.ShapeDtypeStruct((tokens, width), jnp.float32)], [whole]
    if gain is not None:
        shapes.append(jax.ShapeDtypeStruct((tokens, width), jnp.bfloat16))
        shapes.append(jax.ShapeDtypeStruct((tokens, 128), jnp.float32))
        specs.extend([whole, pl.BlockSpec((tokens, 128), lambda z: (0, 0))])
    gain_row = jnp.zeros((1, width), jnp.float32) if gain is None else gain.reshape(1, width)
    return pl.pallas_call(
        lambda *refs: collect_kernel(*refs, normed=gain is not None),
        grid=(shards,),
        in_specs=[
            pl.BlockSpec((tokens, count * rows), lambda z: (0, z)),
            pl.BlockSpec((count, 1, rows, width), lambda z: (0, z, 0, 0)),
            whole,
            pl.BlockSpec((1, width), lambda z: (0, 0)),
        ],
        out_specs=specs,
        out_shape=shapes,
        compiler_params=pltpu.CompilerParams(vmem_limit_bytes=VMEM),
        cost_estimate=FREE,
        name="collect",
    )(left, weight, start, gain_row)


def cross_kernel(core_ref, *refs, lefts, gained, added):
    right_ref, out_ref = refs[lefts], refs[-1]
    first = 0

    def put(part, rows):
        here = (0, slice(None), slice(first, first + rows))
        if added:
            part = part + refs[lefts + 1 + gained][here].astype(jnp.float32)
        out_ref[here] = part.astype(jnp.bfloat16)

    for left_ref in refs[:lefts]:
        shards, _, rows, tokens = left_ref.shape
        left = left_ref[...].reshape(shards * rows, tokens)
        part = jnp.dot(left, right_ref[...], preferred_element_type=jnp.float32)
        put(part.reshape(shards, rows, -1), rows)
        first = first + rows
    if gained:
        gains = refs[lefts + 1][...].astype(jnp.float32)
        put(jnp.broadcast_to(gains[None], (out_ref.shape[1],) + gains.shape), gains.shape[0])


def cross(lefts, right, core, shards, pairs, gains=None, add=None, deps=()):
    tokens, width = right.shape
    cols = width // pairs
    views = [left.reshape(shards, 2, -1, tokens) for left in lefts]
    rows = [view.shape[2] for view in views]
    total = sum(rows) + (0 if gains is None else gains.shape[0])
    if cols % 128:
        picked = jnp.concatenate(
            [lax.dynamic_index_in_dim(view, core[0], 1, keepdims=False) for view in views], 1
        )
        whole = product(picked.reshape(-1, tokens), right).reshape(shards, sum(rows), width)
        if gains is not None:
            extra = jnp.broadcast_to(gains.astype(jnp.float32)[None], (shards,) + gains.shape)
            whole = jnp.concatenate([whole, extra], 1)
        whole = whole.reshape(shards, total, pairs, cols).transpose(2, 0, 1, 3)
        if add is not None:
            whole = whole + add.astype(jnp.float32)
        return whole.astype(jnp.bfloat16)
    block = pl.BlockSpec((1, shards, total, cols), lambda p, s: (p, 0, 0, 0))
    specs = [
        pl.BlockSpec((shards, 1, count, tokens), lambda p, s: (0, s[0], 0, 0)) for count in rows
    ]
    specs.append(pl.BlockSpec((tokens, cols), lambda p, s: (0, p)))
    args = [*views, right]
    if gains is not None:
        specs.append(pl.BlockSpec((gains.shape[0], cols), lambda p, s: (0, p)))
        args.append(gains)
    if add is not None:
        specs.append(block)
        args.append(add)
    return pl.pallas_call(
        lambda *refs: cross_kernel(
            *refs, lefts=len(views), gained=gains is not None, added=add is not None
        ),
        grid_spec=pltpu.PrefetchScalarGridSpec(
            num_scalar_prefetch=1,
            grid=(pairs,),
            in_specs=specs + [pl.BlockSpec(memory_space=pl.ANY)] * len(deps),
            out_specs=block,
        ),
        out_shape=jax.ShapeDtypeStruct((pairs, shards, total, cols), jnp.bfloat16),
        compiler_params=pltpu.CompilerParams(vmem_limit_bytes=VMEM),
        cost_estimate=FREE,
        name="cross",
    )(core, *args, *deps)


def swap(value, axis, bit):
    return lax.ppermute(value, axis, [(i, i ^ bit) for i in range(lax.axis_size(axis))])


def after(value, *others):
    return lax.optimization_barrier((value, *others))[0]


def same_core():
    count = lax.axis_size("ctx")
    return [list(range(0, count, 2)), list(range(1, count, 2))]


def own_part(shard, place):
    part = shard.shape[0] // lax.axis_size("ctx")
    return lax.dynamic_slice_in_dim(shard, place * part, part, 0)


def together(*values):
    return lax.optimization_barrier(values)


def direct_scatter(blocks, axis, place):
    count = lax.axis_size(axis)
    total = lax.dynamic_index_in_dim(blocks, place, 0, keepdims=False).astype(jnp.float32)
    for step in range(1, count):
        give = lax.dynamic_index_in_dim(blocks, lax.rem(place + step, count), 0, keepdims=False)
        got = lax.ppermute(give, axis, [(i, (i + step) % count) for i in range(count)])
        total = total + got.astype(jnp.float32)
    return total


def doubling_gather(value, axis, place):
    count = lax.axis_size(axis)
    out = jnp.zeros((count,) + value.shape, value.dtype)
    out = lax.dynamic_update_index_in_dim(out, value, place, 0)
    held, bit = value[None], 1
    while bit < count:
        got = swap(held, axis, bit)
        theirs = (place // bit) ^ 1
        out = lax.dynamic_update_slice_in_dim(out, got, theirs * bit, 0)
        bit = 2 * bit
        if bit < count:
            held = lax.dynamic_slice_in_dim(out, (place // bit) * bit, bit, 0)
    return out


def ring_gather(value, axis, place):
    count = lax.axis_size(axis)
    out = jnp.zeros((count,) + value.shape, value.dtype)
    for step in range(count):
        out = lax.dynamic_update_index_in_dim(out, value, lax.rem(place + count - step, count), 0)
        if step < count - 1:
            value = lax.ppermute(value, axis, [(i, (i + 1) % count) for i in range(count)])
    return out


def in_order(gathered, first, part):
    mine = gathered[:, :, first : first + part].transpose(1, 0, 2, 3)
    return mine.reshape(-1, gathered.shape[-1])


def body(
    inputs,
    norm_gains,
    q_weight,
    kv_weight,
    o_weight,
    gate_weight,
    up_weight,
    down_weight,
    cotangent,
    doc_lengths,
):
    x_rows = inputs[0].astype(jnp.float32)
    grad_out = cotangent[0]
    tok_rows, width = x_rows.shape
    place = lax.axis_index("ctx")
    ctx_count = lax.axis_size("ctx")
    pairs = ctx_count // 2
    core = place % 2
    pair = place // 2
    own_core = core.reshape(1).astype(jnp.int32)
    shard = lax.axis_index("fsdp")
    shards = lax.axis_size("fsdp")
    reach = min(ctx_count - 1, (WINDOW + tok_rows - 2) // tok_rows)
    key_count = (reach + 1) * tok_rows
    first_token = place * tok_rows
    token_ids, segment, positions = doc_info(doc_lengths[0], first_token, tok_rows)
    low = jnp.maximum(token_ids - positions, token_ids - (WINDOW - 1)) - (
        first_token - reach * tok_rows
    )
    cosine, sine = rope_angles(positions)
    gain_attn = norm_gains[0]
    gain_mlp = norm_gains[1]

    q_part, kv_part, o_part = (own_part(w, place) for w in (q_weight, kv_weight, o_weight))
    q_z = lax.all_gather(q_part, "fsdp", axis=0)
    kv_z = ring_gather(kv_part, "fsdp", shard)
    q_z, kv_z = together(q_z, kv_z)
    q_all = lax.all_gather(q_z, "ctx", axis=0)
    kv_all = doubling_gather(kv_z, "ctx", place)
    o_z = ring_gather(after(o_part, q_z), "fsdp", shard)

    half_rows = gate_weight.shape[0] // 2
    part_rows = half_rows // pairs
    mine = jnp.stack(
        [
            lax.dynamic_slice_in_dim(w, core * half_rows + pair * part_rows, part_rows, 0)
            for w in (gate_weight, up_weight, down_weight)
        ],
        0,
    )
    cut = part_rows // 3
    far_first = swap(after(mine[:, :cut], q_z), "fsdp", 2)
    own_weights = OwnWeights((gate_weight, up_weight, down_weight))

    scale_one = norm_scale(x_rows)
    normed_one = (x_rows * scale_one * gain_attn).astype(jnp.bfloat16)
    kv_full = in_order(kv_all, 0, kv_part.shape[0])
    kv_pre = times_rows(normed_one, kv_full)
    key_rot = rotate(kv_pre[:, :HEAD], cosine, sine).astype(jnp.bfloat16)
    kv_local = jnp.concatenate([key_rot, kv_pre[:, HEAD:].astype(jnp.bfloat16)], 1)
    kv_window = jnp.concatenate(
        [shifted(kv_local, "ctx", hop) for hop in range(reach, 0, -1)] + [kv_local], 0
    )
    cot_across = swap(after(grad_out, q_z), "fsdp", 1)
    q_all, far_first, kv_window, o_z, cot_across = together(
        q_all, far_first, kv_window, o_z, cot_across
    )
    cots = [(grad_out, swap(grad_out, "ctx", 1)), (cot_across, swap(cot_across, "ctx", 1))]
    o_all = pieces(lax.all_gather(o_z, "ctx", axis=0))
    q_all = pieces(q_all)
    far_second = swap(after(mine[:, cut:], far_first), "fsdp", 2)
    query_pre = spread(normed_one, q_all, jnp.float32)
    keys, values = kv_window[:, :HEAD], kv_window[:, HEAD:]
    attn_rows, attn_rows_t, query_rot, log_total = attend(
        query_pre, cosine, sine, low, keys, values.T, (cots[0][1], cots[1][1])
    )
    hidden_one, normed_two, scale_two = collect(attn_rows, o_all, inputs[0], gain_mlp)
    scale_two = scale_two[:, :1]

    near = (normed_two, swap(normed_two, "ctx", 1))
    across = swap(normed_two, "fsdp", 1)
    far_part = jnp.concatenate([far_first, far_second], 1)
    near, far_part = together(near, far_part)
    far_all = lax.all_gather(far_part, "ctx", axis=0, axis_index_groups=same_core())
    own_acts = units(near, cots[0], own_weights, own_core, 0, None)
    across, own_acts = together(across, own_acts)
    far = (across, swap(across, "ctx", 1))
    own_acts = units(far, cots[1], own_weights, own_core, 1, own_acts)
    near_far, cot_rows = near + far, cots[0] + cots[1]
    own_grams = grams(own_acts, near_far, cot_rows, pairs, (0, 1, 2))

    def over_pairs(blocks):
        mine = lax.psum_scatter(
            blocks, "ctx", scatter_dimension=0, tiled=False, axis_index_groups=same_core()
        )
        return lax.optimization_barrier(mine)

    far_all, own_grams = together(far_all, own_grams)
    own_grads = over_pairs(own_grams)

    far_weights = FarWeights(far_all)
    far_acts = units(far, cots[1], far_weights, own_core, 1, None, (own_grams,))
    far_acts = units(near, cots[0], far_weights, own_core, 0, far_acts)
    acts, weights = (own_acts, far_acts), (own_weights, far_weights)

    def far_sum(which, deps=()):
        give = sums(acts, weights, own_core, 1, which, 1, deps)
        got = swap(give, "ctx", 1)
        keep = sums(acts, weights, own_core, 1, which, 0, (give,))
        total = add16(keep, got)
        return total, swap(total, "fsdp", 1)

    back_total, moved = far_sum((0, 1))
    far_grams = [grams(far_acts, near_far, cot_rows, pairs, (0, 1), (back_total,))]
    near_back = sums(acts, weights, own_core, 0, (0, 1), None, (far_grams[0],))
    near_moved = swap(near_back[tok_rows:], "ctx", 1)
    grad_normed_two = (
        near_back[:tok_rows].astype(jnp.float32)
        + near_moved.astype(jnp.float32)
        + moved.astype(jnp.float32)
    )
    grad_hidden = grad_out.astype(jnp.float32) + norm_back(
        grad_normed_two, hidden_one, scale_two, gain_mlp
    )
    gain_mlp_grad = jnp.sum(grad_normed_two * hidden_one * scale_two, 0)
    grad_branch = grad_hidden.astype(jnp.bfloat16)
    grad_attended = spread(grad_branch, o_all, jnp.bfloat16, (own_grads,))

    far_grams.append(grams(far_acts, near_far, cot_rows, pairs, (2,), (grad_attended,)))
    far_sums = [over_pairs(blocks) for blocks in far_grams]
    far_grads = [swap(blocks, "fsdp", 2) for blocks in far_sums]
    out_total, out_moved = far_sum((2,), (far_grams[1],))

    out_cols = width // ctx_count

    def both_halves(mine):
        keep = lax.dynamic_slice_in_dim(mine, core * out_cols, out_cols, 1)
        give = lax.dynamic_slice_in_dim(mine, (1 - core) * out_cols, out_cols, 1)
        got = swap(give.astype(jnp.bfloat16), "ctx", 1).astype(jnp.float32)
        lower = jnp.where(core == 0, keep, got)
        upper = jnp.where(core == 0, got, keep)
        return jnp.concatenate([lower, upper], 0)

    grad_query_pre, grad_query_pre_t, grad_kv = attend_back(
        query_rot, grad_attended, attn_rows, log_total, cosine.T, sine.T, low, keys, values, keys.T,
        (out_total,),
    )
    grad_stack = grad_kv.reshape(reach + 1, tok_rows, 2 * HEAD)
    moved_kv = [shifted(grad_stack[reach - hop], "ctx", -hop) for hop in range(1, reach + 1)]
    o_give = cross([attn_rows_t], grad_branch, 1 - own_core, shards, pairs, deps=(grad_kv, out_moved))
    o_got = swap(o_give, "ctx", 1)
    near_out = sums(acts, weights, own_core, 0, (2,), None, (o_give,))
    near_out_moved = swap(near_out[tok_rows:], "ctx", 1)
    o_sums = cross(
        [attn_rows_t], grad_branch, own_core, shards, pairs, add=o_got, deps=(near_out, far_sums[0])
    )
    moved_kv, o_sums = together(moved_kv, o_sums)
    own_kv_grad = grad_stack[reach].astype(jnp.float32)
    for block in moved_kv:
        own_kv_grad = own_kv_grad + block.astype(jnp.float32)
    grad_kv_pre = jnp.concatenate(
        [rotate_back(own_kv_grad[:, :HEAD], cosine, sine), own_kv_grad[:, HEAD:]], 1
    ).astype(jnp.bfloat16)
    grad_normed_one = collect(grad_query_pre, q_all, product(grad_kv_pre, kv_full))[0]
    gain_attn_grad = jnp.sum(grad_normed_one * x_rows * scale_one, 0)
    gains = jnp.stack([gain_attn_grad, gain_mlp_grad], 0).astype(jnp.bfloat16)
    gains = jnp.concatenate([gains, jnp.zeros((14, width), jnp.bfloat16)], 0)
    lefts = [grad_query_pre_t, grad_kv_pre.T]
    qkv_give = cross(lefts, normed_one, 1 - own_core, shards, pairs, gains)
    qkv_got = swap(qkv_give, "ctx", 1)
    grad_inputs = grad_hidden + norm_back(grad_normed_one, x_rows, scale_one, gain_attn)
    qkv_sums = cross(
        lefts, normed_one, own_core, shards, pairs, gains, qkv_got, (far_grads[0],)
    )

    o_pairs = over_pairs(o_sums)
    o_pairs, qkv_sums = together(o_pairs, qkv_sums)
    qkv_pairs = over_pairs(qkv_sums)
    o_grad = both_halves(direct_scatter(o_pairs, "fsdp", shard))
    qkv_mine = direct_scatter(qkv_pairs, "fsdp", shard)
    q_half, kv_half = q_weight.shape[0] // 2, kv_weight.shape[0] // 2
    q_grad = both_halves(qkv_mine[:q_half])
    kv_grad = both_halves(qkv_mine[q_half : q_half + kv_half])
    gain_total = lax.dynamic_slice_in_dim(
        qkv_mine[q_half + kv_half : q_half + kv_half + 2], core * out_cols, out_cols, 1
    )

    result = hidden_one + (
        near_out[:tok_rows].astype(jnp.float32)
        + near_out_moved.astype(jnp.float32)
        + out_moved.astype(jnp.float32)
    )

    gate_up = own_grads[: 2 * half_rows].astype(jnp.float32) + far_grads[0].astype(jnp.float32)
    down = own_grads[2 * half_rows :].astype(jnp.float32) + far_grads[1].astype(jnp.float32)
    mlp_grads = [both_halves(part) for part in (gate_up[:half_rows], gate_up[half_rows:], down)]

    return (
        result.astype(jnp.bfloat16)[None],
        grad_inputs.astype(jnp.bfloat16)[None],
        gain_total,
        q_grad,
        kv_grad,
        o_grad,
        mlp_grads[0],
        mlp_grads[1],
        mlp_grads[2],
    )


def solution(mesh):
    in_specs = (
        P("fsdp", "ctx", None),
        P(),
        P("fsdp", None),
        P("fsdp", None),
        P("fsdp", None),
        P("fsdp", None),
        P("fsdp", None),
        P("fsdp", None),
        P("fsdp", "ctx", None),
        P("fsdp", None),
    )
    out_specs = (
        P("fsdp", "ctx", None),
        P("fsdp", "ctx", None),
        P(None, "ctx"),
        P("fsdp", "ctx"),
        P("fsdp", "ctx"),
        P("fsdp", "ctx"),
        P("fsdp", "ctx"),
        P("fsdp", "ctx"),
        P("fsdp", "ctx"),
    )
    return jax.shard_map(body, mesh=mesh, in_specs=in_specs, out_specs=out_specs, check_vma=False)
```

```python
import jax
import jax.numpy as jnp
from jax import lax
from jax.experimental import pallas as pl
from jax.experimental.pallas import tpu as pltpu
from jax.sharding import PartitionSpec as P

HEADS = 10
HEAD = 256
WINDOW = 2048


EPSILON = 1e-06
MASKED = -1e30
LOWEST = -1e29
VMEM = 56 * 1024 * 1024
FREE = pl.CostEstimate(flops=0, bytes_accessed=0, transcendentals=0)


def shifted(value, axis, steps):
    count = lax.axis_size(axis)
    initial, last = (max(0, -steps), min(count, count - steps))
    return lax.ppermute(value, axis, [(source, source + steps) for source in range(initial, last)])


def swap(value, axis, bit):
    return lax.ppermute(value, axis, [(i, i ^ bit) for i in range(lax.axis_size(axis))])


def add16(left, right):
    return (left.astype(jnp.float32) + right.astype(jnp.float32)).astype(jnp.bfloat16)


def times_rows(left, right):
    return lax.dot_general(
        left, right, (((1,), (1,)), ((), ())), preferred_element_type=jnp.float32
    )


def gram_rows(left, right):
    return lax.dot_general(
        left, right, (((0,), (0,)), ((), ())), preferred_element_type=jnp.float32
    )


def product(left, right):
    return jnp.dot(left, right, preferred_element_type=jnp.float32)


def doc_info(doc_lengths, first_token, token_count):
    doc_ends = jnp.cumsum(doc_lengths)
    doc_starts = doc_ends - doc_lengths
    token_ids = first_token + jnp.arange(token_count, dtype=jnp.int32)
    segment = jnp.sum((doc_ends[None, :] <= token_ids[:, None]).astype(jnp.int32), 1)
    begins = jnp.max(
        jnp.where(doc_starts[None, :] <= token_ids[:, None], doc_starts[None, :], 0), 1
    )
    return (token_ids, segment, token_ids - begins)


def rope_angles(positions):
    half_width = HEAD // 2
    column = jnp.arange(half_width, dtype=jnp.float32)
    inverse = jnp.power(10000.0, -column / half_width)
    angles = positions.astype(jnp.float32)[:, None] * inverse[None, :]
    return (jnp.cos(angles), jnp.sin(angles))


def rotate(values, cosine, sine):
    half_width = values.shape[-1] // 2
    first_half = values[..., :half_width]
    second_half = values[..., half_width:]
    return jnp.concatenate(
        [first_half * cosine - second_half * sine, second_half * cosine + first_half * sine], -1
    )


def rotate_back(grad_in, cosine, sine):
    half_width = grad_in.shape[-1] // 2
    first_half = grad_in[..., :half_width]
    second_half = grad_in[..., half_width:]
    return jnp.concatenate(
        [first_half * cosine + second_half * sine, second_half * cosine - first_half * sine], -1
    )


def norm_scale(values):
    return lax.rsqrt(jnp.mean(values * values, -1, keepdims=True) + EPSILON)


def norm_back(grad_in, values, scale, gain):
    weighted = grad_in * gain
    return scale * weighted - values * scale * scale * scale * jnp.mean(
        weighted * values, -1, keepdims=True
    )


def head_rows(block, count):
    return jnp.concatenate([block[:, h * HEAD : (h + 1) * HEAD] for h in range(count)], 0)


def row_bounds(low_ref, first_key, tokens, count):
    high = first_key + lax.broadcasted_iota(jnp.int32, (1, tokens), 1)
    low = low_ref[0]
    return jnp.concatenate([low] * count, 1), jnp.concatenate([high] * count, 1)


def seen(start, shape, low, high):
    key = start + lax.broadcasted_iota(jnp.int32, shape, 0)
    return (key >= low) & (key <= high)


def turn(from_ref, to_ref, chunk):
    def step(j, carry):
        here = pl.ds(pl.multiple_of(j * chunk, chunk), chunk)
        to_ref[:, here] = from_ref[here, :].astype(jnp.float32).T.astype(jnp.bfloat16)
        return carry

    lax.fori_loop(0, from_ref.shape[0] // chunk, step, 0)


def attend_kernel(
    span_ref, pre_ref, cos_ref, sin_ref, low_ref, key_ref, value_ref, *refs, base, chunk
):
    out_ref, out_t_ref, rot_ref, log_ref, acc, value_t_ref = refs[-6:]

    @pl.when((pl.program_id(0) == 0) & (pl.program_id(1) == 0))
    def _():
        turn(value_ref, value_t_ref, chunk)

    tile = pl.program_id(0)
    tokens = pre_ref.shape[0]
    count = pre_ref.shape[1] // HEAD
    cosine, sine = cos_ref[...], sin_ref[...]
    half = HEAD // 2
    for h in range(count):
        first = pre_ref[:, h * HEAD : h * HEAD + half]
        second = pre_ref[:, h * HEAD + half : (h + 1) * HEAD]
        rot_ref[:, h * HEAD : h * HEAD + half] = (
            (first * cosine - second * sine) * HEAD ** (-0.5)
        ).astype(jnp.bfloat16)
        rot_ref[:, h * HEAD + half : (h + 1) * HEAD] = (
            (second * cosine + first * sine) * HEAD ** (-0.5)
        ).astype(jnp.bfloat16)
    query = head_rows(rot_ref[...], count)
    low, high = row_bounds(low_ref, base + tile * tokens, tokens, count)
    rows = count * tokens

    acc[...] = jnp.zeros_like(acc)

    def step(j, carry):
        top, total = carry
        start = pl.multiple_of(j * chunk, chunk)
        scores = lax.dot_general(
            key_ref[pl.ds(start, chunk), :], query, (((1,), (1,)), ((), ())),
            preferred_element_type=jnp.float32,
        )
        scores = jnp.where(seen(start, scores.shape, low, high), scores, MASKED)
        higher = jnp.maximum(top, jnp.max(scores, 0, keepdims=True))
        part = jnp.exp(scores - higher)
        shrink = jnp.exp(top - higher)
        acc[...] = acc[...] * shrink + lax.dot_general(
            value_t_ref[:, pl.ds(start, chunk)], part.astype(jnp.bfloat16), (((1,), (0,)), ((), ())),
            preferred_element_type=jnp.float32,
        )
        return higher, total * shrink + jnp.sum(part, 0, keepdims=True)

    top, total = lax.fori_loop(
        span_ref[0, tile], span_ref[1, tile], step,
        (jnp.full((1, rows), LOWEST, jnp.float32), jnp.zeros((1, rows), jnp.float32)),
    )
    log_ref[0, 0] = top + jnp.log(total)
    outs_t = acc[...] * (1.0 / total)
    outs = outs_t.T.astype(jnp.bfloat16)
    outs_t = outs_t.astype(jnp.bfloat16)
    for h in range(count):
        out_t_ref[h * HEAD : (h + 1) * HEAD, :] = outs_t[:, h * tokens : (h + 1) * tokens]
        out_ref[:, h * HEAD : (h + 1) * HEAD] = outs[h * tokens : (h + 1) * tokens]


def attend_back_kernel(
    span_ref, rot_ref, grad_ref, out_ref, log_ref, cos_ref, sin_ref, low_ref, key_ref, value_ref,
    *refs, base, chunk
):
    pre_ref, pre_t_ref, grad_kv_ref, grad_key_ref, grad_value_ref, acc, key_t_ref = refs[-7:]
    tile = pl.program_id(0)
    tokens = rot_ref.shape[0]
    count = rot_ref.shape[1] // HEAD

    @pl.when((tile == 0) & (pl.program_id(1) == 0))
    def _():
        turn(key_ref, key_t_ref, chunk)
        grad_key_ref[...] = jnp.zeros_like(grad_key_ref)
        grad_value_ref[...] = jnp.zeros_like(grad_value_ref)

    query = head_rows(rot_ref[...], count)
    grad = head_rows(grad_ref[...], count)
    outs = head_rows(out_ref[...], count)
    delta = jnp.sum((grad.astype(jnp.float32) * outs.astype(jnp.float32)).T, 0, keepdims=True)
    log_total = log_ref[0, 0]
    low, high = row_bounds(low_ref, base + tile * tokens, tokens, count)
    acc[...] = jnp.zeros_like(acc)

    def step(j, carry):
        start = pl.multiple_of(j * chunk, chunk)
        here = pl.ds(start, chunk)
        scores = lax.dot_general(
            key_ref[here, :], query, (((1,), (1,)), ((), ())), preferred_element_type=jnp.float32
        )
        grad_probs = lax.dot_general(
            value_ref[here, :], grad, (((1,), (1,)), ((), ())), preferred_element_type=jnp.float32
        )
        probs = jnp.where(seen(start, scores.shape, low, high), jnp.exp(scores - log_total), 0.0)
        grad_scores = (probs * (grad_probs - delta)).astype(jnp.bfloat16)
        grad_value_ref[here, :] += jnp.dot(
            probs.astype(jnp.bfloat16), grad, preferred_element_type=jnp.float32
        )
        grad_key_ref[here, :] += jnp.dot(grad_scores, query, preferred_element_type=jnp.float32)
        acc[...] += lax.dot_general(
            key_t_ref[:, here], grad_scores, (((1,), (0,)), ((), ())),
            preferred_element_type=jnp.float32,
        )
        return carry

    lax.fori_loop(span_ref[0, tile], span_ref[1, tile], step, 0)
    cosine, sine = cos_ref[...], sin_ref[...]
    half = HEAD // 2
    for h in range(count):
        own = acc[:, h * tokens : (h + 1) * tokens] * HEAD ** (-0.5)
        first, second = own[:half], own[half:]
        own = jnp.concatenate(
            [first * cosine + second * sine, second * cosine - first * sine], 0
        )
        pre_t_ref[h * HEAD : (h + 1) * HEAD, :] = own.astype(jnp.bfloat16)
        pre_ref[:, h * HEAD : (h + 1) * HEAD] = own.T.astype(jnp.bfloat16)

    @pl.when((tile == pl.num_programs(0) - 1) & (pl.program_id(1) == pl.num_programs(1) - 1))
    def _():
        grad_kv_ref[:, :HEAD] = grad_key_ref[...].astype(jnp.bfloat16)
        grad_kv_ref[:, HEAD:] = grad_value_ref[...].astype(jnp.bfloat16)


def attention_plan(tok_rows, key_count, low):
    tile = min(128, tok_rows)
    chunk = 256 if key_count % 256 == 0 else 128
    base = key_count - tok_rows
    tiles = tok_rows // tile
    begin = low[::tile] // chunk
    end = (base + (jnp.arange(tiles, dtype=jnp.int32) + 1) * tile + chunk - 1) // chunk
    return tile, chunk, base, jnp.stack([begin, end], 0).astype(jnp.int32)


GROUP = 10


def attend(query_pre, cosine, sine, low, window, deps=()):
    tok_rows = query_pre.shape[0]
    key_count = window.shape[0] - tok_rows
    tile, chunk, base, span = attention_plan(tok_rows, key_count, low)
    tiles = tok_rows // tile
    groups = HEADS // GROUP
    wide = GROUP * HEAD
    block = pl.BlockSpec((tile, wide), lambda i, g, s: (i, g))
    angle = pl.BlockSpec((tile, HEAD // 2), lambda i, g, s: (i, 0))
    return pl.pallas_call(
        lambda *refs: attend_kernel(*refs, base=base, chunk=chunk),
        grid_spec=pltpu.PrefetchScalarGridSpec(
            num_scalar_prefetch=1,
            grid=(tiles, groups),
            in_specs=[
                block,
                angle,
                angle,
                pl.BlockSpec((1, 1, tile), lambda i, g, s: (i, 0, 0)),
                pl.BlockSpec((key_count, HEAD), lambda i, g, s: (0, 0)),
                pl.BlockSpec((key_count, HEAD), lambda i, g, s: (0, 1)),
            ]
            + [pl.BlockSpec(memory_space=pl.ANY)] * len(deps),
            out_specs=[
                block,
                pl.BlockSpec((wide, tile), lambda i, g, s: (g, i)),
                block,
                pl.BlockSpec((1, 1, 1, GROUP * tile), lambda i, g, s: (i, g, 0, 0)),
            ],
            scratch_shapes=[
                pltpu.VMEM((HEAD, GROUP * tile), jnp.float32),
                pltpu.VMEM((HEAD, key_count), jnp.bfloat16),
            ],
        ),
        out_shape=[
            jax.ShapeDtypeStruct(query_pre.shape, jnp.bfloat16),
            jax.ShapeDtypeStruct(query_pre.shape[::-1], jnp.bfloat16),
            jax.ShapeDtypeStruct(query_pre.shape, jnp.bfloat16),
            jax.ShapeDtypeStruct((tiles, groups, 1, GROUP * tile), jnp.float32),
        ],
        compiler_params=pltpu.CompilerParams(vmem_limit_bytes=VMEM),
        cost_estimate=FREE,
        name="attend",
    )(span, query_pre, cosine, sine, low.reshape(tiles, 1, tile), window, window, *deps)


def attend_back(query_rot, grad_rows, attn_rows, log_total, cosine_t, sine_t, low, window, deps):
    tok_rows = query_rot.shape[0]
    key_count = window.shape[0] - tok_rows
    tile, chunk, base, span = attention_plan(tok_rows, key_count, low)
    tiles = tok_rows // tile
    groups = HEADS // GROUP
    wide = GROUP * HEAD
    block = pl.BlockSpec((tile, wide), lambda i, g, s: (i, g))
    angle = pl.BlockSpec((HEAD // 2, tile), lambda i, g, s: (0, i))
    return pl.pallas_call(
        lambda *refs: attend_back_kernel(*refs, base=base, chunk=chunk),
        grid_spec=pltpu.PrefetchScalarGridSpec(
            num_scalar_prefetch=1,
            grid=(tiles, groups),
            in_specs=[
                block,
                block,
                block,
                pl.BlockSpec((1, 1, 1, GROUP * tile), lambda i, g, s: (i, g, 0, 0)),
                angle,
                angle,
                pl.BlockSpec((1, 1, tile), lambda i, g, s: (i, 0, 0)),
                pl.BlockSpec((key_count, HEAD), lambda i, g, s: (0, 0)),
                pl.BlockSpec((key_count, HEAD), lambda i, g, s: (0, 1)),
            ]
            + [pl.BlockSpec(memory_space=pl.ANY)] * len(deps),
            out_specs=[
                block,
                pl.BlockSpec((wide, tile), lambda i, g, s: (g, i)),
                pl.BlockSpec((key_count, 2 * HEAD), lambda i, g, s: (0, 0)),
            ],
            scratch_shapes=[
                pltpu.VMEM((key_count, HEAD), jnp.float32),
                pltpu.VMEM((key_count, HEAD), jnp.float32),
                pltpu.VMEM((HEAD, GROUP * tile), jnp.float32),
                pltpu.VMEM((HEAD, key_count), jnp.bfloat16),
            ],
        ),
        out_shape=[
            jax.ShapeDtypeStruct(query_rot.shape, jnp.bfloat16),
            jax.ShapeDtypeStruct(query_rot.shape[::-1], jnp.bfloat16),
            jax.ShapeDtypeStruct((key_count, 2 * HEAD), jnp.bfloat16),
        ],
        compiler_params=pltpu.CompilerParams(vmem_limit_bytes=VMEM),
        cost_estimate=FREE,
        name="attend_back",
    )(
        span, query_rot, grad_rows, attn_rows, log_total, cosine_t, sine_t, low.reshape(tiles, 1, tile),
        window, window, *deps,
    )


def nt(left, right):
    return lax.dot_general(
        left, right, (((1,), (1,)), ((), ())), preferred_element_type=jnp.float32
    )


def tn(left, right):
    return lax.dot_general(
        left, right, (((0,), (0,)), ((), ())), preferred_element_type=jnp.float32
    )


def flat(ref):
    block = ref[...]
    return block.reshape(-1, block.shape[-1])


def units_kernel(core_ref, *refs):
    tokens, cots = refs[0:2], refs[2:4]
    gate_ref, up_ref, down_ref = refs[4:7]
    out_ref = refs[-1]
    gate_rows, up_rows, down_rows = flat(gate_ref), flat(up_ref), flat(down_ref)

    def one(token_ref, cot_ref):
        gate = nt(gate_rows, token_ref[...])
        up = nt(up_rows, token_ref[...])
        grad_mixed = nt(down_rows, cot_ref[...])
        root = (2.0 / jnp.pi) ** 0.5
        square = gate * gate
        curve = jnp.tanh(root * (gate + 0.044715 * (square * gate)))
        upper = 0.5 * (1.0 + curve)
        activated = gate * upper
        slope = upper + 0.5 * gate * (1.0 - curve * curve) * (root * (1.0 + 0.134145 * square))
        out_ref[0] = (grad_mixed * up * slope).astype(jnp.bfloat16)
        out_ref[1] = (grad_mixed * activated).astype(jnp.bfloat16)
        out_ref[2] = (activated * up).astype(jnp.bfloat16)

    for j in (0, 1):
        pl.when(pl.program_id(1) == j)(lambda j=j: one(tokens[j], cots[j]))


def units(tokens, cots, weights, core, group, held, deps=()):
    cols, width = tokens[0].shape
    hidden = weights.hidden
    token_block = pl.BlockSpec((cols, width), lambda i, j, s: (0, 0))
    extra = (() if held is None else (held,)) + tuple(deps)
    return pl.pallas_call(
        units_kernel,
        grid_spec=pltpu.PrefetchScalarGridSpec(
            num_scalar_prefetch=1,
            grid=(2, 2),
            in_specs=[token_block] * 4
            + weights.specs(2, lambda i, j, s: (i, 0), width)
            + [pl.BlockSpec(memory_space=pl.ANY)] * len(extra),
            out_specs=pl.BlockSpec(
                (3, hidden // 2, cols), lambda i, j, s: (0, i, 2 * group + j)
            ),
        ),
        out_shape=jax.ShapeDtypeStruct((3, hidden, 4 * cols), jnp.bfloat16),
        input_output_aliases={} if held is None else {8: 0},
        compiler_params=pltpu.CompilerParams(vmem_limit_bytes=VMEM),
        cost_estimate=FREE,
        name="units",
    )(core, *tokens, *cots, *weights.arrays, *extra)


class OwnWeights:
    def __init__(self, shards):
        self.arrays = tuple(shards)
        self.hidden = shards[0].shape[0] // 2

    def specs(self, cuts, place, width):
        def index(*grid):
            row, col = place(*grid)
            return (grid[-1][0] * cuts + row, col)

        return [pl.BlockSpec((self.hidden // cuts, width), index)] * len(self.arrays)


class FarWeights:
    def __init__(self, gathered):
        parts, count, rows, width = gathered.shape
        self.hidden = parts * rows
        if rows % 16:
            gathered = gathered.reshape(2, parts // 2, count, rows, width)
            gathered = gathered.transpose(0, 2, 1, 3, 4).reshape(2, count, -1, width)
        self.arrays = (gathered,) * count

    def specs(self, cuts, place, width):
        parts, count, rows, _ = self.arrays[0].shape

        def spec(which):
            def index(*grid):
                row, col = place(*grid)
                return (row, which, 0, col)

            return pl.BlockSpec((parts // cuts, 1, rows, width), index)

        return [spec(which) for which in range(count)]


def sums_kernel(core_ref, *refs, count):
    total = 0.0
    for act_ref, weight_ref in zip(refs[:count], refs[count : 2 * count], strict=True):
        total = total + tn(act_ref[0], flat(weight_ref))
    refs[-1][...] = total.astype(jnp.bfloat16)


def sums(acts, weights, core, group, which, block=None, deps=()):
    all_tokens = acts[0].shape[2]
    width = weights[0].arrays[0].shape[-1]
    rows = all_tokens // 4
    blocks = 2 if block is None else 1
    cols = 512 if width % 512 == 0 else width // 2
    first = 2 * group + (block or 0)

    def act_spec(act, kind):
        return pl.BlockSpec((1, act.shape[1], rows), lambda n, t, s: (kind, 0, first + t))

    act_specs, weight_specs, act_args, weight_args = [], [], [], []
    for act, weight in zip(acts, weights, strict=True):
        specs = weight.specs(1, lambda n, t, s: (0, n), cols)
        for kind in which:
            act_specs.append(act_spec(act, kind))
            act_args.append(act)
            weight_specs.append(specs[kind])
            weight_args.append(weight.arrays[kind])
    return pl.pallas_call(
        lambda *refs: sums_kernel(*refs, count=len(act_args)),
        grid_spec=pltpu.PrefetchScalarGridSpec(
            num_scalar_prefetch=1,
            grid=(width // cols, blocks),
            in_specs=act_specs + weight_specs + [pl.BlockSpec(memory_space=pl.ANY)] * len(deps),
            out_specs=pl.BlockSpec((rows, cols), lambda n, t, s: (t, n)),
        ),
        out_shape=jax.ShapeDtypeStruct((blocks * rows, width), jnp.bfloat16),
        compiler_params=pltpu.CompilerParams(vmem_limit_bytes=VMEM),
        cost_estimate=FREE,
        name="sums",
    )(core, *act_args, *weight_args, *deps)


def grams_kernel(acts_ref, *refs, sets):
    out_ref = refs[-1]

    def one(rights):
        step = rights[0].shape[0]
        total = 0.0
        for i, right_ref in enumerate(rights):
            total = total + jnp.dot(
                acts_ref[0, :, i * step : (i + 1) * step], right_ref[...],
                preferred_element_type=jnp.float32,
            )
        out_ref[0] = total.astype(jnp.bfloat16)

    if sets == 1:
        one(refs[0:4])
    else:
        pl.when(pl.program_id(0) < 2)(lambda: one(refs[0:4]))
        pl.when(pl.program_id(0) == 2)(lambda: one(refs[4:8]))


def grams(acts, tokens, cots, pairs, kinds, deps=()):
    _, hidden, all_tokens = acts.shape
    step, width = tokens[0].shape
    cols = width // pairs
    first, count = kinds[0], len(kinds)
    if cols % 128:
        parts = []
        for kind in kinds:
            whole = sum(
                product(acts[kind, :, i * step : (i + 1) * step], right)
                for i, right in enumerate(cots if kind == 2 else tokens)
            )
            parts.append(whole.astype(jnp.bfloat16))
        return jnp.concatenate(parts, 0).reshape(count * hidden, pairs, cols).transpose(1, 0, 2)
    if count == 3:
        specs = [pl.BlockSpec((step, cols), lambda k, p: (0, jnp.where(k < 2, p, pairs - 1)))] * 4
        specs = specs + [pl.BlockSpec((step, cols), lambda k, p: (0, jnp.where(k < 2, 0, p)))] * 4
        rights = tuple(tokens) + tuple(cots)
    else:
        specs = [pl.BlockSpec((step, cols), lambda k, p: (0, p))] * 4
        rights = tuple(cots) if first == 2 else tuple(tokens)
    return pl.pallas_call(
        lambda *refs: grams_kernel(*refs, sets=len(rights) // 4),
        grid=(count, pairs),
        in_specs=[pl.BlockSpec((1, hidden, all_tokens), lambda k, p: (first + k, 0, 0))]
        + specs
        + [pl.BlockSpec(memory_space=pl.ANY)] * len(deps),
        out_specs=pl.BlockSpec((1, hidden, cols), lambda k, p: (p, k, 0)),
        out_shape=jax.ShapeDtypeStruct((pairs, count * hidden, cols), jnp.bfloat16),
        compiler_params=pltpu.CompilerParams(vmem_limit_bytes=VMEM),
        cost_estimate=FREE,
        name="grams",
    )(acts, *rights, *deps)


class Gathered:
    def __init__(self, own, others, shard):
        count, _, rows, width = others.shape
        if rows % 16:
            others = others.transpose(1, 0, 2, 3).reshape(1, -1, count * rows, width)
        self.own, self.others = own, others
        self.shard = shard.reshape(1).astype(jnp.int32)
        self.shards = others.shape[1] + 1

    def place(self, step, shard_ref):
        return lax.rem(shard_ref[0] + self.shards - step, self.shards)

    def specs(self):
        count, _, rows, width = self.others.shape
        return [
            pl.BlockSpec(self.own.shape, lambda r, s: (0, 0)),
            pl.BlockSpec((count, 1, rows, width), lambda r, s: (0, jnp.maximum(r - 1, 0), 0, 0)),
        ]


def by_shard(own_ref, others_ref, use):
    pl.when(pl.program_id(0) == 0)(lambda: use(own_ref[...]))
    pl.when(pl.program_id(0) > 0)(lambda: use(flat(others_ref)))


def spread_kernel(shard_ref, left_ref, own_ref, others_ref, *refs):
    out_ref = refs[-1]

    def use(weight):
        out_ref[...] = nt(left_ref[...], weight).astype(out_ref.dtype)

    by_shard(own_ref, others_ref, use)


def spread(left, weight, dtype, deps=()):
    tokens, width = left.shape
    rows = weight.own.shape[0]
    return pl.pallas_call(
        spread_kernel,
        grid_spec=pltpu.PrefetchScalarGridSpec(
            num_scalar_prefetch=1,
            grid=(weight.shards,),
            in_specs=[pl.BlockSpec((tokens, width), lambda r, s: (0, 0))]
            + weight.specs()
            + [pl.BlockSpec(memory_space=pl.ANY)] * len(deps),
            out_specs=pl.BlockSpec((tokens, rows), lambda r, s: (0, weight.place(r, s))),
        ),
        out_shape=jax.ShapeDtypeStruct((tokens, weight.shards * rows), dtype),
        compiler_params=pltpu.CompilerParams(vmem_limit_bytes=VMEM),
        cost_estimate=FREE,
        name="spread",
    )(weight.shard, left, weight.own, weight.others, *deps)


def collect_kernel(shard_ref, left_ref, own_ref, others_ref, start_ref, gain_ref, *refs, outs):
    refs = refs[-outs:]
    total_ref = refs[0]

    @pl.when(pl.program_id(0) == 0)
    def _():
        total_ref[...] = start_ref[...].astype(jnp.float32)

    def use(weight):
        total_ref[...] += jnp.dot(left_ref[...], weight, preferred_element_type=jnp.float32)

    by_shard(own_ref, others_ref, use)
    if outs > 1:

        @pl.when(pl.program_id(0) == pl.num_programs(0) - 1)
        def _():
            rows = min(128, total_ref.shape[0])

            def norm(i, carry):
                here = pl.ds(pl.multiple_of(i * rows, rows), rows)
                total = total_ref[here, :]
                scale = norm_scale(total)
                refs[1][here, :] = (total * scale * gain_ref[...]).astype(jnp.bfloat16)
                refs[2][here, :] = jnp.broadcast_to(scale, (rows, 128))
                return carry

            lax.fori_loop(0, total_ref.shape[0] // rows, norm, 0)


def collect(left, weight, start, gain=None, deps=()):
    tokens = left.shape[0]
    rows, width = weight.own.shape
    whole = pl.BlockSpec((tokens, width), lambda r, s: (0, 0))
    shapes, specs = [jax.ShapeDtypeStruct((tokens, width), jnp.float32)], [whole]
    if gain is not None:
        shapes.append(jax.ShapeDtypeStruct((tokens, width), jnp.bfloat16))
        shapes.append(jax.ShapeDtypeStruct((tokens, 128), jnp.float32))
        specs.extend([whole, pl.BlockSpec((tokens, 128), lambda r, s: (0, 0))])
    gain_row = jnp.zeros((1, width), jnp.float32) if gain is None else gain.reshape(1, width)
    return pl.pallas_call(
        lambda *refs: collect_kernel(*refs, outs=len(specs)),
        grid_spec=pltpu.PrefetchScalarGridSpec(
            num_scalar_prefetch=1,
            grid=(weight.shards,),
            in_specs=[pl.BlockSpec((tokens, rows), lambda r, s: (0, weight.place(r, s)))]
            + weight.specs()
            + [whole, pl.BlockSpec((1, width), lambda r, s: (0, 0))]
            + [pl.BlockSpec(memory_space=pl.ANY)] * len(deps),
            out_specs=specs,
        ),
        out_shape=shapes,
        compiler_params=pltpu.CompilerParams(vmem_limit_bytes=VMEM),
        cost_estimate=FREE,
        name="collect",
    )(weight.shard, left, weight.own, weight.others, start, gain_row, *deps)


def cross_kernel(core_ref, *refs, lefts, gained, added):
    right_ref, out_ref = refs[lefts], refs[-1]
    first = 0

    def put(part, rows):
        here = (0, slice(None), slice(first, first + rows))
        if added:
            part = part + refs[lefts + 1 + gained][here].astype(jnp.float32)
        out_ref[here] = part.astype(jnp.bfloat16)

    for left_ref in refs[:lefts]:
        shards, _, rows, tokens = left_ref.shape
        left = left_ref[...].reshape(shards * rows, tokens)
        part = jnp.dot(left, right_ref[...], preferred_element_type=jnp.float32)
        put(part.reshape(shards, rows, -1), rows)
        first = first + rows
    if gained:
        gains = refs[lefts + 1][...].astype(jnp.float32)
        put(jnp.broadcast_to(gains[None], (out_ref.shape[1],) + gains.shape), gains.shape[0])


def cross(lefts, right, core, shards, pairs, gains=None, add=None, deps=(), first=0, of=None, into=None):
    tokens, width = right.shape
    cols = width // pairs
    views = [left.reshape(shards, 2, -1, tokens) for left in lefts]
    rows = [view.shape[2] for view in views]
    total = sum(rows) + (0 if gains is None else gains.shape[0])
    if cols % 128:
        picked = jnp.concatenate(
            [lax.dynamic_index_in_dim(view, core[0], 1, keepdims=False) for view in views], 1
        )
        whole = product(picked.reshape(-1, tokens), right).reshape(shards, sum(rows), width)
        if gains is not None:
            extra = jnp.broadcast_to(gains.astype(jnp.float32)[None], (shards,) + gains.shape)
            whole = jnp.concatenate([whole, extra], 1)
        whole = whole.reshape(shards, total, pairs, cols).transpose(2, 0, 1, 3)
        if add is not None:
            whole = whole + add[:, :, first : first + total].astype(jnp.float32)
        whole = whole.astype(jnp.bfloat16)
        if of is None:
            return whole
        if into is None:
            into = jnp.zeros((pairs, shards, of, cols), jnp.bfloat16)
        return lax.dynamic_update_slice(into, whole, (0, 0, first, 0))
    block = pl.BlockSpec((1, shards, total, cols), lambda p, s: (p, 0, first // total, 0))
    kept = () if into is None else (into,)
    specs = [
        pl.BlockSpec((shards, 1, count, tokens), lambda p, s: (0, s[0], 0, 0)) for count in rows
    ]
    specs.append(pl.BlockSpec((tokens, cols), lambda p, s: (0, p)))
    args = [*views, right]
    if gains is not None:
        specs.append(pl.BlockSpec((gains.shape[0], cols), lambda p, s: (0, p)))
        args.append(gains)
    if add is not None:
        specs.append(block)
        args.append(add)
    return pl.pallas_call(
        lambda *refs: cross_kernel(
            *refs, lefts=len(views), gained=gains is not None, added=add is not None
        ),
        grid_spec=pltpu.PrefetchScalarGridSpec(
            num_scalar_prefetch=1,
            grid=(pairs,),
            in_specs=specs + [pl.BlockSpec(memory_space=pl.ANY)] * (len(kept) + len(deps)),
            out_specs=block,
        ),
        out_shape=jax.ShapeDtypeStruct((pairs, shards, of or total, cols), jnp.bfloat16),
        input_output_aliases={1 + len(args): 0} if kept else {},
        compiler_params=pltpu.CompilerParams(vmem_limit_bytes=VMEM),
        cost_estimate=FREE,
        name="cross",
    )(core, *args, *kept, *deps)


def swap(value, axis, bit):
    return lax.ppermute(value, axis, [(i, i ^ bit) for i in range(lax.axis_size(axis))])


def after(value, *others):
    return lax.optimization_barrier((value, *others))[0]


def same_core():
    count = lax.axis_size("ctx")
    return [list(range(0, count, 2)), list(range(1, count, 2))]


def own_part(shard, place):
    part = shard.shape[0] // lax.axis_size("ctx")
    return lax.dynamic_slice_in_dim(shard, place * part, part, 0)


def together(*values):
    return lax.optimization_barrier(values)


def halving_scatter(blocks, axis, place):
    held, bit = blocks, 1
    while held.shape[0] > 1:
        both = held.reshape((held.shape[0] // 2, 2) + held.shape[1:])
        mine = (place // bit) % 2
        keep = lax.dynamic_index_in_dim(both, mine, 1, keepdims=False)
        give = lax.dynamic_index_in_dim(both, 1 - mine, 1, keepdims=False)
        total = keep.astype(jnp.float32) + swap(give, axis, bit).astype(jnp.float32)
        held = total.astype(jnp.bfloat16)
        bit = 2 * bit
    return total[0]


def step_ring(value, axis):
    count = lax.axis_size(axis)
    return lax.ppermute(value, axis, [(i, (i + 1) % count) for i in range(count)])


def ring(value, axis):
    arrived = []
    for _ in range(lax.axis_size(axis) - 1):
        value = step_ring(value, axis)
        arrived.append(value)
    return arrived


def exchanges(axis):
    bits, bit = [], 2
    while bit < lax.axis_size(axis):
        bits.append(bit)
        bit = 2 * bit
    return bits + [1]


def pairs_gather(value):
    pairs = lax.axis_size("ctx") // 2
    if pairs == 4:
        half = value.shape[0] // 2
        x_all, y_all = swap(value, "ctx", 2), swap(value, "ctx", 4)
        low = swap(y_all[:half], "ctx", 2)
        high = swap(x_all[half:], "ctx", 4)
        return [(0, [value]), (2, [x_all]), (4, [y_all]), (6, [low, high])]
    held, bit = [(0, value)], 2
    while bit < 2 * pairs:
        held = held + [(bits ^ bit, swap(item, "ctx", bit)) for bits, item in held]
        bit = 2 * bit
    return [(bits, [item]) for bits, item in held]


def window_gather(value, reach, place):
    rows = value.shape[0]
    out = jnp.zeros(((reach + 2) * rows,) + value.shape[1:], value.dtype)
    parts = [(bits, part, i) for bits, held in pairs_gather(value) for i, part in enumerate(held)]
    for bits, part, i in parts:
        both = ((bits, part), (bits ^ 1, swap(part, "ctx", 1)))
        for other, block in both:
            spot = (place ^ other) - place + reach
            spot = jnp.where((spot < 0) | (spot > reach), reach + 1, spot)
            start = spot * rows + (i * block.shape[0])
            out = lax.dynamic_update_slice_in_dim(out, block, start, 0)
    return out


def place_block(out, block, place):
    return lax.dynamic_update_index_in_dim(out, block, place, 0)


def in_places(own, arrived, place):
    count = len(arrived) + 1
    out = jnp.zeros((count,) + own.shape, own.dtype)
    for step, value in enumerate([own, *arrived]):
        out = lax.dynamic_update_index_in_dim(out, value, lax.rem(place + count - step, count), 0)
    return out


def in_order(gathered, first, part):
    mine = gathered[:, :, first : first + part].transpose(1, 0, 2, 3)
    return mine.reshape(-1, gathered.shape[-1])


def body(
    inputs,
    norm_gains,
    q_weight,
    kv_weight,
    o_weight,
    gate_weight,
    up_weight,
    down_weight,
    cotangent,
    doc_lengths,
):
    x_rows = inputs[0].astype(jnp.float32)
    grad_out = cotangent[0]
    tok_rows, width = x_rows.shape
    place = lax.axis_index("ctx")
    ctx_count = lax.axis_size("ctx")
    pairs = ctx_count // 2
    core = place % 2
    pair = place // 2
    own_core = core.reshape(1).astype(jnp.int32)
    shard = lax.axis_index("fsdp")
    shards = lax.axis_size("fsdp")
    reach = min(ctx_count - 1, (WINDOW + tok_rows - 2) // tok_rows)
    key_count = (reach + 1) * tok_rows
    first_token = place * tok_rows
    token_ids, segment, positions = doc_info(doc_lengths[0], first_token, tok_rows)
    low = jnp.maximum(token_ids - positions, token_ids - (WINDOW - 1)) - (
        first_token - reach * tok_rows
    )
    cosine, sine = rope_angles(positions)
    gain_attn = norm_gains[0]
    gain_mlp = norm_gains[1]

    q_part, kv_part, o_part = (own_part(w, place) for w in (q_weight, kv_weight, o_weight))
    kv_z = in_places(kv_part, ring(kv_part, "fsdp"), shard)
    moving = after(q_part, kv_z)
    held, origins = kv_z[None], [place]
    q_arrived = []
    for bit in exchanges("ctx"):
        if len(q_arrived) < shards - 1:
            moving = step_ring(moving, "fsdp")
            q_arrived.append(moving)
        held = jnp.concatenate([held, swap(held, "ctx", bit)], 0)
        origins = origins + [origin ^ bit for origin in origins]
        held, moving = together(held, moving)
    while len(q_arrived) < shards - 1:
        moving = step_ring(moving, "fsdp")
        q_arrived.append(moving)
    kv_all = jnp.zeros_like(held)
    for step, origin in enumerate(origins):
        kv_all = place_block(kv_all, held[step], origin)
    q_ring = jnp.stack(q_arrived, 0)
    q_ring, kv_all = together(q_ring, kv_all)
    q_all = lax.all_gather(q_ring, "ctx", axis=0)

    half_rows = gate_weight.shape[0] // 2
    part_rows = half_rows // pairs
    cut = (part_rows * 7 // 15 + 15) // 16 * 16
    far_rows, last_rows = cut // 4, part_rows - cut
    mine = jnp.stack(
        [
            lax.dynamic_slice_in_dim(w, core * half_rows + pair * part_rows, part_rows, 0)
            for w in (gate_weight, up_weight, down_weight)
        ],
        0,
    )
    mine, _ = together(mine, q_ring)
    own_weights = OwnWeights((gate_weight, up_weight, down_weight))

    scale_one = norm_scale(x_rows)
    normed_one = (x_rows * scale_one * gain_attn).astype(jnp.bfloat16)
    kv_full = in_order(kv_all, 0, kv_part.shape[0])
    kv_pre = times_rows(normed_one, kv_full)
    key_rot = rotate(kv_pre[:, :HEAD], cosine, sine).astype(jnp.bfloat16)
    kv_local = jnp.concatenate([key_rot, kv_pre[:, HEAD:].astype(jnp.bfloat16)], 1)
    kv_local, moving = together(kv_local, o_part)
    kv_window = window_gather(kv_local, reach, place)
    o_arrived = ring(moving, "fsdp")
    cot_rows = tok_rows // 8
    cot_first = swap(after(grad_out[:cot_rows], o_arrived[-1]), "fsdp", 1)
    far_first = swap(after(mine[:, :far_rows], o_arrived[-1]), "fsdp", 2)
    o_ring = jnp.stack(o_arrived, 0)
    q_all, o_ring, far_first, cot_first, kv_window, normed_one, cosine_t, sine_t = together(
        q_all, o_ring, far_first, cot_first, kv_window, normed_one, cosine.T, sine.T
    )
    o_all = lax.all_gather(o_ring, "ctx", axis=0)
    q_full = Gathered(q_weight, q_all, shard)
    o_full = Gathered(o_weight, o_all, shard)
    far_second = swap(after(mine[:, far_rows : part_rows - last_rows], o_ring), "fsdp", 2)
    cot_second = swap(after(grad_out[cot_rows:], o_ring), "fsdp", 1)
    query_pre = spread(normed_one, q_full, jnp.float32)
    attn_rows, attn_rows_t, query_rot, log_total = attend(
        query_pre, cosine, sine, low, kv_window
    )
    far_last = mine[:, part_rows - last_rows :]
    log_total, cot_second, far_second, far_last = together(
        log_total, cot_second, far_second, far_last
    )
    far_third = swap(far_last, "fsdp", 2)
    near_cots = (grad_out, swap(grad_out, "ctx", 1))
    cot_across = jnp.concatenate([cot_first, cot_second], 0)
    cots = [near_cots, (cot_across, swap(cot_across, "ctx", 1))]

    def over_plane(part):
        return lax.all_gather(part, "ctx", axis=0, axis_index_groups=same_core())

    far_a = FarWeights(
        over_plane(jnp.concatenate([far_first, far_second], 1))
    )
    hidden_one, normed_two, scale_two = collect(attn_rows, o_full, inputs[0], gain_mlp)
    scale_two = scale_two[:, :1]

    near = (normed_two, swap(normed_two, "ctx", 1))
    across = swap(normed_two, "fsdp", 1)
    own_acts = units(near, near_cots, own_weights, own_core, 0, None)
    a_acts = units(near, near_cots, far_a, own_core, 0, None, (own_acts, cots[1][1]))
    across, a_acts, far_third = together(across, a_acts, far_third)
    far = (across, swap(across, "ctx", 1))
    far_b = FarWeights(over_plane(far_third))
    own_acts = units(far, cots[1], own_weights, own_core, 1, own_acts, (a_acts,))
    a_acts = units(far, cots[1], far_a, own_core, 1, a_acts, (own_acts,))
    near_far, cot_rows = near + far, cots[0] + cots[1]

    def over_pairs(blocks):
        mine = lax.psum_scatter(
            blocks, "ctx", scatter_dimension=0, tiled=False, axis_index_groups=same_core()
        )
        return lax.optimization_barrier(mine)

    a_grams = grams(a_acts, near_far, cot_rows, pairs, (0, 1, 2))
    b_acts = units(near, cots[0], far_b, own_core, 0, None, (a_grams,))
    b_acts = units(far, cots[1], far_b, own_core, 1, b_acts)
    b_grams = grams(b_acts, near_far, cot_rows, pairs, (0, 1, 2))
    a_sums, b_sums = over_pairs(a_grams), over_pairs(b_grams)
    acts, weights = (own_acts, a_acts, b_acts), (own_weights, far_a, far_b)

    def group_sums(group, which, block, deps):
        return sums(acts, weights, own_core, group, which, block, deps)

    own_gate_up = grams(own_acts, near_far, cot_rows, pairs, (0, 1), (b_grams,))
    give = group_sums(1, (0, 1), 1, (own_gate_up,))
    own_gate_up = over_pairs(own_gate_up)
    got = swap(give, "ctx", 1)
    near_give = group_sums(0, (0, 1), 1, (give,))
    near_got = swap(near_give, "ctx", 1)
    keep = group_sums(1, (0, 1), 0, (near_give, a_sums))
    total = add16(keep, got)
    moved = swap(total, "fsdp", 1)
    own_down = grams(own_acts, near_far, cot_rows, pairs, (2,), (total, near_got))
    near_keep = group_sums(0, (0, 1), 0, (own_down,))
    out_give = group_sums(1, (2,), 1, (near_keep,))
    out_got = swap(out_give, "ctx", 1)
    out_keep = group_sums(1, (2,), 0, (out_give,))
    moved, own_down, near_keep, out_keep, a_sums = together(
        moved, own_down, near_keep, out_keep, a_sums
    )
    own_down = over_pairs(own_down)
    grad_normed_two = (
        near_keep.astype(jnp.float32) + near_got.astype(jnp.float32) + moved.astype(jnp.float32)
    )
    grad_hidden = grad_out.astype(jnp.float32) + norm_back(
        grad_normed_two, hidden_one, scale_two, gain_mlp
    )
    gain_mlp_grad = jnp.sum(grad_normed_two * hidden_one * scale_two, 0)
    grad_branch = grad_hidden.astype(jnp.bfloat16)
    grad_attended = spread(grad_branch, o_full, jnp.bfloat16, (b_sums,))

    gate_rows = b_sums.shape[0] // 3
    a_all = swap(a_sums, "fsdp", 2)
    grad_query_pre, grad_query_pre_t, grad_kv = attend_back(
        query_rot, grad_attended, attn_rows, log_total, cosine_t, sine_t, low, kv_window,
        (out_keep,),
    )
    grad_stack = grad_kv.reshape(reach + 1, tok_rows, 2 * HEAD)
    moved_kv = [shifted(grad_stack[reach - hop], "ctx", -hop) for hop in range(1, reach + 1)]
    out_total = add16(out_keep, out_got)
    q_give = cross(
        [grad_query_pre_t], normed_one, 1 - own_core, shards, pairs,
        deps=(grad_kv, a_all, own_gate_up, out_total),
    )
    q_got = swap(q_give, "ctx", 1)
    q_half, kv_half = q_weight.shape[0] // 2, kv_weight.shape[0] // 2
    okv_rows = q_half + kv_half + 16
    okv_give = cross(
        [attn_rows_t], grad_branch, 1 - own_core, shards, pairs, deps=(q_give,), of=okv_rows
    )
    q_sums = cross(
        [grad_query_pre_t], normed_one, own_core, shards, pairs, None, q_got, (okv_give,)
    )
    moved_kv, q_sums, b_sums = together(moved_kv, q_sums, b_sums)
    b_gate = swap(b_sums[:gate_rows], "fsdp", 2)
    b_up = swap(after(b_sums[gate_rows : 2 * gate_rows], b_gate), "fsdp", 2)
    b_down = swap(after(b_sums[2 * gate_rows :], b_up), "fsdp", 2)
    q_pairs = over_pairs(q_sums)
    own_kv_grad = grad_stack[reach].astype(jnp.float32)
    for block in moved_kv:
        own_kv_grad = own_kv_grad + block.astype(jnp.float32)
    grad_kv_pre = jnp.concatenate(
        [rotate_back(own_kv_grad[:, :HEAD], cosine, sine), own_kv_grad[:, HEAD:]], 1
    ).astype(jnp.bfloat16)
    (grad_normed_one,) = collect(
        grad_query_pre, q_full, product(grad_kv_pre, kv_full)
    )
    gain_attn_grad = jnp.sum(grad_normed_one * x_rows * scale_one, 0)
    gains = jnp.stack([gain_attn_grad, gain_mlp_grad], 0).astype(jnp.bfloat16)
    gains = jnp.concatenate([gains, jnp.zeros((14, width), jnp.bfloat16)], 0)
    kv_left = [grad_kv_pre.T]
    okv_give = cross(
        kv_left, normed_one, 1 - own_core, shards, pairs, gains, None, (b_gate,), q_half,
        okv_rows, okv_give,
    )
    okv_got = swap(okv_give, "ctx", 1)
    near_out = sums(acts, weights, own_core, 0, (2,), None, (okv_give,))
    near_out_got = swap(near_out[tok_rows:], "ctx", 1)
    okv_sums = cross(
        [attn_rows_t], grad_branch, own_core, shards, pairs, None, okv_got, (near_out, b_up),
        of=okv_rows,
    )
    okv_sums = cross(
        kv_left, normed_one, own_core, shards, pairs, gains, okv_got, (own_down, q_pairs), q_half, okv_rows,
        okv_sums,
    )
    grad_inputs = grad_hidden + norm_back(grad_normed_one, x_rows, scale_one, gain_attn)

    out_cols = width // ctx_count

    def both_halves(mine):
        keep = lax.dynamic_slice_in_dim(mine, core * out_cols, out_cols, 1)
        give = lax.dynamic_slice_in_dim(mine, (1 - core) * out_cols, out_cols, 1)
        got = swap(give.astype(jnp.bfloat16), "ctx", 1).astype(jnp.float32)
        lower = jnp.where(core == 0, keep, got)
        upper = jnp.where(core == 0, got, keep)
        return jnp.concatenate([lower, upper], 0)

    okv_pairs = over_pairs(okv_sums)
    out_moved = swap(out_total, "fsdp", 1)
    q_mine = halving_scatter(q_pairs, "fsdp", shard)
    result = hidden_one + (
        near_out[:tok_rows].astype(jnp.float32)
        + near_out_got.astype(jnp.float32)
        + out_moved.astype(jnp.float32)
    )
    q_grad = both_halves(q_mine)
    okv_mine = halving_scatter(okv_pairs, "fsdp", shard)
    o_grad = both_halves(okv_mine[:q_half])
    kv_grad = both_halves(okv_mine[q_half : q_half + kv_half])
    gain_total = lax.dynamic_slice_in_dim(
        okv_mine[q_half + kv_half : q_half + kv_half + 2], core * out_cols, out_cols, 1
    )

    a_all = a_all.reshape(3, pairs, cut, -1)
    b_all = jnp.concatenate([b_gate, b_up, b_down], 0).reshape(3, pairs, part_rows - cut, -1)
    own_all = (own_gate_up[:half_rows], own_gate_up[half_rows:], own_down)
    mlp_grads = []
    for kind in range(3):
        others = jnp.concatenate([a_all[kind], b_all[kind]], 1).reshape(half_rows, -1)
        mlp_grads.append(
            both_halves(own_all[kind].astype(jnp.float32) + others.astype(jnp.float32))
        )

    return (
        result.astype(jnp.bfloat16)[None],
        grad_inputs.astype(jnp.bfloat16)[None],
        gain_total,
        q_grad,
        kv_grad,
        o_grad,
        mlp_grads[0],
        mlp_grads[1],
        mlp_grads[2],
    )


def solution(mesh):
    in_specs = (
        P("fsdp", "ctx", None),
        P(),
        P("fsdp", None),
        P("fsdp", None),
        P("fsdp", None),
        P("fsdp", None),
        P("fsdp", None),
        P("fsdp", None),
        P("fsdp", "ctx", None),
        P("fsdp", None),
    )
    out_specs = (
        P("fsdp", "ctx", None),
        P("fsdp", "ctx", None),
        P(None, "ctx"),
        P("fsdp", "ctx"),
        P("fsdp", "ctx"),
        P("fsdp", "ctx"),
        P("fsdp", "ctx"),
        P("fsdp", "ctx"),
        P("fsdp", "ctx"),
    )
    return jax.shard_map(body, mesh=mesh, in_specs=in_specs, out_specs=out_specs, check_vma=False)
```

```python
import jax
import jax.numpy as jnp
from jax import lax
from jax.experimental import pallas as pl
from jax.experimental.pallas import tpu as pltpu
from jax.sharding import PartitionSpec as P

HEADS = 10
HEAD = 256
WINDOW = 2048


EPSILON = 1e-06
MASKED = -1e30
LOWEST = -1e29
VMEM = 56 * 1024 * 1024
FREE = pl.CostEstimate(flops=0, bytes_accessed=0, transcendentals=0)


def shifted(value, axis, steps):
    count = lax.axis_size(axis)
    initial, last = (max(0, -steps), min(count, count - steps))
    return lax.ppermute(value, axis, [(source, source + steps) for source in range(initial, last)])


def swap(value, axis, bit):
    return lax.ppermute(value, axis, [(i, i ^ bit) for i in range(lax.axis_size(axis))])


def add16(left, right):
    return (left.astype(jnp.float32) + right.astype(jnp.float32)).astype(jnp.bfloat16)


def times_rows(left, right):
    return lax.dot_general(
        left, right, (((1,), (1,)), ((), ())), preferred_element_type=jnp.float32
    )


def gram_rows(left, right):
    return lax.dot_general(
        left, right, (((0,), (0,)), ((), ())), preferred_element_type=jnp.float32
    )


def product(left, right):
    return jnp.dot(left, right, preferred_element_type=jnp.float32)


def doc_info(doc_lengths, first_token, token_count):
    doc_ends = jnp.cumsum(doc_lengths)
    doc_starts = doc_ends - doc_lengths
    token_ids = first_token + jnp.arange(token_count, dtype=jnp.int32)
    segment = jnp.sum((doc_ends[None, :] <= token_ids[:, None]).astype(jnp.int32), 1)
    begins = jnp.max(
        jnp.where(doc_starts[None, :] <= token_ids[:, None], doc_starts[None, :], 0), 1
    )
    return (token_ids, segment, token_ids - begins)


def rope_angles(positions):
    half_width = HEAD // 2
    column = jnp.arange(half_width, dtype=jnp.float32)
    inverse = jnp.power(10000.0, -column / half_width)
    angles = positions.astype(jnp.float32)[:, None] * inverse[None, :]
    return (jnp.cos(angles), jnp.sin(angles))


def rotate(values, cosine, sine):
    half_width = values.shape[-1] // 2
    first_half = values[..., :half_width]
    second_half = values[..., half_width:]
    return jnp.concatenate(
        [first_half * cosine - second_half * sine, second_half * cosine + first_half * sine], -1
    )


def rotate_back(grad_in, cosine, sine):
    half_width = grad_in.shape[-1] // 2
    first_half = grad_in[..., :half_width]
    second_half = grad_in[..., half_width:]
    return jnp.concatenate(
        [first_half * cosine + second_half * sine, second_half * cosine - first_half * sine], -1
    )


def norm_scale(values):
    return lax.rsqrt(jnp.mean(values * values, -1, keepdims=True) + EPSILON)


def norm_back(grad_in, values, scale, gain):
    weighted = grad_in * gain
    return scale * weighted - values * scale * scale * scale * jnp.mean(
        weighted * values, -1, keepdims=True
    )


def head_rows(block, count):
    return jnp.concatenate([block[:, h * HEAD : (h + 1) * HEAD] for h in range(count)], 0)


def row_bounds(low_ref, first_key, tokens, count):
    high = first_key + lax.broadcasted_iota(jnp.int32, (1, tokens), 1)
    low = low_ref[0]
    return jnp.concatenate([low] * count, 1), jnp.concatenate([high] * count, 1)


def seen(start, shape, low, high):
    key = start + lax.broadcasted_iota(jnp.int32, shape, 0)
    return (key >= low) & (key <= high)


def turn(from_ref, to_ref, chunk):
    def step(j, carry):
        here = pl.ds(pl.multiple_of(j * chunk, chunk), chunk)
        to_ref[:, here] = from_ref[here, :].astype(jnp.float32).T.astype(jnp.bfloat16)
        return carry

    lax.fori_loop(0, from_ref.shape[0] // chunk, step, 0)


def attend_kernel(
    span_ref, pre_ref, cos_ref, sin_ref, low_ref, key_ref, value_ref, *refs, base, chunk
):
    out_ref, out_t_ref, rot_ref, log_ref, acc, value_t_ref = refs[-6:]

    @pl.when((pl.program_id(0) == 0) & (pl.program_id(1) == 0))
    def _():
        turn(value_ref, value_t_ref, chunk)

    tile = pl.program_id(0)
    tokens = pre_ref.shape[0]
    count = pre_ref.shape[1] // HEAD
    cosine, sine = cos_ref[...], sin_ref[...]
    half = HEAD // 2
    for h in range(count):
        first = pre_ref[:, h * HEAD : h * HEAD + half]
        second = pre_ref[:, h * HEAD + half : (h + 1) * HEAD]
        rot_ref[:, h * HEAD : h * HEAD + half] = (
            (first * cosine - second * sine) * HEAD ** (-0.5)
        ).astype(jnp.bfloat16)
        rot_ref[:, h * HEAD + half : (h + 1) * HEAD] = (
            (second * cosine + first * sine) * HEAD ** (-0.5)
        ).astype(jnp.bfloat16)
    query = head_rows(rot_ref[...], count)
    low, high = row_bounds(low_ref, base + tile * tokens, tokens, count)
    rows = count * tokens

    acc[...] = jnp.zeros_like(acc)

    def step(j, carry):
        top, total = carry
        start = pl.multiple_of(j * chunk, chunk)
        scores = lax.dot_general(
            key_ref[pl.ds(start, chunk), :], query, (((1,), (1,)), ((), ())),
            preferred_element_type=jnp.float32,
        )
        scores = jnp.where(seen(start, scores.shape, low, high), scores, MASKED)
        higher = jnp.maximum(top, jnp.max(scores, 0, keepdims=True))
        part = jnp.exp(scores - higher)
        shrink = jnp.exp(top - higher)
        acc[...] = acc[...] * shrink + lax.dot_general(
            value_t_ref[:, pl.ds(start, chunk)], part.astype(jnp.bfloat16), (((1,), (0,)), ((), ())),
            preferred_element_type=jnp.float32,
        )
        return higher, total * shrink + jnp.sum(part, 0, keepdims=True)

    top, total = lax.fori_loop(
        span_ref[0, tile], span_ref[1, tile], step,
        (jnp.full((1, rows), LOWEST, jnp.float32), jnp.zeros((1, rows), jnp.float32)),
    )
    log_ref[0, 0] = top + jnp.log(total)
    outs_t = acc[...] * (1.0 / total)
    outs = outs_t.T.astype(jnp.bfloat16)
    outs_t = outs_t.astype(jnp.bfloat16)
    for h in range(count):
        out_t_ref[h * HEAD : (h + 1) * HEAD, :] = outs_t[:, h * tokens : (h + 1) * tokens]
        out_ref[:, h * HEAD : (h + 1) * HEAD] = outs[h * tokens : (h + 1) * tokens]


def attend_back_kernel(
    span_ref, rot_ref, grad_ref, out_ref, log_ref, cos_ref, sin_ref, low_ref, key_ref, value_ref,
    *refs, base, chunk
):
    pre_ref, pre_t_ref, grad_kv_ref, grad_key_ref, grad_value_ref, acc, key_t_ref = refs[-7:]
    tile = pl.program_id(0)
    tokens = rot_ref.shape[0]
    count = rot_ref.shape[1] // HEAD

    @pl.when((tile == 0) & (pl.program_id(1) == 0))
    def _():
        turn(key_ref, key_t_ref, chunk)
        grad_key_ref[...] = jnp.zeros_like(grad_key_ref)
        grad_value_ref[...] = jnp.zeros_like(grad_value_ref)

    query = head_rows(rot_ref[...], count)
    grad = head_rows(grad_ref[...], count)
    outs = head_rows(out_ref[...], count)
    delta = jnp.sum((grad.astype(jnp.float32) * outs.astype(jnp.float32)).T, 0, keepdims=True)
    log_total = log_ref[0, 0]
    low, high = row_bounds(low_ref, base + tile * tokens, tokens, count)
    acc[...] = jnp.zeros_like(acc)

    def step(j, carry):
        start = pl.multiple_of(j * chunk, chunk)
        here = pl.ds(start, chunk)
        scores = lax.dot_general(
            key_ref[here, :], query, (((1,), (1,)), ((), ())), preferred_element_type=jnp.float32
        )
        grad_probs = lax.dot_general(
            value_ref[here, :], grad, (((1,), (1,)), ((), ())), preferred_element_type=jnp.float32
        )
        probs = jnp.where(seen(start, scores.shape, low, high), jnp.exp(scores - log_total), 0.0)
        grad_scores = (probs * (grad_probs - delta)).astype(jnp.bfloat16)
        grad_value_ref[here, :] += jnp.dot(
            probs.astype(jnp.bfloat16), grad, preferred_element_type=jnp.float32
        )
        grad_key_ref[here, :] += jnp.dot(grad_scores, query, preferred_element_type=jnp.float32)
        acc[...] += lax.dot_general(
            key_t_ref[:, here], grad_scores, (((1,), (0,)), ((), ())),
            preferred_element_type=jnp.float32,
        )
        return carry

    lax.fori_loop(span_ref[0, tile], span_ref[1, tile], step, 0)
    cosine, sine = cos_ref[...], sin_ref[...]
    half = HEAD // 2
    for h in range(count):
        own = acc[:, h * tokens : (h + 1) * tokens] * HEAD ** (-0.5)
        first, second = own[:half], own[half:]
        own = jnp.concatenate(
            [first * cosine + second * sine, second * cosine - first * sine], 0
        )
        pre_t_ref[h * HEAD : (h + 1) * HEAD, :] = own.astype(jnp.bfloat16)
        pre_ref[:, h * HEAD : (h + 1) * HEAD] = own.T.astype(jnp.bfloat16)

    @pl.when((tile == pl.num_programs(0) - 1) & (pl.program_id(1) == pl.num_programs(1) - 1))
    def _():
        grad_kv_ref[:, :HEAD] = grad_key_ref[...].astype(jnp.bfloat16)
        grad_kv_ref[:, HEAD:] = grad_value_ref[...].astype(jnp.bfloat16)


def attention_plan(tok_rows, key_count, low):
    tile = min(128, tok_rows)
    chunk = 256 if key_count % 256 == 0 else 128
    base = key_count - tok_rows
    tiles = tok_rows // tile
    begin = low[::tile] // chunk
    end = (base + (jnp.arange(tiles, dtype=jnp.int32) + 1) * tile + chunk - 1) // chunk
    return tile, chunk, base, jnp.stack([begin, end], 0).astype(jnp.int32)


GROUP = 10


def attend(query_pre, cosine, sine, low, window, deps=()):
    tok_rows = query_pre.shape[0]
    key_count = window.shape[0] - tok_rows
    tile, chunk, base, span = attention_plan(tok_rows, key_count, low)
    tiles = tok_rows // tile
    groups = HEADS // GROUP
    wide = GROUP * HEAD
    block = pl.BlockSpec((tile, wide), lambda i, g, s: (i, g))
    angle = pl.BlockSpec((tile, HEAD // 2), lambda i, g, s: (i, 0))
    return pl.pallas_call(
        lambda *refs: attend_kernel(*refs, base=base, chunk=chunk),
        grid_spec=pltpu.PrefetchScalarGridSpec(
            num_scalar_prefetch=1,
            grid=(tiles, groups),
            in_specs=[
                block,
                angle,
                angle,
                pl.BlockSpec((1, 1, tile), lambda i, g, s: (i, 0, 0)),
                pl.BlockSpec((key_count, HEAD), lambda i, g, s: (0, 0)),
                pl.BlockSpec((key_count, HEAD), lambda i, g, s: (0, 1)),
            ]
            + [pl.BlockSpec(memory_space=pl.ANY)] * len(deps),
            out_specs=[
                block,
                pl.BlockSpec((wide, tile), lambda i, g, s: (g, i)),
                block,
                pl.BlockSpec((1, 1, 1, GROUP * tile), lambda i, g, s: (i, g, 0, 0)),
            ],
            scratch_shapes=[
                pltpu.VMEM((HEAD, GROUP * tile), jnp.float32),
                pltpu.VMEM((HEAD, key_count), jnp.bfloat16),
            ],
        ),
        out_shape=[
            jax.ShapeDtypeStruct(query_pre.shape, jnp.bfloat16),
            jax.ShapeDtypeStruct(query_pre.shape[::-1], jnp.bfloat16),
            jax.ShapeDtypeStruct(query_pre.shape, jnp.bfloat16),
            jax.ShapeDtypeStruct((tiles, groups, 1, GROUP * tile), jnp.float32),
        ],
        compiler_params=pltpu.CompilerParams(vmem_limit_bytes=VMEM),
        cost_estimate=FREE,
        name="attend",
    )(span, query_pre, cosine, sine, low.reshape(tiles, 1, tile), window, window, *deps)


def attend_back(query_rot, grad_rows, attn_rows, log_total, cosine_t, sine_t, low, window, deps):
    tok_rows = query_rot.shape[0]
    key_count = window.shape[0] - tok_rows
    tile, chunk, base, span = attention_plan(tok_rows, key_count, low)
    tiles = tok_rows // tile
    groups = HEADS // GROUP
    wide = GROUP * HEAD
    block = pl.BlockSpec((tile, wide), lambda i, g, s: (i, g))
    angle = pl.BlockSpec((HEAD // 2, tile), lambda i, g, s: (0, i))
    return pl.pallas_call(
        lambda *refs: attend_back_kernel(*refs, base=base, chunk=chunk),
        grid_spec=pltpu.PrefetchScalarGridSpec(
            num_scalar_prefetch=1,
            grid=(tiles, groups),
            in_specs=[
                block,
                block,
                block,
                pl.BlockSpec((1, 1, 1, GROUP * tile), lambda i, g, s: (i, g, 0, 0)),
                angle,
                angle,
                pl.BlockSpec((1, 1, tile), lambda i, g, s: (i, 0, 0)),
                pl.BlockSpec((key_count, HEAD), lambda i, g, s: (0, 0)),
                pl.BlockSpec((key_count, HEAD), lambda i, g, s: (0, 1)),
            ]
            + [pl.BlockSpec(memory_space=pl.ANY)] * len(deps),
            out_specs=[
                block,
                pl.BlockSpec((wide, tile), lambda i, g, s: (g, i)),
                pl.BlockSpec((key_count, 2 * HEAD), lambda i, g, s: (0, 0)),
            ],
            scratch_shapes=[
                pltpu.VMEM((key_count, HEAD), jnp.float32),
                pltpu.VMEM((key_count, HEAD), jnp.float32),
                pltpu.VMEM((HEAD, GROUP * tile), jnp.float32),
                pltpu.VMEM((HEAD, key_count), jnp.bfloat16),
            ],
        ),
        out_shape=[
            jax.ShapeDtypeStruct(query_rot.shape, jnp.bfloat16),
            jax.ShapeDtypeStruct(query_rot.shape[::-1], jnp.bfloat16),
            jax.ShapeDtypeStruct((key_count, 2 * HEAD), jnp.bfloat16),
        ],
        compiler_params=pltpu.CompilerParams(vmem_limit_bytes=VMEM),
        cost_estimate=FREE,
        name="attend_back",
    )(
        span, query_rot, grad_rows, attn_rows, log_total, cosine_t, sine_t, low.reshape(tiles, 1, tile),
        window, window, *deps,
    )


def nt(left, right):
    return lax.dot_general(
        left, right, (((1,), (1,)), ((), ())), preferred_element_type=jnp.float32
    )


def tn(left, right):
    return lax.dot_general(
        left, right, (((0,), (0,)), ((), ())), preferred_element_type=jnp.float32
    )


def flat(ref):
    block = ref[...]
    return block.reshape(-1, block.shape[-1])


def units_kernel(core_ref, *refs):
    tokens, cots = refs[0:2], refs[2:4]
    gate_ref, up_ref, down_ref = refs[4:7]
    out_ref = refs[-1]
    gate_rows, up_rows, down_rows = flat(gate_ref), flat(up_ref), flat(down_ref)

    def one(token_ref, cot_ref):
        gate = nt(gate_rows, token_ref[...])
        up = nt(up_rows, token_ref[...])
        grad_mixed = nt(down_rows, cot_ref[...])
        root = (2.0 / jnp.pi) ** 0.5
        square = gate * gate
        curve = jnp.tanh(root * (gate + 0.044715 * (square * gate)))
        upper = 0.5 * (1.0 + curve)
        activated = gate * upper
        slope = upper + 0.5 * gate * (1.0 - curve * curve) * (root * (1.0 + 0.134145 * square))
        out_ref[0] = (grad_mixed * up * slope).astype(jnp.bfloat16)
        out_ref[1] = (grad_mixed * activated).astype(jnp.bfloat16)
        out_ref[2] = (activated * up).astype(jnp.bfloat16)

    for j in (0, 1):
        pl.when(pl.program_id(1) == j)(lambda j=j: one(tokens[j], cots[j]))


def units(tokens, cots, weights, core, group, held, deps=()):
    cols, width = tokens[0].shape
    hidden = weights.hidden
    token_block = pl.BlockSpec((cols, width), lambda i, j, s: (0, 0))
    extra = (() if held is None else (held,)) + tuple(deps)
    return pl.pallas_call(
        units_kernel,
        grid_spec=pltpu.PrefetchScalarGridSpec(
            num_scalar_prefetch=1,
            grid=(2, 2),
            in_specs=[token_block] * 4
            + weights.specs(2, lambda i, j, s: (i, 0), width)
            + [pl.BlockSpec(memory_space=pl.ANY)] * len(extra),
            out_specs=pl.BlockSpec(
                (3, hidden // 2, cols), lambda i, j, s: (0, i, 2 * group + j)
            ),
        ),
        out_shape=jax.ShapeDtypeStruct((3, hidden, 4 * cols), jnp.bfloat16),
        input_output_aliases={} if held is None else {8: 0},
        compiler_params=pltpu.CompilerParams(vmem_limit_bytes=VMEM),
        cost_estimate=FREE,
        name="units",
    )(core, *tokens, *cots, *weights.arrays, *extra)


class OwnWeights:
    def __init__(self, shards):
        self.arrays = tuple(shards)
        self.hidden = shards[0].shape[0] // 2

    def specs(self, cuts, place, width):
        def index(*grid):
            row, col = place(*grid)
            return (grid[-1][0] * cuts + row, col)

        return [pl.BlockSpec((self.hidden // cuts, width), index)] * len(self.arrays)


class FarWeights:
    def __init__(self, gathered):
        parts, count, rows, width = gathered.shape
        self.hidden = parts * rows
        if rows % 16:
            gathered = gathered.reshape(2, parts // 2, count, rows, width)
            gathered = gathered.transpose(0, 2, 1, 3, 4).reshape(2, count, -1, width)
        self.arrays = (gathered,) * count

    def specs(self, cuts, place, width):
        parts, count, rows, _ = self.arrays[0].shape

        def spec(which):
            def index(*grid):
                row, col = place(*grid)
                return (row, which, 0, col)

            return pl.BlockSpec((parts // cuts, 1, rows, width), index)

        return [spec(which) for which in range(count)]


def sums_kernel(core_ref, *refs, count):
    total = 0.0
    for act_ref, weight_ref in zip(refs[:count], refs[count : 2 * count], strict=True):
        total = total + tn(act_ref[0], flat(weight_ref))
    refs[-1][...] = total.astype(jnp.bfloat16)


def sums(acts, weights, core, group, which, block=None, deps=()):
    all_tokens = acts[0].shape[2]
    width = weights[0].arrays[0].shape[-1]
    rows = all_tokens // 4
    blocks = 2 if block is None else 1
    cols = 512 if width % 512 == 0 else width // 2
    first = 2 * group + (block or 0)

    def act_spec(act, kind):
        return pl.BlockSpec((1, act.shape[1], rows), lambda n, t, s: (kind, 0, first + t))

    act_specs, weight_specs, act_args, weight_args = [], [], [], []
    for act, weight in zip(acts, weights, strict=True):
        specs = weight.specs(1, lambda n, t, s: (0, n), cols)
        for kind in which:
            act_specs.append(act_spec(act, kind))
            act_args.append(act)
            weight_specs.append(specs[kind])
            weight_args.append(weight.arrays[kind])
    return pl.pallas_call(
        lambda *refs: sums_kernel(*refs, count=len(act_args)),
        grid_spec=pltpu.PrefetchScalarGridSpec(
            num_scalar_prefetch=1,
            grid=(width // cols, blocks),
            in_specs=act_specs + weight_specs + [pl.BlockSpec(memory_space=pl.ANY)] * len(deps),
            out_specs=pl.BlockSpec((rows, cols), lambda n, t, s: (t, n)),
        ),
        out_shape=jax.ShapeDtypeStruct((blocks * rows, width), jnp.bfloat16),
        compiler_params=pltpu.CompilerParams(vmem_limit_bytes=VMEM),
        cost_estimate=FREE,
        name="sums",
    )(core, *act_args, *weight_args, *deps)


def grams_kernel(acts_ref, *refs, sets):
    out_ref = refs[-1]

    def one(rights):
        step = rights[0].shape[0]
        total = 0.0
        for i, right_ref in enumerate(rights):
            total = total + jnp.dot(
                acts_ref[0, :, i * step : (i + 1) * step], right_ref[...],
                preferred_element_type=jnp.float32,
            )
        out_ref[0] = total.astype(jnp.bfloat16)

    if sets == 1:
        one(refs[0:4])
    else:
        pl.when(pl.program_id(0) < 2)(lambda: one(refs[0:4]))
        pl.when(pl.program_id(0) == 2)(lambda: one(refs[4:8]))


def grams(acts, tokens, cots, pairs, kinds, deps=()):
    _, hidden, all_tokens = acts.shape
    step, width = tokens[0].shape
    cols = width // pairs
    first, count = kinds[0], len(kinds)
    if cols % 128:
        parts = []
        for kind in kinds:
            whole = sum(
                product(acts[kind, :, i * step : (i + 1) * step], right)
                for i, right in enumerate(cots if kind == 2 else tokens)
            )
            parts.append(whole.astype(jnp.bfloat16))
        return jnp.concatenate(parts, 0).reshape(count * hidden, pairs, cols).transpose(1, 0, 2)
    if count == 3:
        specs = [pl.BlockSpec((step, cols), lambda k, p: (0, jnp.where(k < 2, p, pairs - 1)))] * 4
        specs = specs + [pl.BlockSpec((step, cols), lambda k, p: (0, jnp.where(k < 2, 0, p)))] * 4
        rights = tuple(tokens) + tuple(cots)
    else:
        specs = [pl.BlockSpec((step, cols), lambda k, p: (0, p))] * 4
        rights = tuple(cots) if first == 2 else tuple(tokens)
    return pl.pallas_call(
        lambda *refs: grams_kernel(*refs, sets=len(rights) // 4),
        grid=(count, pairs),
        in_specs=[pl.BlockSpec((1, hidden, all_tokens), lambda k, p: (first + k, 0, 0))]
        + specs
        + [pl.BlockSpec(memory_space=pl.ANY)] * len(deps),
        out_specs=pl.BlockSpec((1, hidden, cols), lambda k, p: (p, k, 0)),
        out_shape=jax.ShapeDtypeStruct((pairs, count * hidden, cols), jnp.bfloat16),
        compiler_params=pltpu.CompilerParams(vmem_limit_bytes=VMEM),
        cost_estimate=FREE,
        name="grams",
    )(acts, *rights, *deps)


class Gathered:
    def __init__(self, own, others, shard):
        count, _, rows, width = others.shape
        if rows % 16:
            others = others.transpose(1, 0, 2, 3).reshape(1, -1, count * rows, width)
        self.own, self.others = own, others
        self.shard = shard.reshape(1).astype(jnp.int32)
        self.shards = others.shape[1] + 1

    def place(self, step, shard_ref):
        return lax.rem(shard_ref[0] + self.shards - step, self.shards)

    def specs(self):
        count, _, rows, width = self.others.shape
        return [
            pl.BlockSpec(self.own.shape, lambda r, s: (0, 0)),
            pl.BlockSpec((count, 1, rows, width), lambda r, s: (0, jnp.maximum(r - 1, 0), 0, 0)),
        ]


def by_shard(own_ref, others_ref, use):
    pl.when(pl.program_id(0) == 0)(lambda: use(own_ref[...]))
    pl.when(pl.program_id(0) > 0)(lambda: use(flat(others_ref)))


def spread_kernel(shard_ref, left_ref, own_ref, others_ref, *refs):
    out_ref = refs[-1]

    def use(weight):
        out_ref[...] = nt(left_ref[...], weight).astype(out_ref.dtype)

    by_shard(own_ref, others_ref, use)


def spread(left, weight, dtype, deps=()):
    tokens, width = left.shape
    rows = weight.own.shape[0]
    return pl.pallas_call(
        spread_kernel,
        grid_spec=pltpu.PrefetchScalarGridSpec(
            num_scalar_prefetch=1,
            grid=(weight.shards,),
            in_specs=[pl.BlockSpec((tokens, width), lambda r, s: (0, 0))]
            + weight.specs()
            + [pl.BlockSpec(memory_space=pl.ANY)] * len(deps),
            out_specs=pl.BlockSpec((tokens, rows), lambda r, s: (0, weight.place(r, s))),
        ),
        out_shape=jax.ShapeDtypeStruct((tokens, weight.shards * rows), dtype),
        compiler_params=pltpu.CompilerParams(vmem_limit_bytes=VMEM),
        cost_estimate=FREE,
        name="spread",
    )(weight.shard, left, weight.own, weight.others, *deps)


def collect_kernel(shard_ref, left_ref, own_ref, others_ref, start_ref, gain_ref, *refs, outs):
    refs = refs[-outs:]
    total_ref = refs[0]

    @pl.when(pl.program_id(0) == 0)
    def _():
        total_ref[...] = start_ref[...].astype(jnp.float32)

    def use(weight):
        total_ref[...] += jnp.dot(left_ref[...], weight, preferred_element_type=jnp.float32)

    by_shard(own_ref, others_ref, use)
    if outs > 1:

        @pl.when(pl.program_id(0) == pl.num_programs(0) - 1)
        def _():
            rows = min(128, total_ref.shape[0])

            def norm(i, carry):
                here = pl.ds(pl.multiple_of(i * rows, rows), rows)
                total = total_ref[here, :]
                scale = norm_scale(total)
                refs[1][here, :] = (total * scale * gain_ref[...]).astype(jnp.bfloat16)
                refs[2][here, :] = jnp.broadcast_to(scale, (rows, 128))
                return carry

            lax.fori_loop(0, total_ref.shape[0] // rows, norm, 0)


def collect(left, weight, start, gain=None, deps=()):
    tokens = left.shape[0]
    rows, width = weight.own.shape
    whole = pl.BlockSpec((tokens, width), lambda r, s: (0, 0))
    shapes, specs = [jax.ShapeDtypeStruct((tokens, width), jnp.float32)], [whole]
    if gain is not None:
        shapes.append(jax.ShapeDtypeStruct((tokens, width), jnp.bfloat16))
        shapes.append(jax.ShapeDtypeStruct((tokens, 128), jnp.float32))
        specs.extend([whole, pl.BlockSpec((tokens, 128), lambda r, s: (0, 0))])
    gain_row = jnp.zeros((1, width), jnp.float32) if gain is None else gain.reshape(1, width)
    return pl.pallas_call(
        lambda *refs: collect_kernel(*refs, outs=len(specs)),
        grid_spec=pltpu.PrefetchScalarGridSpec(
            num_scalar_prefetch=1,
            grid=(weight.shards,),
            in_specs=[pl.BlockSpec((tokens, rows), lambda r, s: (0, weight.place(r, s)))]
            + weight.specs()
            + [whole, pl.BlockSpec((1, width), lambda r, s: (0, 0))]
            + [pl.BlockSpec(memory_space=pl.ANY)] * len(deps),
            out_specs=specs,
        ),
        out_shape=shapes,
        compiler_params=pltpu.CompilerParams(vmem_limit_bytes=VMEM),
        cost_estimate=FREE,
        name="collect",
    )(weight.shard, left, weight.own, weight.others, start, gain_row, *deps)


def cross_kernel(core_ref, *refs, lefts, gained, added):
    right_ref, out_ref = refs[lefts], refs[-1]
    first = 0

    def put(part, rows):
        here = (0, slice(None), slice(first, first + rows))
        if added:
            part = part + refs[lefts + 1 + gained][here].astype(jnp.float32)
        out_ref[here] = part.astype(jnp.bfloat16)

    for left_ref in refs[:lefts]:
        shards, _, rows, tokens = left_ref.shape
        left = left_ref[...].reshape(shards * rows, tokens)
        part = jnp.dot(left, right_ref[...], preferred_element_type=jnp.float32)
        put(part.reshape(shards, rows, -1), rows)
        first = first + rows
    if gained:
        gains = refs[lefts + 1][...].astype(jnp.float32)
        put(jnp.broadcast_to(gains[None], (out_ref.shape[1],) + gains.shape), gains.shape[0])


def cross(lefts, right, core, shards, pairs, gains=None, add=None, deps=(), first=0, of=None, into=None):
    tokens, width = right.shape
    cols = width // pairs
    views = [left.reshape(shards, 2, -1, tokens) for left in lefts]
    rows = [view.shape[2] for view in views]
    total = sum(rows) + (0 if gains is None else gains.shape[0])
    if cols % 128:
        picked = jnp.concatenate(
            [lax.dynamic_index_in_dim(view, core[0], 1, keepdims=False) for view in views], 1
        )
        whole = product(picked.reshape(-1, tokens), right).reshape(shards, sum(rows), width)
        if gains is not None:
            extra = jnp.broadcast_to(gains.astype(jnp.float32)[None], (shards,) + gains.shape)
            whole = jnp.concatenate([whole, extra], 1)
        whole = whole.reshape(shards, total, pairs, cols).transpose(2, 0, 1, 3)
        if add is not None:
            whole = whole + add[:, :, first : first + total].astype(jnp.float32)
        whole = whole.astype(jnp.bfloat16)
        if of is None:
            return whole
        if into is None:
            into = jnp.zeros((pairs, shards, of, cols), jnp.bfloat16)
        return lax.dynamic_update_slice(into, whole, (0, 0, first, 0))
    block = pl.BlockSpec((1, shards, total, cols), lambda p, s: (p, 0, first // total, 0))
    kept = () if into is None else (into,)
    specs = [
        pl.BlockSpec((shards, 1, count, tokens), lambda p, s: (0, s[0], 0, 0)) for count in rows
    ]
    specs.append(pl.BlockSpec((tokens, cols), lambda p, s: (0, p)))
    args = [*views, right]
    if gains is not None:
        specs.append(pl.BlockSpec((gains.shape[0], cols), lambda p, s: (0, p)))
        args.append(gains)
    if add is not None:
        specs.append(block)
        args.append(add)
    return pl.pallas_call(
        lambda *refs: cross_kernel(
            *refs, lefts=len(views), gained=gains is not None, added=add is not None
        ),
        grid_spec=pltpu.PrefetchScalarGridSpec(
            num_scalar_prefetch=1,
            grid=(pairs,),
            in_specs=specs + [pl.BlockSpec(memory_space=pl.ANY)] * (len(kept) + len(deps)),
            out_specs=block,
        ),
        out_shape=jax.ShapeDtypeStruct((pairs, shards, of or total, cols), jnp.bfloat16),
        input_output_aliases={1 + len(args): 0} if kept else {},
        compiler_params=pltpu.CompilerParams(vmem_limit_bytes=VMEM),
        cost_estimate=FREE,
        name="cross",
    )(core, *args, *kept, *deps)


def swap(value, axis, bit):
    return lax.ppermute(value, axis, [(i, i ^ bit) for i in range(lax.axis_size(axis))])


def after(value, *others):
    return lax.optimization_barrier((value, *others))[0]


def same_core():
    count = lax.axis_size("ctx")
    return [list(range(0, count, 2)), list(range(1, count, 2))]


def own_part(shard, place):
    part = shard.shape[0] // lax.axis_size("ctx")
    return lax.dynamic_slice_in_dim(shard, place * part, part, 0)


def together(*values):
    return lax.optimization_barrier(values)


def halving_scatter(blocks, axis, place):
    held, bit = blocks, 1
    while held.shape[0] > 1:
        both = held.reshape((held.shape[0] // 2, 2) + held.shape[1:])
        mine = (place // bit) % 2
        keep = lax.dynamic_index_in_dim(both, mine, 1, keepdims=False)
        give = lax.dynamic_index_in_dim(both, 1 - mine, 1, keepdims=False)
        total = keep.astype(jnp.float32) + swap(give, axis, bit).astype(jnp.float32)
        held = total.astype(jnp.bfloat16)
        bit = 2 * bit
    return total[0]


def step_ring(value, axis):
    count = lax.axis_size(axis)
    return lax.ppermute(value, axis, [(i, (i + 1) % count) for i in range(count)])


def ring(value, axis):
    arrived = []
    for _ in range(lax.axis_size(axis) - 1):
        value = step_ring(value, axis)
        arrived.append(value)
    return arrived


def exchanges(axis):
    bits, bit = [], 2
    while bit < lax.axis_size(axis):
        bits.append(bit)
        bit = 2 * bit
    return bits + [1]


def pairs_gather(value):
    pairs = lax.axis_size("ctx") // 2
    if pairs == 4:
        half = value.shape[0] // 2
        x_all, y_all = swap(value, "ctx", 2), swap(value, "ctx", 4)
        low = swap(y_all[:half], "ctx", 2)
        high = swap(x_all[half:], "ctx", 4)
        return [(0, [value]), (2, [x_all]), (4, [y_all]), (6, [low, high])]
    held, bit = [(0, value)], 2
    while bit < 2 * pairs:
        held = held + [(bits ^ bit, swap(item, "ctx", bit)) for bits, item in held]
        bit = 2 * bit
    return [(bits, [item]) for bits, item in held]


def window_gather(value, reach, place):
    rows = value.shape[0]
    out = jnp.zeros(((reach + 2) * rows,) + value.shape[1:], value.dtype)
    parts = [(bits, part, i) for bits, held in pairs_gather(value) for i, part in enumerate(held)]
    for bits, part, i in parts:
        both = ((bits, part), (bits ^ 1, swap(part, "ctx", 1)))
        for other, block in both:
            spot = (place ^ other) - place + reach
            spot = jnp.where((spot < 0) | (spot > reach), reach + 1, spot)
            start = spot * rows + (i * block.shape[0])
            out = lax.dynamic_update_slice_in_dim(out, block, start, 0)
    return out


def place_block(out, block, place):
    return lax.dynamic_update_index_in_dim(out, block, place, 0)


def in_places(own, arrived, place):
    count = len(arrived) + 1
    out = jnp.zeros((count,) + own.shape, own.dtype)
    for step, value in enumerate([own, *arrived]):
        out = lax.dynamic_update_index_in_dim(out, value, lax.rem(place + count - step, count), 0)
    return out


def in_order(gathered, first, part):
    mine = gathered[:, :, first : first + part].transpose(1, 0, 2, 3)
    return mine.reshape(-1, gathered.shape[-1])


def body(
    inputs,
    norm_gains,
    q_weight,
    kv_weight,
    o_weight,
    gate_weight,
    up_weight,
    down_weight,
    cotangent,
    doc_lengths,
):
    x_rows = inputs[0].astype(jnp.float32)
    grad_out = cotangent[0]
    tok_rows, width = x_rows.shape
    place = lax.axis_index("ctx")
    ctx_count = lax.axis_size("ctx")
    pairs = ctx_count // 2
    core = place % 2
    pair = place // 2
    own_core = core.reshape(1).astype(jnp.int32)
    shard = lax.axis_index("fsdp")
    shards = lax.axis_size("fsdp")
    reach = min(ctx_count - 1, (WINDOW + tok_rows - 2) // tok_rows)
    key_count = (reach + 1) * tok_rows
    first_token = place * tok_rows
    token_ids, segment, positions = doc_info(doc_lengths[0], first_token, tok_rows)
    low = jnp.maximum(token_ids - positions, token_ids - (WINDOW - 1)) - (
        first_token - reach * tok_rows
    )
    cosine, sine = rope_angles(positions)
    gain_attn = norm_gains[0]
    gain_mlp = norm_gains[1]

    q_part, kv_part, o_part = (own_part(w, place) for w in (q_weight, kv_weight, o_weight))
    kv_z = in_places(kv_part, ring(kv_part, "fsdp"), shard)
    moving = after(q_part, kv_z)
    held, origins = kv_z[None], [place]
    q_arrived = []
    for bit in exchanges("ctx"):
        if len(q_arrived) < shards - 1:
            moving = step_ring(moving, "fsdp")
            q_arrived.append(moving)
        held = jnp.concatenate([held, swap(held, "ctx", bit)], 0)
        origins = origins + [origin ^ bit for origin in origins]
        held, moving = together(held, moving)
    while len(q_arrived) < shards - 1:
        moving = step_ring(moving, "fsdp")
        q_arrived.append(moving)
    kv_all = jnp.zeros_like(held)
    for step, origin in enumerate(origins):
        kv_all = place_block(kv_all, held[step], origin)
    q_ring = jnp.stack(q_arrived, 0)
    q_ring, kv_all = together(q_ring, kv_all)
    q_all = lax.all_gather(q_ring, "ctx", axis=0)

    half_rows = gate_weight.shape[0] // 2
    part_rows = half_rows // pairs
    cut = (part_rows * 7 // 15 + 15) // 16 * 16
    far_rows, last_rows = cut // 4, part_rows * 5 // 12 // 4 * 4
    mine = jnp.stack(
        [
            lax.dynamic_slice_in_dim(w, core * half_rows + pair * part_rows, part_rows, 0)
            for w in (gate_weight, up_weight, down_weight)
        ],
        0,
    )
    mine, _ = together(mine, q_ring)
    own_weights = OwnWeights((gate_weight, up_weight, down_weight))

    scale_one = norm_scale(x_rows)
    normed_one = (x_rows * scale_one * gain_attn).astype(jnp.bfloat16)
    kv_full = in_order(kv_all, 0, kv_part.shape[0])
    kv_pre = times_rows(normed_one, kv_full)
    key_rot = rotate(kv_pre[:, :HEAD], cosine, sine).astype(jnp.bfloat16)
    kv_local = jnp.concatenate([key_rot, kv_pre[:, HEAD:].astype(jnp.bfloat16)], 1)
    kv_local, moving = together(kv_local, o_part)
    kv_window = window_gather(kv_local, reach, place)
    far_zero = swap(after(mine[:, :far_rows], q_ring), "fsdp", 2)
    moving, far_zero = together(step_ring(moving, "fsdp"), far_zero)
    o_arrived = [moving]
    for _ in range(shards - 2):
        moving = step_ring(moving, "fsdp")
        o_arrived.append(moving)
    cot_rows = tok_rows // 8
    cot_first = swap(after(grad_out[:cot_rows], o_arrived[-1]), "fsdp", 1)
    far_first = swap(after(mine[:, far_rows : 2 * far_rows], o_arrived[-1]), "fsdp", 2)
    o_ring = jnp.stack(o_arrived, 0)
    q_all, o_ring, far_first, cot_first, kv_window, normed_one, cosine_t, sine_t = together(
        q_all, o_ring, far_first, cot_first, kv_window, normed_one, cosine.T, sine.T
    )
    o_all = lax.all_gather(o_ring, "ctx", axis=0)
    q_full = Gathered(q_weight, q_all, shard)
    o_full = Gathered(o_weight, o_all, shard)
    far_second = swap(after(mine[:, 2 * far_rows : part_rows - last_rows], o_ring), "fsdp", 2)
    cot_second = swap(after(grad_out[cot_rows:], o_ring), "fsdp", 1)
    query_pre = spread(normed_one, q_full, jnp.float32)
    attn_rows, attn_rows_t, query_rot, log_total = attend(
        query_pre, cosine, sine, low, kv_window
    )
    far_last = mine[:, part_rows - last_rows :]
    log_total, cot_second, far_second, far_last = together(
        log_total, cot_second, far_second, far_last
    )
    far_third = swap(far_last, "fsdp", 2)
    near_cots = (grad_out, swap(grad_out, "ctx", 1))
    cot_across = jnp.concatenate([cot_first, cot_second], 0)
    cots = [near_cots, (cot_across, swap(cot_across, "ctx", 1))]

    def over_plane(part):
        return lax.all_gather(part, "ctx", axis=0, axis_index_groups=same_core())

    far_a = FarWeights(
        over_plane(jnp.concatenate([far_zero, far_first, far_second[:, : cut - 2 * far_rows]], 1))
    )
    hidden_one, normed_two, scale_two = collect(attn_rows, o_full, inputs[0], gain_mlp)
    scale_two = scale_two[:, :1]

    near = (normed_two, swap(normed_two, "ctx", 1))
    across = swap(normed_two, "fsdp", 1)
    own_acts = units(near, near_cots, own_weights, own_core, 0, None)
    a_acts = units(near, near_cots, far_a, own_core, 0, None, (own_acts, cots[1][1]))
    across, a_acts, far_third = together(across, a_acts, far_third)
    far = (across, swap(across, "ctx", 1))
    far_b = FarWeights(
        over_plane(jnp.concatenate([far_second[:, cut - 2 * far_rows :], far_third], 1))
    )
    own_acts = units(far, cots[1], own_weights, own_core, 1, own_acts, (a_acts,))
    a_acts = units(far, cots[1], far_a, own_core, 1, a_acts, (own_acts,))
    near_far, cot_rows = near + far, cots[0] + cots[1]

    def over_pairs(blocks):
        mine = lax.psum_scatter(
            blocks, "ctx", scatter_dimension=0, tiled=False, axis_index_groups=same_core()
        )
        return lax.optimization_barrier(mine)

    a_grams = grams(a_acts, near_far, cot_rows, pairs, (0, 1, 2))
    b_acts = units(near, cots[0], far_b, own_core, 0, None, (a_grams,))
    b_acts = units(far, cots[1], far_b, own_core, 1, b_acts)
    b_grams = grams(b_acts, near_far, cot_rows, pairs, (0, 1, 2))
    a_sums, b_sums = over_pairs(a_grams), over_pairs(b_grams)
    acts, weights = (own_acts, a_acts, b_acts), (own_weights, far_a, far_b)

    def group_sums(group, which, block, deps):
        return sums(acts, weights, own_core, group, which, block, deps)

    own_gate_up = grams(own_acts, near_far, cot_rows, pairs, (0, 1), (b_grams,))
    give = group_sums(1, (0, 1), 1, (own_gate_up,))
    own_gate_up = over_pairs(own_gate_up)
    got = swap(give, "ctx", 1)
    near_give = group_sums(0, (0, 1), 1, (give,))
    near_got = swap(near_give, "ctx", 1)
    keep = group_sums(1, (0, 1), 0, (near_give, a_sums))
    total = add16(keep, got)
    moved = swap(total, "fsdp", 1)
    own_down = grams(own_acts, near_far, cot_rows, pairs, (2,), (total, near_got))
    near_keep = group_sums(0, (0, 1), 0, (own_down,))
    out_give = group_sums(1, (2,), 1, (near_keep,))
    out_got = swap(out_give, "ctx", 1)
    out_keep = group_sums(1, (2,), 0, (out_give,))
    moved, own_down, near_keep, out_keep, a_sums = together(
        moved, own_down, near_keep, out_keep, a_sums
    )
    own_down = over_pairs(own_down)
    grad_normed_two = (
        near_keep.astype(jnp.float32) + near_got.astype(jnp.float32) + moved.astype(jnp.float32)
    )
    grad_hidden = grad_out.astype(jnp.float32) + norm_back(
        grad_normed_two, hidden_one, scale_two, gain_mlp
    )
    gain_mlp_grad = jnp.sum(grad_normed_two * hidden_one * scale_two, 0)
    grad_branch = grad_hidden.astype(jnp.bfloat16)
    grad_attended = spread(grad_branch, o_full, jnp.bfloat16, (b_sums,))

    gate_rows = b_sums.shape[0] // 3
    a_all = swap(a_sums, "fsdp", 2)
    grad_query_pre, grad_query_pre_t, grad_kv = attend_back(
        query_rot, grad_attended, attn_rows, log_total, cosine_t, sine_t, low, kv_window,
        (out_keep,),
    )
    grad_stack = grad_kv.reshape(reach + 1, tok_rows, 2 * HEAD)
    moved_kv = [shifted(grad_stack[reach - hop], "ctx", -hop) for hop in range(1, reach + 1)]
    out_total = add16(out_keep, out_got)
    q_give = cross(
        [grad_query_pre_t], normed_one, 1 - own_core, shards, pairs,
        deps=(grad_kv, a_all, own_gate_up, out_total),
    )
    q_got = swap(q_give, "ctx", 1)
    q_half, kv_half = q_weight.shape[0] // 2, kv_weight.shape[0] // 2
    okv_rows = q_half + kv_half + 16
    okv_give = cross(
        [attn_rows_t], grad_branch, 1 - own_core, shards, pairs, deps=(q_give,), of=okv_rows
    )
    q_sums = cross(
        [grad_query_pre_t], normed_one, own_core, shards, pairs, None, q_got, (okv_give,)
    )
    moved_kv, q_sums, b_sums, out_total = together(moved_kv, q_sums, b_sums, out_total)
    out_rows = tok_rows // 4
    out_first = swap(out_total[:out_rows], "fsdp", 1)
    out_second = swap(after(out_total[out_rows : 2 * out_rows], out_first), "fsdp", 1)
    out_third = swap(after(out_total[2 * out_rows :], out_second), "fsdp", 1)
    b_gate = swap(b_sums[:gate_rows], "fsdp", 2)
    b_up = swap(after(b_sums[gate_rows : 2 * gate_rows], b_gate), "fsdp", 2)
    b_down = swap(after(b_sums[2 * gate_rows :], b_up), "fsdp", 2)
    q_pairs = over_pairs(q_sums)
    own_kv_grad = grad_stack[reach].astype(jnp.float32)
    for block in moved_kv:
        own_kv_grad = own_kv_grad + block.astype(jnp.float32)
    grad_kv_pre = jnp.concatenate(
        [rotate_back(own_kv_grad[:, :HEAD], cosine, sine), own_kv_grad[:, HEAD:]], 1
    ).astype(jnp.bfloat16)
    (grad_normed_one,) = collect(
        grad_query_pre, q_full, product(grad_kv_pre, kv_full)
    )
    gain_attn_grad = jnp.sum(grad_normed_one * x_rows * scale_one, 0)
    gains = jnp.stack([gain_attn_grad, gain_mlp_grad], 0).astype(jnp.bfloat16)
    gains = jnp.concatenate([gains, jnp.zeros((14, width), jnp.bfloat16)], 0)
    kv_left = [grad_kv_pre.T]
    okv_give = cross(
        kv_left, normed_one, 1 - own_core, shards, pairs, gains, None, (b_gate, out_first), q_half,
        okv_rows, okv_give,
    )
    okv_got = swap(okv_give, "ctx", 1)
    near_out = sums(acts, weights, own_core, 0, (2,), None, (okv_give,))
    near_out_got = swap(near_out[tok_rows:], "ctx", 1)
    okv_sums = cross(
        [attn_rows_t], grad_branch, own_core, shards, pairs, None, okv_got, (near_out, b_up, out_second),
        of=okv_rows,
    )
    okv_sums = cross(
        kv_left, normed_one, own_core, shards, pairs, gains, okv_got, (own_down, q_pairs), q_half, okv_rows,
        okv_sums,
    )
    grad_inputs = grad_hidden + norm_back(grad_normed_one, x_rows, scale_one, gain_attn)

    out_cols = width // ctx_count

    def both_halves(mine):
        keep = lax.dynamic_slice_in_dim(mine, core * out_cols, out_cols, 1)
        give = lax.dynamic_slice_in_dim(mine, (1 - core) * out_cols, out_cols, 1)
        got = swap(give.astype(jnp.bfloat16), "ctx", 1).astype(jnp.float32)
        lower = jnp.where(core == 0, keep, got)
        upper = jnp.where(core == 0, got, keep)
        return jnp.concatenate([lower, upper], 0)

    okv_pairs = over_pairs(okv_sums)
    out_moved = jnp.concatenate([out_first, out_second, out_third], 0)
    q_mine = halving_scatter(q_pairs, "fsdp", shard)
    b_down, q_mine = together(b_down, q_mine)
    result = hidden_one + (
        near_out[:tok_rows].astype(jnp.float32)
        + near_out_got.astype(jnp.float32)
        + out_moved.astype(jnp.float32)
    )
    q_grad = both_halves(q_mine)
    okv_mine = halving_scatter(okv_pairs, "fsdp", shard)
    o_grad = both_halves(okv_mine[:q_half])
    kv_grad = both_halves(okv_mine[q_half : q_half + kv_half])
    gain_total = lax.dynamic_slice_in_dim(
        okv_mine[q_half + kv_half : q_half + kv_half + 2], core * out_cols, out_cols, 1
    )

    a_all = a_all.reshape(3, pairs, cut, -1)
    b_all = jnp.concatenate([b_gate, b_up, b_down], 0).reshape(3, pairs, part_rows - cut, -1)
    own_all = (own_gate_up[:half_rows], own_gate_up[half_rows:], own_down)
    mlp_grads = []
    for kind in range(3):
        others = jnp.concatenate([a_all[kind], b_all[kind]], 1).reshape(half_rows, -1)
        mlp_grads.append(
            both_halves(own_all[kind].astype(jnp.float32) + others.astype(jnp.float32))
        )

    return (
        result.astype(jnp.bfloat16)[None],
        grad_inputs.astype(jnp.bfloat16)[None],
        gain_total,
        q_grad,
        kv_grad,
        o_grad,
        mlp_grads[0],
        mlp_grads[1],
        mlp_grads[2],
    )


def solution(mesh):
    in_specs = (
        P("fsdp", "ctx", None),
        P(),
        P("fsdp", None),
        P("fsdp", None),
        P("fsdp", None),
        P("fsdp", None),
        P("fsdp", None),
        P("fsdp", None),
        P("fsdp", "ctx", None),
        P("fsdp", None),
    )
    out_specs = (
        P("fsdp", "ctx", None),
        P("fsdp", "ctx", None),
        P(None, "ctx"),
        P("fsdp", "ctx"),
        P("fsdp", "ctx"),
        P("fsdp", "ctx"),
        P("fsdp", "ctx"),
        P("fsdp", "ctx"),
        P("fsdp", "ctx"),
    )
    return jax.shard_map(body, mesh=mesh, in_specs=in_specs, out_specs=out_specs, check_vma=False)
```

```python
import jax
import jax.numpy as jnp
from jax import lax
from jax.experimental import pallas as pl
from jax.experimental.pallas import tpu as pltpu
from jax.sharding import PartitionSpec as P

HEADS = 10
HEAD = 256
WINDOW = 2048


EPSILON = 1e-06
MASKED = -1e30
LOWEST = -1e29
VMEM = 56 * 1024 * 1024
FREE = pl.CostEstimate(flops=0, bytes_accessed=0, transcendentals=0)


def shifted(value, axis, steps):
    count = lax.axis_size(axis)
    initial, last = (max(0, -steps), min(count, count - steps))
    return lax.ppermute(value, axis, [(source, source + steps) for source in range(initial, last)])


def swap(value, axis, bit):
    return lax.ppermute(value, axis, [(i, i ^ bit) for i in range(lax.axis_size(axis))])


def add16(left, right):
    return (left.astype(jnp.float32) + right.astype(jnp.float32)).astype(jnp.bfloat16)


def times_rows(left, right):
    return lax.dot_general(
        left, right, (((1,), (1,)), ((), ())), preferred_element_type=jnp.float32
    )


def gram_rows(left, right):
    return lax.dot_general(
        left, right, (((0,), (0,)), ((), ())), preferred_element_type=jnp.float32
    )


def product(left, right):
    return jnp.dot(left, right, preferred_element_type=jnp.float32)


def doc_info(doc_lengths, first_token, token_count):
    doc_ends = jnp.cumsum(doc_lengths)
    doc_starts = doc_ends - doc_lengths
    token_ids = first_token + jnp.arange(token_count, dtype=jnp.int32)
    segment = jnp.sum((doc_ends[None, :] <= token_ids[:, None]).astype(jnp.int32), 1)
    begins = jnp.max(
        jnp.where(doc_starts[None, :] <= token_ids[:, None], doc_starts[None, :], 0), 1
    )
    return (token_ids, segment, token_ids - begins)


def rope_angles(positions):
    half_width = HEAD // 2
    column = jnp.arange(half_width, dtype=jnp.float32)
    inverse = jnp.power(10000.0, -column / half_width)
    angles = positions.astype(jnp.float32)[:, None] * inverse[None, :]
    return (jnp.cos(angles), jnp.sin(angles))


def rotate(values, cosine, sine):
    half_width = values.shape[-1] // 2
    first_half = values[..., :half_width]
    second_half = values[..., half_width:]
    return jnp.concatenate(
        [first_half * cosine - second_half * sine, second_half * cosine + first_half * sine], -1
    )


def rotate_back(grad_in, cosine, sine):
    half_width = grad_in.shape[-1] // 2
    first_half = grad_in[..., :half_width]
    second_half = grad_in[..., half_width:]
    return jnp.concatenate(
        [first_half * cosine + second_half * sine, second_half * cosine - first_half * sine], -1
    )


def norm_scale(values):
    return lax.rsqrt(jnp.mean(values * values, -1, keepdims=True) + EPSILON)


def norm_back(grad_in, values, scale, gain):
    weighted = grad_in * gain
    return scale * weighted - values * scale * scale * scale * jnp.mean(
        weighted * values, -1, keepdims=True
    )


def head_rows(block, count):
    return jnp.concatenate([block[:, h * HEAD : (h + 1) * HEAD] for h in range(count)], 0)


def row_bounds(low_ref, first_key, tokens, count):
    high = first_key + lax.broadcasted_iota(jnp.int32, (1, tokens), 1)
    low = low_ref[0]
    return jnp.concatenate([low] * count, 1), jnp.concatenate([high] * count, 1)


def seen(start, shape, low, high):
    key = start + lax.broadcasted_iota(jnp.int32, shape, 0)
    return (key >= low) & (key <= high)


def turn(from_ref, to_ref, chunk):
    def step(j, carry):
        here = pl.ds(pl.multiple_of(j * chunk, chunk), chunk)
        to_ref[:, here] = from_ref[here, :].astype(jnp.float32).T.astype(jnp.bfloat16)
        return carry

    lax.fori_loop(0, from_ref.shape[0] // chunk, step, 0)


def attend_kernel(
    span_ref, pre_ref, cos_ref, sin_ref, low_ref, key_ref, value_ref, *refs, base, chunk
):
    out_ref, out_t_ref, rot_ref, log_ref, acc, value_t_ref = refs[-6:]

    @pl.when((pl.program_id(0) == 0) & (pl.program_id(1) == 0))
    def _():
        turn(value_ref, value_t_ref, chunk)

    tile = pl.program_id(0)
    tokens = pre_ref.shape[0]
    count = pre_ref.shape[1] // HEAD
    cosine, sine = cos_ref[...], sin_ref[...]
    half = HEAD // 2
    for h in range(count):
        first = pre_ref[:, h * HEAD : h * HEAD + half]
        second = pre_ref[:, h * HEAD + half : (h + 1) * HEAD]
        rot_ref[:, h * HEAD : h * HEAD + half] = (
            (first * cosine - second * sine) * HEAD ** (-0.5)
        ).astype(jnp.bfloat16)
        rot_ref[:, h * HEAD + half : (h + 1) * HEAD] = (
            (second * cosine + first * sine) * HEAD ** (-0.5)
        ).astype(jnp.bfloat16)
    query = head_rows(rot_ref[...], count)
    low, high = row_bounds(low_ref, base + tile * tokens, tokens, count)
    rows = count * tokens

    acc[...] = jnp.zeros_like(acc)

    def step(j, carry):
        top, total = carry
        start = pl.multiple_of(j * chunk, chunk)
        scores = lax.dot_general(
            key_ref[pl.ds(start, chunk), :], query, (((1,), (1,)), ((), ())),
            preferred_element_type=jnp.float32,
        )
        scores = jnp.where(seen(start, scores.shape, low, high), scores, MASKED)
        higher = jnp.maximum(top, jnp.max(scores, 0, keepdims=True))
        part = jnp.exp(scores - higher)
        shrink = jnp.exp(top - higher)
        acc[...] = acc[...] * shrink + lax.dot_general(
            value_t_ref[:, pl.ds(start, chunk)], part.astype(jnp.bfloat16), (((1,), (0,)), ((), ())),
            preferred_element_type=jnp.float32,
        )
        return higher, total * shrink + jnp.sum(part, 0, keepdims=True)

    top, total = lax.fori_loop(
        span_ref[0, tile], span_ref[1, tile], step,
        (jnp.full((1, rows), LOWEST, jnp.float32), jnp.zeros((1, rows), jnp.float32)),
    )
    log_ref[0, 0] = top + jnp.log(total)
    outs_t = acc[...] * (1.0 / total)
    outs = outs_t.T.astype(jnp.bfloat16)
    outs_t = outs_t.astype(jnp.bfloat16)
    for h in range(count):
        out_t_ref[h * HEAD : (h + 1) * HEAD, :] = outs_t[:, h * tokens : (h + 1) * tokens]
        out_ref[:, h * HEAD : (h + 1) * HEAD] = outs[h * tokens : (h + 1) * tokens]


def attend_back_kernel(
    span_ref, rot_ref, grad_ref, out_ref, log_ref, cos_ref, sin_ref, low_ref, key_ref, value_ref,
    *refs, base, chunk
):
    pre_ref, pre_t_ref, grad_kv_ref, grad_key_ref, grad_value_ref, acc, key_t_ref = refs[-7:]
    tile = pl.program_id(0)
    tokens = rot_ref.shape[0]
    count = rot_ref.shape[1] // HEAD

    @pl.when((tile == 0) & (pl.program_id(1) == 0))
    def _():
        turn(key_ref, key_t_ref, chunk)
        grad_key_ref[...] = jnp.zeros_like(grad_key_ref)
        grad_value_ref[...] = jnp.zeros_like(grad_value_ref)

    query = head_rows(rot_ref[...], count)
    grad = head_rows(grad_ref[...], count)
    outs = head_rows(out_ref[...], count)
    delta = jnp.sum((grad.astype(jnp.float32) * outs.astype(jnp.float32)).T, 0, keepdims=True)
    log_total = log_ref[0, 0]
    low, high = row_bounds(low_ref, base + tile * tokens, tokens, count)
    acc[...] = jnp.zeros_like(acc)

    def step(j, carry):
        start = pl.multiple_of(j * chunk, chunk)
        here = pl.ds(start, chunk)
        scores = lax.dot_general(
            key_ref[here, :], query, (((1,), (1,)), ((), ())), preferred_element_type=jnp.float32
        )
        grad_probs = lax.dot_general(
            value_ref[here, :], grad, (((1,), (1,)), ((), ())), preferred_element_type=jnp.float32
        )
        probs = jnp.where(seen(start, scores.shape, low, high), jnp.exp(scores - log_total), 0.0)
        grad_scores = (probs * (grad_probs - delta)).astype(jnp.bfloat16)
        grad_value_ref[here, :] += jnp.dot(
            probs.astype(jnp.bfloat16), grad, preferred_element_type=jnp.float32
        )
        grad_key_ref[here, :] += jnp.dot(grad_scores, query, preferred_element_type=jnp.float32)
        acc[...] += lax.dot_general(
            key_t_ref[:, here], grad_scores, (((1,), (0,)), ((), ())),
            preferred_element_type=jnp.float32,
        )
        return carry

    lax.fori_loop(span_ref[0, tile], span_ref[1, tile], step, 0)
    cosine, sine = cos_ref[...], sin_ref[...]
    half = HEAD // 2
    for h in range(count):
        own = acc[:, h * tokens : (h + 1) * tokens] * HEAD ** (-0.5)
        first, second = own[:half], own[half:]
        own = jnp.concatenate(
            [first * cosine + second * sine, second * cosine - first * sine], 0
        )
        pre_t_ref[h * HEAD : (h + 1) * HEAD, :] = own.astype(jnp.bfloat16)
        pre_ref[:, h * HEAD : (h + 1) * HEAD] = own.T.astype(jnp.bfloat16)

    @pl.when((tile == pl.num_programs(0) - 1) & (pl.program_id(1) == pl.num_programs(1) - 1))
    def _():
        grad_kv_ref[:, :HEAD] = grad_key_ref[...].astype(jnp.bfloat16)
        grad_kv_ref[:, HEAD:] = grad_value_ref[...].astype(jnp.bfloat16)


def attention_plan(tok_rows, key_count, low):
    tile = min(128, tok_rows)
    chunk = 256 if key_count % 256 == 0 else 128
    base = key_count - tok_rows
    tiles = tok_rows // tile
    begin = low[::tile] // chunk
    end = (base + (jnp.arange(tiles, dtype=jnp.int32) + 1) * tile + chunk - 1) // chunk
    return tile, chunk, base, jnp.stack([begin, end], 0).astype(jnp.int32)


GROUP = 10


def attend(query_pre, cosine, sine, low, window, deps=()):
    tok_rows = query_pre.shape[0]
    key_count = window.shape[0] - tok_rows
    tile, chunk, base, span = attention_plan(tok_rows, key_count, low)
    tiles = tok_rows // tile
    groups = HEADS // GROUP
    wide = GROUP * HEAD
    block = pl.BlockSpec((tile, wide), lambda i, g, s: (i, g))
    angle = pl.BlockSpec((tile, HEAD // 2), lambda i, g, s: (i, 0))
    return pl.pallas_call(
        lambda *refs: attend_kernel(*refs, base=base, chunk=chunk),
        grid_spec=pltpu.PrefetchScalarGridSpec(
            num_scalar_prefetch=1,
            grid=(tiles, groups),
            in_specs=[
                block,
                angle,
                angle,
                pl.BlockSpec((1, 1, tile), lambda i, g, s: (i, 0, 0)),
                pl.BlockSpec((key_count, HEAD), lambda i, g, s: (0, 0)),
                pl.BlockSpec((key_count, HEAD), lambda i, g, s: (0, 1)),
            ]
            + [pl.BlockSpec(memory_space=pl.ANY)] * len(deps),
            out_specs=[
                block,
                pl.BlockSpec((wide, tile), lambda i, g, s: (g, i)),
                block,
                pl.BlockSpec((1, 1, 1, GROUP * tile), lambda i, g, s: (i, g, 0, 0)),
            ],
            scratch_shapes=[
                pltpu.VMEM((HEAD, GROUP * tile), jnp.float32),
                pltpu.VMEM((HEAD, key_count), jnp.bfloat16),
            ],
        ),
        out_shape=[
            jax.ShapeDtypeStruct(query_pre.shape, jnp.bfloat16),
            jax.ShapeDtypeStruct(query_pre.shape[::-1], jnp.bfloat16),
            jax.ShapeDtypeStruct(query_pre.shape, jnp.bfloat16),
            jax.ShapeDtypeStruct((tiles, groups, 1, GROUP * tile), jnp.float32),
        ],
        compiler_params=pltpu.CompilerParams(vmem_limit_bytes=VMEM),
        cost_estimate=FREE,
        name="attend",
    )(span, query_pre, cosine, sine, low.reshape(tiles, 1, tile), window, window, *deps)


def attend_back(query_rot, grad_rows, attn_rows, log_total, cosine_t, sine_t, low, window, deps):
    tok_rows = query_rot.shape[0]
    key_count = window.shape[0] - tok_rows
    tile, chunk, base, span = attention_plan(tok_rows, key_count, low)
    tiles = tok_rows // tile
    groups = HEADS // GROUP
    wide = GROUP * HEAD
    block = pl.BlockSpec((tile, wide), lambda i, g, s: (i, g))
    angle = pl.BlockSpec((HEAD // 2, tile), lambda i, g, s: (0, i))
    return pl.pallas_call(
        lambda *refs: attend_back_kernel(*refs, base=base, chunk=chunk),
        grid_spec=pltpu.PrefetchScalarGridSpec(
            num_scalar_prefetch=1,
            grid=(tiles, groups),
            in_specs=[
                block,
                block,
                block,
                pl.BlockSpec((1, 1, 1, GROUP * tile), lambda i, g, s: (i, g, 0, 0)),
                angle,
                angle,
                pl.BlockSpec((1, 1, tile), lambda i, g, s: (i, 0, 0)),
                pl.BlockSpec((key_count, HEAD), lambda i, g, s: (0, 0)),
                pl.BlockSpec((key_count, HEAD), lambda i, g, s: (0, 1)),
            ]
            + [pl.BlockSpec(memory_space=pl.ANY)] * len(deps),
            out_specs=[
                block,
                pl.BlockSpec((wide, tile), lambda i, g, s: (g, i)),
                pl.BlockSpec((key_count, 2 * HEAD), lambda i, g, s: (0, 0)),
            ],
            scratch_shapes=[
                pltpu.VMEM((key_count, HEAD), jnp.float32),
                pltpu.VMEM((key_count, HEAD), jnp.float32),
                pltpu.VMEM((HEAD, GROUP * tile), jnp.float32),
                pltpu.VMEM((HEAD, key_count), jnp.bfloat16),
            ],
        ),
        out_shape=[
            jax.ShapeDtypeStruct(query_rot.shape, jnp.bfloat16),
            jax.ShapeDtypeStruct(query_rot.shape[::-1], jnp.bfloat16),
            jax.ShapeDtypeStruct((key_count, 2 * HEAD), jnp.bfloat16),
        ],
        compiler_params=pltpu.CompilerParams(vmem_limit_bytes=VMEM),
        cost_estimate=FREE,
        name="attend_back",
    )(
        span, query_rot, grad_rows, attn_rows, log_total, cosine_t, sine_t, low.reshape(tiles, 1, tile),
        window, window, *deps,
    )


def nt(left, right):
    return lax.dot_general(
        left, right, (((1,), (1,)), ((), ())), preferred_element_type=jnp.float32
    )


def tn(left, right):
    return lax.dot_general(
        left, right, (((0,), (0,)), ((), ())), preferred_element_type=jnp.float32
    )


def flat(ref):
    block = ref[...]
    return block.reshape(-1, block.shape[-1])


def units_kernel(core_ref, *refs):
    tokens, cots = refs[0:2], refs[2:4]
    gate_ref, up_ref, down_ref = refs[4:7]
    out_ref = refs[-1]
    gate_rows, up_rows, down_rows = flat(gate_ref), flat(up_ref), flat(down_ref)

    def one(token_ref, cot_ref):
        gate = nt(gate_rows, token_ref[...])
        up = nt(up_rows, token_ref[...])
        grad_mixed = nt(down_rows, cot_ref[...])
        root = (2.0 / jnp.pi) ** 0.5
        square = gate * gate
        curve = jnp.tanh(root * (gate + 0.044715 * (square * gate)))
        upper = 0.5 * (1.0 + curve)
        activated = gate * upper
        slope = upper + 0.5 * gate * (1.0 - curve * curve) * (root * (1.0 + 0.134145 * square))
        out_ref[0] = (grad_mixed * up * slope).astype(jnp.bfloat16)
        out_ref[1] = (grad_mixed * activated).astype(jnp.bfloat16)
        out_ref[2] = (activated * up).astype(jnp.bfloat16)

    for j in (0, 1):
        pl.when(pl.program_id(1) == j)(lambda j=j: one(tokens[j], cots[j]))


def units(tokens, cots, weights, core, group, held, deps=()):
    cols, width = tokens[0].shape
    hidden = weights.hidden
    token_block = pl.BlockSpec((cols, width), lambda i, j, s: (0, 0))
    extra = (() if held is None else (held,)) + tuple(deps)
    return pl.pallas_call(
        units_kernel,
        grid_spec=pltpu.PrefetchScalarGridSpec(
            num_scalar_prefetch=1,
            grid=(2, 2),
            in_specs=[token_block] * 4
            + weights.specs(2, lambda i, j, s: (i, 0), width)
            + [pl.BlockSpec(memory_space=pl.ANY)] * len(extra),
            out_specs=pl.BlockSpec(
                (3, hidden // 2, cols), lambda i, j, s: (0, i, 2 * group + j)
            ),
        ),
        out_shape=jax.ShapeDtypeStruct((3, hidden, 4 * cols), jnp.bfloat16),
        input_output_aliases={} if held is None else {8: 0},
        compiler_params=pltpu.CompilerParams(vmem_limit_bytes=VMEM),
        cost_estimate=FREE,
        name="units",
    )(core, *tokens, *cots, *weights.arrays, *extra)


class OwnWeights:
    def __init__(self, shards):
        self.arrays = tuple(shards)
        self.hidden = shards[0].shape[0] // 2

    def specs(self, cuts, place, width):
        def index(*grid):
            row, col = place(*grid)
            return (grid[-1][0] * cuts + row, col)

        return [pl.BlockSpec((self.hidden // cuts, width), index)] * len(self.arrays)


class FarWeights:
    def __init__(self, gathered):
        parts, count, rows, width = gathered.shape
        self.hidden = parts * rows
        if rows % 16:
            gathered = gathered.reshape(2, parts // 2, count, rows, width)
            gathered = gathered.transpose(0, 2, 1, 3, 4).reshape(2, count, -1, width)
        self.arrays = (gathered,) * count

    def specs(self, cuts, place, width):
        parts, count, rows, _ = self.arrays[0].shape

        def spec(which):
            def index(*grid):
                row, col = place(*grid)
                return (row, which, 0, col)

            return pl.BlockSpec((parts // cuts, 1, rows, width), index)

        return [spec(which) for which in range(count)]


def sums_kernel(core_ref, *refs, count):
    total = 0.0
    for act_ref, weight_ref in zip(refs[:count], refs[count : 2 * count], strict=True):
        total = total + tn(act_ref[0], flat(weight_ref))
    refs[-1][...] = total.astype(jnp.bfloat16)


def sums(acts, weights, core, group, which, block=None, deps=()):
    all_tokens = acts[0].shape[2]
    width = weights[0].arrays[0].shape[-1]
    rows = all_tokens // 4
    blocks = 2 if block is None else 1
    cols = 512 if width % 512 == 0 else width // 2
    first = 2 * group + (block or 0)

    def act_spec(act, kind):
        return pl.BlockSpec((1, act.shape[1], rows), lambda n, t, s: (kind, 0, first + t))

    act_specs, weight_specs, act_args, weight_args = [], [], [], []
    for act, weight in zip(acts, weights, strict=True):
        specs = weight.specs(1, lambda n, t, s: (0, n), cols)
        for kind in which:
            act_specs.append(act_spec(act, kind))
            act_args.append(act)
            weight_specs.append(specs[kind])
            weight_args.append(weight.arrays[kind])
    return pl.pallas_call(
        lambda *refs: sums_kernel(*refs, count=len(act_args)),
        grid_spec=pltpu.PrefetchScalarGridSpec(
            num_scalar_prefetch=1,
            grid=(width // cols, blocks),
            in_specs=act_specs + weight_specs + [pl.BlockSpec(memory_space=pl.ANY)] * len(deps),
            out_specs=pl.BlockSpec((rows, cols), lambda n, t, s: (t, n)),
        ),
        out_shape=jax.ShapeDtypeStruct((blocks * rows, width), jnp.bfloat16),
        compiler_params=pltpu.CompilerParams(vmem_limit_bytes=VMEM),
        cost_estimate=FREE,
        name="sums",
    )(core, *act_args, *weight_args, *deps)


def grams_kernel(acts_ref, *refs, sets):
    out_ref = refs[-1]

    def one(rights):
        step = rights[0].shape[0]
        total = 0.0
        for i, right_ref in enumerate(rights):
            total = total + jnp.dot(
                acts_ref[0, :, i * step : (i + 1) * step], right_ref[...],
                preferred_element_type=jnp.float32,
            )
        out_ref[0] = total.astype(jnp.bfloat16)

    if sets == 1:
        one(refs[0:4])
    else:
        pl.when(pl.program_id(0) < 2)(lambda: one(refs[0:4]))
        pl.when(pl.program_id(0) == 2)(lambda: one(refs[4:8]))


def grams(acts, tokens, cots, pairs, kinds, deps=()):
    _, hidden, all_tokens = acts.shape
    step, width = tokens[0].shape
    cols = width // pairs
    first, count = kinds[0], len(kinds)
    if cols % 128:
        parts = []
        for kind in kinds:
            whole = sum(
                product(acts[kind, :, i * step : (i + 1) * step], right)
                for i, right in enumerate(cots if kind == 2 else tokens)
            )
            parts.append(whole.astype(jnp.bfloat16))
        return jnp.concatenate(parts, 0).reshape(count * hidden, pairs, cols).transpose(1, 0, 2)
    if count == 3:
        specs = [pl.BlockSpec((step, cols), lambda k, p: (0, jnp.where(k < 2, p, pairs - 1)))] * 4
        specs = specs + [pl.BlockSpec((step, cols), lambda k, p: (0, jnp.where(k < 2, 0, p)))] * 4
        rights = tuple(tokens) + tuple(cots)
    else:
        specs = [pl.BlockSpec((step, cols), lambda k, p: (0, p))] * 4
        rights = tuple(cots) if first == 2 else tuple(tokens)
    return pl.pallas_call(
        lambda *refs: grams_kernel(*refs, sets=len(rights) // 4),
        grid=(count, pairs),
        in_specs=[pl.BlockSpec((1, hidden, all_tokens), lambda k, p: (first + k, 0, 0))]
        + specs
        + [pl.BlockSpec(memory_space=pl.ANY)] * len(deps),
        out_specs=pl.BlockSpec((1, hidden, cols), lambda k, p: (p, k, 0)),
        out_shape=jax.ShapeDtypeStruct((pairs, count * hidden, cols), jnp.bfloat16),
        compiler_params=pltpu.CompilerParams(vmem_limit_bytes=VMEM),
        cost_estimate=FREE,
        name="grams",
    )(acts, *rights, *deps)


class Gathered:
    def __init__(self, own, others, shard):
        count, _, rows, width = others.shape
        if rows % 16:
            others = others.transpose(1, 0, 2, 3).reshape(1, -1, count * rows, width)
        self.own, self.others = own, others
        self.shard = shard.reshape(1).astype(jnp.int32)
        self.shards = others.shape[1] + 1

    def place(self, step, shard_ref):
        return lax.rem(shard_ref[0] + self.shards - step, self.shards)

    def specs(self):
        count, _, rows, width = self.others.shape
        return [
            pl.BlockSpec(self.own.shape, lambda r, s: (0, 0)),
            pl.BlockSpec((count, 1, rows, width), lambda r, s: (0, jnp.maximum(r - 1, 0), 0, 0)),
        ]


def by_shard(own_ref, others_ref, use):
    pl.when(pl.program_id(0) == 0)(lambda: use(own_ref[...]))
    pl.when(pl.program_id(0) > 0)(lambda: use(flat(others_ref)))


def spread_kernel(shard_ref, left_ref, own_ref, others_ref, *refs):
    out_ref = refs[-1]

    def use(weight):
        out_ref[...] = nt(left_ref[...], weight).astype(out_ref.dtype)

    by_shard(own_ref, others_ref, use)


def spread(left, weight, dtype, deps=()):
    tokens, width = left.shape
    rows = weight.own.shape[0]
    return pl.pallas_call(
        spread_kernel,
        grid_spec=pltpu.PrefetchScalarGridSpec(
            num_scalar_prefetch=1,
            grid=(weight.shards,),
            in_specs=[pl.BlockSpec((tokens, width), lambda r, s: (0, 0))]
            + weight.specs()
            + [pl.BlockSpec(memory_space=pl.ANY)] * len(deps),
            out_specs=pl.BlockSpec((tokens, rows), lambda r, s: (0, weight.place(r, s))),
        ),
        out_shape=jax.ShapeDtypeStruct((tokens, weight.shards * rows), dtype),
        compiler_params=pltpu.CompilerParams(vmem_limit_bytes=VMEM),
        cost_estimate=FREE,
        name="spread",
    )(weight.shard, left, weight.own, weight.others, *deps)


def collect_kernel(shard_ref, left_ref, own_ref, others_ref, start_ref, gain_ref, *refs, outs):
    refs = refs[-outs:]
    total_ref = refs[0]

    @pl.when(pl.program_id(0) == 0)
    def _():
        total_ref[...] = start_ref[...].astype(jnp.float32)

    def use(weight):
        total_ref[...] += jnp.dot(left_ref[...], weight, preferred_element_type=jnp.float32)

    by_shard(own_ref, others_ref, use)
    if outs > 1:

        @pl.when(pl.program_id(0) == pl.num_programs(0) - 1)
        def _():
            rows = min(128, total_ref.shape[0])

            def norm(i, carry):
                here = pl.ds(pl.multiple_of(i * rows, rows), rows)
                total = total_ref[here, :]
                scale = norm_scale(total)
                refs[1][here, :] = (total * scale * gain_ref[...]).astype(jnp.bfloat16)
                refs[2][here, :] = jnp.broadcast_to(scale, (rows, 128))
                return carry

            lax.fori_loop(0, total_ref.shape[0] // rows, norm, 0)


def collect(left, weight, start, gain=None, deps=()):
    tokens = left.shape[0]
    rows, width = weight.own.shape
    whole = pl.BlockSpec((tokens, width), lambda r, s: (0, 0))
    shapes, specs = [jax.ShapeDtypeStruct((tokens, width), jnp.float32)], [whole]
    if gain is not None:
        shapes.append(jax.ShapeDtypeStruct((tokens, width), jnp.bfloat16))
        shapes.append(jax.ShapeDtypeStruct((tokens, 128), jnp.float32))
        specs.extend([whole, pl.BlockSpec((tokens, 128), lambda r, s: (0, 0))])
    gain_row = jnp.zeros((1, width), jnp.float32) if gain is None else gain.reshape(1, width)
    return pl.pallas_call(
        lambda *refs: collect_kernel(*refs, outs=len(specs)),
        grid_spec=pltpu.PrefetchScalarGridSpec(
            num_scalar_prefetch=1,
            grid=(weight.shards,),
            in_specs=[pl.BlockSpec((tokens, rows), lambda r, s: (0, weight.place(r, s)))]
            + weight.specs()
            + [whole, pl.BlockSpec((1, width), lambda r, s: (0, 0))]
            + [pl.BlockSpec(memory_space=pl.ANY)] * len(deps),
            out_specs=specs,
        ),
        out_shape=shapes,
        compiler_params=pltpu.CompilerParams(vmem_limit_bytes=VMEM),
        cost_estimate=FREE,
        name="collect",
    )(weight.shard, left, weight.own, weight.others, start, gain_row, *deps)


def cross_kernel(core_ref, *refs, lefts, gained, added):
    right_ref, out_ref = refs[lefts], refs[-1]
    first = 0

    def put(part, rows):
        here = (0, slice(None), slice(first, first + rows))
        if added:
            part = part + refs[lefts + 1 + gained][here].astype(jnp.float32)
        out_ref[here] = part.astype(jnp.bfloat16)

    for left_ref in refs[:lefts]:
        shards, _, rows, tokens = left_ref.shape
        left = left_ref[...].reshape(shards * rows, tokens)
        part = jnp.dot(left, right_ref[...], preferred_element_type=jnp.float32)
        put(part.reshape(shards, rows, -1), rows)
        first = first + rows
    if gained:
        gains = refs[lefts + 1][...].astype(jnp.float32)
        put(jnp.broadcast_to(gains[None], (out_ref.shape[1],) + gains.shape), gains.shape[0])


def cross(lefts, right, core, shards, pairs, gains=None, add=None, deps=(), first=0, of=None, into=None):
    tokens, width = right.shape
    cols = width // pairs
    views = [left.reshape(shards, 2, -1, tokens) for left in lefts]
    rows = [view.shape[2] for view in views]
    total = sum(rows) + (0 if gains is None else gains.shape[0])
    if cols % 128:
        picked = jnp.concatenate(
            [lax.dynamic_index_in_dim(view, core[0], 1, keepdims=False) for view in views], 1
        )
        whole = product(picked.reshape(-1, tokens), right).reshape(shards, sum(rows), width)
        if gains is not None:
            extra = jnp.broadcast_to(gains.astype(jnp.float32)[None], (shards,) + gains.shape)
            whole = jnp.concatenate([whole, extra], 1)
        whole = whole.reshape(shards, total, pairs, cols).transpose(2, 0, 1, 3)
        if add is not None:
            whole = whole + add[:, :, first : first + total].astype(jnp.float32)
        whole = whole.astype(jnp.bfloat16)
        if of is None:
            return whole
        if into is None:
            into = jnp.zeros((pairs, shards, of, cols), jnp.bfloat16)
        return lax.dynamic_update_slice(into, whole, (0, 0, first, 0))
    block = pl.BlockSpec((1, shards, total, cols), lambda p, s: (p, 0, first // total, 0))
    kept = () if into is None else (into,)
    specs = [
        pl.BlockSpec((shards, 1, count, tokens), lambda p, s: (0, s[0], 0, 0)) for count in rows
    ]
    specs.append(pl.BlockSpec((tokens, cols), lambda p, s: (0, p)))
    args = [*views, right]
    if gains is not None:
        specs.append(pl.BlockSpec((gains.shape[0], cols), lambda p, s: (0, p)))
        args.append(gains)
    if add is not None:
        specs.append(block)
        args.append(add)
    return pl.pallas_call(
        lambda *refs: cross_kernel(
            *refs, lefts=len(views), gained=gains is not None, added=add is not None
        ),
        grid_spec=pltpu.PrefetchScalarGridSpec(
            num_scalar_prefetch=1,
            grid=(pairs,),
            in_specs=specs + [pl.BlockSpec(memory_space=pl.ANY)] * (len(kept) + len(deps)),
            out_specs=block,
        ),
        out_shape=jax.ShapeDtypeStruct((pairs, shards, of or total, cols), jnp.bfloat16),
        input_output_aliases={1 + len(args): 0} if kept else {},
        compiler_params=pltpu.CompilerParams(vmem_limit_bytes=VMEM),
        cost_estimate=FREE,
        name="cross",
    )(core, *args, *kept, *deps)


def swap(value, axis, bit):
    return lax.ppermute(value, axis, [(i, i ^ bit) for i in range(lax.axis_size(axis))])


def after(value, *others):
    return lax.optimization_barrier((value, *others))[0]


def same_core():
    count = lax.axis_size("ctx")
    return [list(range(0, count, 2)), list(range(1, count, 2))]


def own_part(shard, place):
    part = shard.shape[0] // lax.axis_size("ctx")
    return lax.dynamic_slice_in_dim(shard, place * part, part, 0)


def together(*values):
    return lax.optimization_barrier(values)


def halving_scatter(blocks, axis, place):
    held, bit = blocks, 1
    while held.shape[0] > 1:
        both = held.reshape((held.shape[0] // 2, 2) + held.shape[1:])
        mine = (place // bit) % 2
        keep = lax.dynamic_index_in_dim(both, mine, 1, keepdims=False)
        give = lax.dynamic_index_in_dim(both, 1 - mine, 1, keepdims=False)
        total = keep.astype(jnp.float32) + swap(give, axis, bit).astype(jnp.float32)
        held = total.astype(jnp.bfloat16)
        bit = 2 * bit
    return total[0]


def step_ring(value, axis):
    count = lax.axis_size(axis)
    return lax.ppermute(value, axis, [(i, (i + 1) % count) for i in range(count)])


def ring(value, axis):
    arrived = []
    for _ in range(lax.axis_size(axis) - 1):
        value = step_ring(value, axis)
        arrived.append(value)
    return arrived


def exchanges(axis):
    bits, bit = [], 2
    while bit < lax.axis_size(axis):
        bits.append(bit)
        bit = 2 * bit
    return bits + [1]


def pairs_gather(value):
    pairs = lax.axis_size("ctx") // 2
    if pairs == 4:
        half = value.shape[0] // 2
        x_all, y_all = swap(value, "ctx", 2), swap(value, "ctx", 4)
        low = swap(y_all[:half], "ctx", 2)
        high = swap(x_all[half:], "ctx", 4)
        return [(0, [value]), (2, [x_all]), (4, [y_all]), (6, [low, high])]
    held, bit = [(0, value)], 2
    while bit < 2 * pairs:
        held = held + [(bits ^ bit, swap(item, "ctx", bit)) for bits, item in held]
        bit = 2 * bit
    return [(bits, [item]) for bits, item in held]


def window_gather(value, reach, place):
    rows = value.shape[0]
    out = jnp.zeros(((reach + 2) * rows,) + value.shape[1:], value.dtype)
    parts = [(bits, part, i) for bits, held in pairs_gather(value) for i, part in enumerate(held)]
    for bits, part, i in parts:
        both = ((bits, part), (bits ^ 1, swap(part, "ctx", 1)))
        for other, block in both:
            spot = (place ^ other) - place + reach
            spot = jnp.where((spot < 0) | (spot > reach), reach + 1, spot)
            start = spot * rows + (i * block.shape[0])
            out = lax.dynamic_update_slice_in_dim(out, block, start, 0)
    return out


def place_block(out, block, place):
    return lax.dynamic_update_index_in_dim(out, block, place, 0)


def in_places(own, arrived, place):
    count = len(arrived) + 1
    out = jnp.zeros((count,) + own.shape, own.dtype)
    for step, value in enumerate([own, *arrived]):
        out = lax.dynamic_update_index_in_dim(out, value, lax.rem(place + count - step, count), 0)
    return out


def in_order(gathered, first, part):
    mine = gathered[:, :, first : first + part].transpose(1, 0, 2, 3)
    return mine.reshape(-1, gathered.shape[-1])


def body(
    inputs,
    norm_gains,
    q_weight,
    kv_weight,
    o_weight,
    gate_weight,
    up_weight,
    down_weight,
    cotangent,
    doc_lengths,
):
    x_rows = inputs[0].astype(jnp.float32)
    grad_out = cotangent[0]
    tok_rows, width = x_rows.shape
    place = lax.axis_index("ctx")
    ctx_count = lax.axis_size("ctx")
    pairs = ctx_count // 2
    core = place % 2
    pair = place // 2
    own_core = core.reshape(1).astype(jnp.int32)
    shard = lax.axis_index("fsdp")
    shards = lax.axis_size("fsdp")
    reach = min(ctx_count - 1, (WINDOW + tok_rows - 2) // tok_rows)
    key_count = (reach + 1) * tok_rows
    first_token = place * tok_rows
    token_ids, segment, positions = doc_info(doc_lengths[0], first_token, tok_rows)
    low = jnp.maximum(token_ids - positions, token_ids - (WINDOW - 1)) - (
        first_token - reach * tok_rows
    )
    cosine, sine = rope_angles(positions)
    gain_attn = norm_gains[0]
    gain_mlp = norm_gains[1]

    q_part, kv_part, o_part = (own_part(w, place) for w in (q_weight, kv_weight, o_weight))
    kv_z = in_places(kv_part, ring(kv_part, "fsdp"), shard)
    moving = after(q_part, kv_z)
    held, origins = kv_z[None], [place]
    q_arrived = []
    for bit in exchanges("ctx"):
        if len(q_arrived) < shards - 1:
            moving = step_ring(moving, "fsdp")
            q_arrived.append(moving)
        held = jnp.concatenate([held, swap(held, "ctx", bit)], 0)
        origins = origins + [origin ^ bit for origin in origins]
        held, moving = together(held, moving)
    while len(q_arrived) < shards - 1:
        moving = step_ring(moving, "fsdp")
        q_arrived.append(moving)
    kv_all = jnp.zeros_like(held)
    for step, origin in enumerate(origins):
        kv_all = place_block(kv_all, held[step], origin)
    q_ring = jnp.stack(q_arrived, 0)
    q_ring, kv_all = together(q_ring, kv_all)
    q_all = lax.all_gather(q_ring, "ctx", axis=0)

    half_rows = gate_weight.shape[0] // 2
    part_rows = half_rows // pairs
    cut = (part_rows * 7 // 15 + 15) // 16 * 16
    far_rows, last_rows = cut // 4, part_rows - cut
    mine = jnp.stack(
        [
            lax.dynamic_slice_in_dim(w, core * half_rows + pair * part_rows, part_rows, 0)
            for w in (gate_weight, up_weight, down_weight)
        ],
        0,
    )
    mine, _ = together(mine, q_ring)
    own_weights = OwnWeights((gate_weight, up_weight, down_weight))

    scale_one = norm_scale(x_rows)
    normed_one = (x_rows * scale_one * gain_attn).astype(jnp.bfloat16)
    kv_full = in_order(kv_all, 0, kv_part.shape[0])
    kv_pre = times_rows(normed_one, kv_full)
    key_rot = rotate(kv_pre[:, :HEAD], cosine, sine).astype(jnp.bfloat16)
    kv_local = jnp.concatenate([key_rot, kv_pre[:, HEAD:].astype(jnp.bfloat16)], 1)
    kv_local, moving = together(kv_local, o_part)
    kv_window = window_gather(kv_local, reach, place)
    o_arrived = ring(moving, "fsdp")
    cot_rows = tok_rows // 8
    cot_first = swap(after(grad_out[:cot_rows], o_arrived[-1]), "fsdp", 1)
    far_first = swap(after(mine[:, :far_rows], o_arrived[-1]), "fsdp", 2)
    o_ring = jnp.stack(o_arrived, 0)
    q_all, o_ring, far_first, cot_first, kv_window, normed_one, cosine_t, sine_t = together(
        q_all, o_ring, far_first, cot_first, kv_window, normed_one, cosine.T, sine.T
    )
    o_all = lax.all_gather(o_ring, "ctx", axis=0)
    q_full = Gathered(q_weight, q_all, shard)
    o_full = Gathered(o_weight, o_all, shard)
    far_second = swap(after(mine[:, far_rows : part_rows - last_rows], o_ring), "fsdp", 2)
    cot_second = swap(after(grad_out[cot_rows:], o_ring), "fsdp", 1)
    query_pre = spread(normed_one, q_full, jnp.float32)
    attn_rows, attn_rows_t, query_rot, log_total = attend(
        query_pre, cosine, sine, low, kv_window
    )
    far_last = mine[:, part_rows - last_rows :]
    log_total, cot_second, far_second, far_last = together(
        log_total, cot_second, far_second, far_last
    )
    far_third = swap(far_last, "fsdp", 2)
    near_cots = (grad_out, swap(grad_out, "ctx", 1))
    cot_across = jnp.concatenate([cot_first, cot_second], 0)
    cots = [near_cots, (cot_across, swap(cot_across, "ctx", 1))]

    def over_plane(part):
        return lax.all_gather(part, "ctx", axis=0, axis_index_groups=same_core())

    far_a = FarWeights(
        over_plane(jnp.concatenate([far_first, far_second], 1))
    )
    hidden_one, normed_two, scale_two = collect(attn_rows, o_full, inputs[0], gain_mlp)
    scale_two = scale_two[:, :1]

    near = (normed_two, swap(normed_two, "ctx", 1))
    across = swap(normed_two, "fsdp", 1)
    own_acts = units(near, near_cots, own_weights, own_core, 0, None)
    a_acts = units(near, near_cots, far_a, own_core, 0, None, (own_acts, cots[1][1]))
    across, a_acts, far_third = together(across, a_acts, far_third)
    far = (across, swap(across, "ctx", 1))
    far_b = FarWeights(over_plane(far_third))
    own_acts = units(far, cots[1], own_weights, own_core, 1, own_acts, (a_acts,))
    a_acts = units(far, cots[1], far_a, own_core, 1, a_acts, (own_acts,))
    near_far, cot_rows = near + far, cots[0] + cots[1]

    def over_pairs(blocks):
        mine = lax.psum_scatter(
            blocks, "ctx", scatter_dimension=0, tiled=False, axis_index_groups=same_core()
        )
        return lax.optimization_barrier(mine)

    a_grams = grams(a_acts, near_far, cot_rows, pairs, (0, 1, 2))
    b_acts = units(near, cots[0], far_b, own_core, 0, None, (a_grams,))
    b_acts = units(far, cots[1], far_b, own_core, 1, b_acts)
    b_grams = grams(b_acts, near_far, cot_rows, pairs, (0, 1, 2))
    a_sums, b_sums = over_pairs(a_grams), over_pairs(b_grams)
    acts, weights = (own_acts, a_acts, b_acts), (own_weights, far_a, far_b)

    def group_sums(group, which, block, deps):
        return sums(acts, weights, own_core, group, which, block, deps)

    own_gate_up = grams(own_acts, near_far, cot_rows, pairs, (0, 1), (b_grams,))
    give = group_sums(1, (0, 1), 1, (own_gate_up,))
    own_gate_up = over_pairs(own_gate_up)
    got = swap(give, "ctx", 1)
    near_give = group_sums(0, (0, 1), 1, (give,))
    near_got = swap(near_give, "ctx", 1)
    keep = group_sums(1, (0, 1), 0, (near_give, a_sums))
    total = add16(keep, got)
    moved = swap(total, "fsdp", 1)
    own_down = grams(own_acts, near_far, cot_rows, pairs, (2,), (total, near_got))
    near_keep = group_sums(0, (0, 1), 0, (own_down,))
    out_give = group_sums(1, (2,), 1, (near_keep,))
    out_got = swap(out_give, "ctx", 1)
    out_keep = group_sums(1, (2,), 0, (out_give,))
    moved, own_down, near_keep, out_keep, a_sums = together(
        moved, own_down, near_keep, out_keep, a_sums
    )
    own_down = over_pairs(own_down)
    grad_normed_two = (
        near_keep.astype(jnp.float32) + near_got.astype(jnp.float32) + moved.astype(jnp.float32)
    )
    grad_hidden = grad_out.astype(jnp.float32) + norm_back(
        grad_normed_two, hidden_one, scale_two, gain_mlp
    )
    gain_mlp_grad = jnp.sum(grad_normed_two * hidden_one * scale_two, 0)
    grad_branch = grad_hidden.astype(jnp.bfloat16)
    grad_attended = spread(grad_branch, o_full, jnp.bfloat16, (b_sums,))

    gate_rows = b_sums.shape[0] // 3
    a_all = swap(a_sums, "fsdp", 2)
    grad_query_pre, grad_query_pre_t, grad_kv = attend_back(
        query_rot, grad_attended, attn_rows, log_total, cosine_t, sine_t, low, kv_window,
        (out_keep,),
    )
    grad_stack = grad_kv.reshape(reach + 1, tok_rows, 2 * HEAD)
    moved_kv = [shifted(grad_stack[reach - hop], "ctx", -hop) for hop in range(1, reach + 1)]
    out_total = add16(out_keep, out_got)
    q_give = cross(
        [grad_query_pre_t], normed_one, 1 - own_core, shards, pairs,
        deps=(grad_kv, a_all, own_gate_up, out_total),
    )
    q_got = swap(q_give, "ctx", 1)
    q_half, kv_half = q_weight.shape[0] // 2, kv_weight.shape[0] // 2
    okv_rows = q_half + kv_half + 16
    okv_give = cross(
        [attn_rows_t], grad_branch, 1 - own_core, shards, pairs, deps=(q_give,), of=okv_rows
    )
    q_sums = cross(
        [grad_query_pre_t], normed_one, own_core, shards, pairs, None, q_got, (okv_give,)
    )
    moved_kv, q_sums, b_sums = together(moved_kv, q_sums, b_sums)
    b_gate = swap(b_sums[:gate_rows], "fsdp", 2)
    b_up = swap(after(b_sums[gate_rows : 2 * gate_rows], b_gate), "fsdp", 2)
    b_down = swap(after(b_sums[2 * gate_rows :], b_up), "fsdp", 2)
    q_pairs = over_pairs(q_sums)
    own_kv_grad = grad_stack[reach].astype(jnp.float32)
    for block in moved_kv:
        own_kv_grad = own_kv_grad + block.astype(jnp.float32)
    grad_kv_pre = jnp.concatenate(
        [rotate_back(own_kv_grad[:, :HEAD], cosine, sine), own_kv_grad[:, HEAD:]], 1
    ).astype(jnp.bfloat16)
    (grad_normed_one,) = collect(
        grad_query_pre, q_full, product(grad_kv_pre, kv_full)
    )
    gain_attn_grad = jnp.sum(grad_normed_one * x_rows * scale_one, 0)
    gains = jnp.stack([gain_attn_grad, gain_mlp_grad], 0).astype(jnp.bfloat16)
    gains = jnp.concatenate([gains, jnp.zeros((14, width), jnp.bfloat16)], 0)
    kv_left = [grad_kv_pre.T]
    okv_give = cross(
        kv_left, normed_one, 1 - own_core, shards, pairs, gains, None, (b_gate,), q_half,
        okv_rows, okv_give,
    )
    okv_got = swap(okv_give, "ctx", 1)
    near_out = sums(acts, weights, own_core, 0, (2,), None, (okv_give,))
    near_out_got = swap(near_out[tok_rows:], "ctx", 1)
    okv_sums = cross(
        [attn_rows_t], grad_branch, own_core, shards, pairs, None, okv_got, (near_out, b_up),
        of=okv_rows,
    )
    okv_sums = cross(
        kv_left, normed_one, own_core, shards, pairs, gains, okv_got, (own_down, q_pairs), q_half, okv_rows,
        okv_sums,
    )
    grad_inputs = grad_hidden + norm_back(grad_normed_one, x_rows, scale_one, gain_attn)

    out_cols = width // ctx_count

    def both_halves(mine):
        keep = lax.dynamic_slice_in_dim(mine, core * out_cols, out_cols, 1)
        give = lax.dynamic_slice_in_dim(mine, (1 - core) * out_cols, out_cols, 1)
        got = swap(give.astype(jnp.bfloat16), "ctx", 1).astype(jnp.float32)
        lower = jnp.where(core == 0, keep, got)
        upper = jnp.where(core == 0, got, keep)
        return jnp.concatenate([lower, upper], 0)

    okv_pairs = over_pairs(okv_sums)
    out_moved = swap(out_total, "fsdp", 1)
    q_mine = halving_scatter(q_pairs, "fsdp", shard)
    b_down, q_mine = together(b_down, q_mine)
    result = hidden_one + (
        near_out[:tok_rows].astype(jnp.float32)
        + near_out_got.astype(jnp.float32)
        + out_moved.astype(jnp.float32)
    )
    q_grad = both_halves(q_mine)
    okv_mine = halving_scatter(okv_pairs, "fsdp", shard)
    o_grad = both_halves(okv_mine[:q_half])
    kv_grad = both_halves(okv_mine[q_half : q_half + kv_half])
    gain_total = lax.dynamic_slice_in_dim(
        okv_mine[q_half + kv_half : q_half + kv_half + 2], core * out_cols, out_cols, 1
    )

    a_all = a_all.reshape(3, pairs, cut, -1)
    b_all = jnp.concatenate([b_gate, b_up, b_down], 0).reshape(3, pairs, part_rows - cut, -1)
    own_all = (own_gate_up[:half_rows], own_gate_up[half_rows:], own_down)
    mlp_grads = []
    for kind in range(3):
        others = jnp.concatenate([a_all[kind], b_all[kind]], 1).reshape(half_rows, -1)
        mlp_grads.append(
            both_halves(own_all[kind].astype(jnp.float32) + others.astype(jnp.float32))
        )

    return (
        result.astype(jnp.bfloat16)[None],
        grad_inputs.astype(jnp.bfloat16)[None],
        gain_total,
        q_grad,
        kv_grad,
        o_grad,
        mlp_grads[0],
        mlp_grads[1],
        mlp_grads[2],
    )


def solution(mesh):
    in_specs = (
        P("fsdp", "ctx", None),
        P(),
        P("fsdp", None),
        P("fsdp", None),
        P("fsdp", None),
        P("fsdp", None),
        P("fsdp", None),
        P("fsdp", None),
        P("fsdp", "ctx", None),
        P("fsdp", None),
    )
    out_specs = (
        P("fsdp", "ctx", None),
        P("fsdp", "ctx", None),
        P(None, "ctx"),
        P("fsdp", "ctx"),
        P("fsdp", "ctx"),
        P("fsdp", "ctx"),
        P("fsdp", "ctx"),
        P("fsdp", "ctx"),
        P("fsdp", "ctx"),
    )
    return jax.shard_map(body, mesh=mesh, in_specs=in_specs, out_specs=out_specs, check_vma=False)
```

```python
import jax
import jax.numpy as jnp
from jax import lax
from jax.experimental import pallas as pl
from jax.experimental.pallas import tpu as pltpu
from jax.sharding import PartitionSpec as P

HEADS = 10
HEAD = 256
WINDOW = 2048


EPSILON = 1e-06
MASKED = -1e30
LOWEST = -1e29
VMEM = 56 * 1024 * 1024
FREE = pl.CostEstimate(flops=0, bytes_accessed=0, transcendentals=0)


def shifted(value, axis, steps):
    count = lax.axis_size(axis)
    initial, last = (max(0, -steps), min(count, count - steps))
    return lax.ppermute(value, axis, [(source, source + steps) for source in range(initial, last)])


def swap(value, axis, bit):
    return lax.ppermute(value, axis, [(i, i ^ bit) for i in range(lax.axis_size(axis))])


def add16(left, right):
    return (left.astype(jnp.float32) + right.astype(jnp.float32)).astype(jnp.bfloat16)


def times_rows(left, right):
    return lax.dot_general(
        left, right, (((1,), (1,)), ((), ())), preferred_element_type=jnp.float32
    )


def gram_rows(left, right):
    return lax.dot_general(
        left, right, (((0,), (0,)), ((), ())), preferred_element_type=jnp.float32
    )


def product(left, right):
    return jnp.dot(left, right, preferred_element_type=jnp.float32)


def doc_info(doc_lengths, first_token, token_count):
    doc_ends = jnp.cumsum(doc_lengths)
    doc_starts = doc_ends - doc_lengths
    token_ids = first_token + jnp.arange(token_count, dtype=jnp.int32)
    segment = jnp.sum((doc_ends[None, :] <= token_ids[:, None]).astype(jnp.int32), 1)
    begins = jnp.max(
        jnp.where(doc_starts[None, :] <= token_ids[:, None], doc_starts[None, :], 0), 1
    )
    return (token_ids, segment, token_ids - begins)


def rope_angles(positions):
    half_width = HEAD // 2
    column = jnp.arange(half_width, dtype=jnp.float32)
    inverse = jnp.power(10000.0, -column / half_width)
    angles = positions.astype(jnp.float32)[:, None] * inverse[None, :]
    return (jnp.cos(angles), jnp.sin(angles))


def rotate(values, cosine, sine):
    half_width = values.shape[-1] // 2
    first_half = values[..., :half_width]
    second_half = values[..., half_width:]
    return jnp.concatenate(
        [first_half * cosine - second_half * sine, second_half * cosine + first_half * sine], -1
    )


def rotate_back(grad_in, cosine, sine):
    half_width = grad_in.shape[-1] // 2
    first_half = grad_in[..., :half_width]
    second_half = grad_in[..., half_width:]
    return jnp.concatenate(
        [first_half * cosine + second_half * sine, second_half * cosine - first_half * sine], -1
    )


def norm_scale(values):
    return lax.rsqrt(jnp.mean(values * values, -1, keepdims=True) + EPSILON)


def norm_back(grad_in, values, scale, gain):
    weighted = grad_in * gain
    return scale * weighted - values * scale * scale * scale * jnp.mean(
        weighted * values, -1, keepdims=True
    )


def head_rows(block, count):
    return jnp.concatenate([block[:, h * HEAD : (h + 1) * HEAD] for h in range(count)], 0)


def row_bounds(low_ref, first_key, tokens, count):
    high = first_key + lax.broadcasted_iota(jnp.int32, (1, tokens), 1)
    low = low_ref[0]
    return jnp.concatenate([low] * count, 1), jnp.concatenate([high] * count, 1)


def seen(start, shape, low, high):
    key = start + lax.broadcasted_iota(jnp.int32, shape, 0)
    return (key >= low) & (key <= high)


def turn(from_ref, to_ref, chunk):
    def step(j, carry):
        here = pl.ds(pl.multiple_of(j * chunk, chunk), chunk)
        to_ref[:, here] = from_ref[here, :].astype(jnp.float32).T.astype(jnp.bfloat16)
        return carry

    lax.fori_loop(0, from_ref.shape[0] // chunk, step, 0)


def attend_kernel(
    span_ref, pre_ref, cos_ref, sin_ref, low_ref, key_ref, value_ref, *refs, base, chunk
):
    out_ref, out_t_ref, rot_ref, log_ref, acc, value_t_ref = refs[-6:]

    @pl.when((pl.program_id(0) == 0) & (pl.program_id(1) == 0))
    def _():
        turn(value_ref, value_t_ref, chunk)

    tile = pl.program_id(0)
    tokens = pre_ref.shape[0]
    count = pre_ref.shape[1] // HEAD
    cosine, sine = cos_ref[...], sin_ref[...]
    half = HEAD // 2
    for h in range(count):
        first = pre_ref[:, h * HEAD : h * HEAD + half]
        second = pre_ref[:, h * HEAD + half : (h + 1) * HEAD]
        rot_ref[:, h * HEAD : h * HEAD + half] = (
            (first * cosine - second * sine) * HEAD ** (-0.5)
        ).astype(jnp.bfloat16)
        rot_ref[:, h * HEAD + half : (h + 1) * HEAD] = (
            (second * cosine + first * sine) * HEAD ** (-0.5)
        ).astype(jnp.bfloat16)
    query = head_rows(rot_ref[...], count)
    low, high = row_bounds(low_ref, base + tile * tokens, tokens, count)
    rows = count * tokens

    acc[...] = jnp.zeros_like(acc)

    def step(j, carry):
        top, total = carry
        start = pl.multiple_of(j * chunk, chunk)
        scores = lax.dot_general(
            key_ref[pl.ds(start, chunk), :], query, (((1,), (1,)), ((), ())),
            preferred_element_type=jnp.float32,
        )
        scores = jnp.where(seen(start, scores.shape, low, high), scores, MASKED)
        higher = jnp.maximum(top, jnp.max(scores, 0, keepdims=True))
        part = jnp.exp(scores - higher)
        shrink = jnp.exp(top - higher)
        acc[...] = acc[...] * shrink + lax.dot_general(
            value_t_ref[:, pl.ds(start, chunk)], part.astype(jnp.bfloat16), (((1,), (0,)), ((), ())),
            preferred_element_type=jnp.float32,
        )
        return higher, total * shrink + jnp.sum(part, 0, keepdims=True)

    top, total = lax.fori_loop(
        span_ref[0, tile], span_ref[1, tile], step,
        (jnp.full((1, rows), LOWEST, jnp.float32), jnp.zeros((1, rows), jnp.float32)),
    )
    log_ref[0, 0] = top + jnp.log(total)
    outs_t = acc[...] * (1.0 / total)
    outs = outs_t.T.astype(jnp.bfloat16)
    outs_t = outs_t.astype(jnp.bfloat16)
    for h in range(count):
        out_t_ref[h * HEAD : (h + 1) * HEAD, :] = outs_t[:, h * tokens : (h + 1) * tokens]
        out_ref[:, h * HEAD : (h + 1) * HEAD] = outs[h * tokens : (h + 1) * tokens]


def attend_back_kernel(
    span_ref, rot_ref, grad_ref, out_ref, log_ref, cos_ref, sin_ref, low_ref, key_ref, value_ref,
    *refs, base, chunk
):
    pre_ref, pre_t_ref, grad_kv_ref, grad_key_ref, grad_value_ref, acc, key_t_ref = refs[-7:]
    tile = pl.program_id(0)
    tokens = rot_ref.shape[0]
    count = rot_ref.shape[1] // HEAD

    @pl.when((tile == 0) & (pl.program_id(1) == 0))
    def _():
        turn(key_ref, key_t_ref, chunk)
        grad_key_ref[...] = jnp.zeros_like(grad_key_ref)
        grad_value_ref[...] = jnp.zeros_like(grad_value_ref)

    query = head_rows(rot_ref[...], count)
    grad = head_rows(grad_ref[...], count)
    outs = head_rows(out_ref[...], count)
    delta = jnp.sum((grad.astype(jnp.float32) * outs.astype(jnp.float32)).T, 0, keepdims=True)
    log_total = log_ref[0, 0]
    low, high = row_bounds(low_ref, base + tile * tokens, tokens, count)
    acc[...] = jnp.zeros_like(acc)

    def step(j, carry):
        start = pl.multiple_of(j * chunk, chunk)
        here = pl.ds(start, chunk)
        scores = lax.dot_general(
            key_ref[here, :], query, (((1,), (1,)), ((), ())), preferred_element_type=jnp.float32
        )
        grad_probs = lax.dot_general(
            value_ref[here, :], grad, (((1,), (1,)), ((), ())), preferred_element_type=jnp.float32
        )
        probs = jnp.where(seen(start, scores.shape, low, high), jnp.exp(scores - log_total), 0.0)
        grad_scores = (probs * (grad_probs - delta)).astype(jnp.bfloat16)
        grad_value_ref[here, :] += jnp.dot(
            probs.astype(jnp.bfloat16), grad, preferred_element_type=jnp.float32
        )
        grad_key_ref[here, :] += jnp.dot(grad_scores, query, preferred_element_type=jnp.float32)
        acc[...] += lax.dot_general(
            key_t_ref[:, here], grad_scores, (((1,), (0,)), ((), ())),
            preferred_element_type=jnp.float32,
        )
        return carry

    lax.fori_loop(span_ref[0, tile], span_ref[1, tile], step, 0)
    cosine, sine = cos_ref[...], sin_ref[...]
    half = HEAD // 2
    for h in range(count):
        own = acc[:, h * tokens : (h + 1) * tokens] * HEAD ** (-0.5)
        first, second = own[:half], own[half:]
        own = jnp.concatenate(
            [first * cosine + second * sine, second * cosine - first * sine], 0
        )
        pre_t_ref[h * HEAD : (h + 1) * HEAD, :] = own.astype(jnp.bfloat16)
        pre_ref[:, h * HEAD : (h + 1) * HEAD] = own.T.astype(jnp.bfloat16)

    @pl.when((tile == pl.num_programs(0) - 1) & (pl.program_id(1) == pl.num_programs(1) - 1))
    def _():
        grad_kv_ref[:, :HEAD] = grad_key_ref[...].astype(jnp.bfloat16)
        grad_kv_ref[:, HEAD:] = grad_value_ref[...].astype(jnp.bfloat16)


def attention_plan(tok_rows, key_count, low):
    tile = min(128, tok_rows)
    chunk = 256 if key_count % 256 == 0 else 128
    base = key_count - tok_rows
    tiles = tok_rows // tile
    begin = low[::tile] // chunk
    end = (base + (jnp.arange(tiles, dtype=jnp.int32) + 1) * tile + chunk - 1) // chunk
    return tile, chunk, base, jnp.stack([begin, end], 0).astype(jnp.int32)


GROUP = 10


def attend(query_pre, cosine, sine, low, window, deps=()):
    tok_rows = query_pre.shape[0]
    key_count = window.shape[0] - tok_rows
    tile, chunk, base, span = attention_plan(tok_rows, key_count, low)
    tiles = tok_rows // tile
    groups = HEADS // GROUP
    wide = GROUP * HEAD
    block = pl.BlockSpec((tile, wide), lambda i, g, s: (i, g))
    angle = pl.BlockSpec((tile, HEAD // 2), lambda i, g, s: (i, 0))
    return pl.pallas_call(
        lambda *refs: attend_kernel(*refs, base=base, chunk=chunk),
        grid_spec=pltpu.PrefetchScalarGridSpec(
            num_scalar_prefetch=1,
            grid=(tiles, groups),
            in_specs=[
                block,
                angle,
                angle,
                pl.BlockSpec((1, 1, tile), lambda i, g, s: (i, 0, 0)),
                pl.BlockSpec((key_count, HEAD), lambda i, g, s: (0, 0)),
                pl.BlockSpec((key_count, HEAD), lambda i, g, s: (0, 1)),
            ]
            + [pl.BlockSpec(memory_space=pl.ANY)] * len(deps),
            out_specs=[
                block,
                pl.BlockSpec((wide, tile), lambda i, g, s: (g, i)),
                block,
                pl.BlockSpec((1, 1, 1, GROUP * tile), lambda i, g, s: (i, g, 0, 0)),
            ],
            scratch_shapes=[
                pltpu.VMEM((HEAD, GROUP * tile), jnp.float32),
                pltpu.VMEM((HEAD, key_count), jnp.bfloat16),
            ],
        ),
        out_shape=[
            jax.ShapeDtypeStruct(query_pre.shape, jnp.bfloat16),
            jax.ShapeDtypeStruct(query_pre.shape[::-1], jnp.bfloat16),
            jax.ShapeDtypeStruct(query_pre.shape, jnp.bfloat16),
            jax.ShapeDtypeStruct((tiles, groups, 1, GROUP * tile), jnp.float32),
        ],
        compiler_params=pltpu.CompilerParams(vmem_limit_bytes=VMEM),
        cost_estimate=FREE,
        name="attend",
    )(span, query_pre, cosine, sine, low.reshape(tiles, 1, tile), window, window, *deps)


def attend_back(query_rot, grad_rows, attn_rows, log_total, cosine_t, sine_t, low, window, deps):
    tok_rows = query_rot.shape[0]
    key_count = window.shape[0] - tok_rows
    tile, chunk, base, span = attention_plan(tok_rows, key_count, low)
    tiles = tok_rows // tile
    groups = HEADS // GROUP
    wide = GROUP * HEAD
    block = pl.BlockSpec((tile, wide), lambda i, g, s: (i, g))
    angle = pl.BlockSpec((HEAD // 2, tile), lambda i, g, s: (0, i))
    return pl.pallas_call(
        lambda *refs: attend_back_kernel(*refs, base=base, chunk=chunk),
        grid_spec=pltpu.PrefetchScalarGridSpec(
            num_scalar_prefetch=1,
            grid=(tiles, groups),
            in_specs=[
                block,
                block,
                block,
                pl.BlockSpec((1, 1, 1, GROUP * tile), lambda i, g, s: (i, g, 0, 0)),
                angle,
                angle,
                pl.BlockSpec((1, 1, tile), lambda i, g, s: (i, 0, 0)),
                pl.BlockSpec((key_count, HEAD), lambda i, g, s: (0, 0)),
                pl.BlockSpec((key_count, HEAD), lambda i, g, s: (0, 1)),
            ]
            + [pl.BlockSpec(memory_space=pl.ANY)] * len(deps),
            out_specs=[
                block,
                pl.BlockSpec((wide, tile), lambda i, g, s: (g, i)),
                pl.BlockSpec((key_count, 2 * HEAD), lambda i, g, s: (0, 0)),
            ],
            scratch_shapes=[
                pltpu.VMEM((key_count, HEAD), jnp.float32),
                pltpu.VMEM((key_count, HEAD), jnp.float32),
                pltpu.VMEM((HEAD, GROUP * tile), jnp.float32),
                pltpu.VMEM((HEAD, key_count), jnp.bfloat16),
            ],
        ),
        out_shape=[
            jax.ShapeDtypeStruct(query_rot.shape, jnp.bfloat16),
            jax.ShapeDtypeStruct(query_rot.shape[::-1], jnp.bfloat16),
            jax.ShapeDtypeStruct((key_count, 2 * HEAD), jnp.bfloat16),
        ],
        compiler_params=pltpu.CompilerParams(vmem_limit_bytes=VMEM),
        cost_estimate=FREE,
        name="attend_back",
    )(
        span, query_rot, grad_rows, attn_rows, log_total, cosine_t, sine_t, low.reshape(tiles, 1, tile),
        window, window, *deps,
    )


def nt(left, right):
    return lax.dot_general(
        left, right, (((1,), (1,)), ((), ())), preferred_element_type=jnp.float32
    )


def tn(left, right):
    return lax.dot_general(
        left, right, (((0,), (0,)), ((), ())), preferred_element_type=jnp.float32
    )


def flat(ref):
    block = ref[...]
    return block.reshape(-1, block.shape[-1])


def units_kernel(core_ref, *refs):
    tokens, cots = refs[0:2], refs[2:4]
    gate_ref, up_ref, down_ref = refs[4:7]
    out_ref = refs[-1]
    gate_rows, up_rows, down_rows = flat(gate_ref), flat(up_ref), flat(down_ref)

    def one(token_ref, cot_ref):
        gate = nt(gate_rows, token_ref[...])
        up = nt(up_rows, token_ref[...])
        grad_mixed = nt(down_rows, cot_ref[...])
        root = (2.0 / jnp.pi) ** 0.5
        square = gate * gate
        curve = jnp.tanh(root * (gate + 0.044715 * (square * gate)))
        upper = 0.5 * (1.0 + curve)
        activated = gate * upper
        slope = upper + 0.5 * gate * (1.0 - curve * curve) * (root * (1.0 + 0.134145 * square))
        out_ref[0] = (grad_mixed * up * slope).astype(jnp.bfloat16)
        out_ref[1] = (grad_mixed * activated).astype(jnp.bfloat16)
        out_ref[2] = (activated * up).astype(jnp.bfloat16)

    for j in (0, 1):
        pl.when(pl.program_id(1) == j)(lambda j=j: one(tokens[j], cots[j]))


def units(tokens, cots, weights, core, group, held, deps=()):
    cols, width = tokens[0].shape
    hidden = weights.hidden
    token_block = pl.BlockSpec((cols, width), lambda i, j, s: (0, 0))
    extra = (() if held is None else (held,)) + tuple(deps)
    return pl.pallas_call(
        units_kernel,
        grid_spec=pltpu.PrefetchScalarGridSpec(
            num_scalar_prefetch=1,
            grid=(2, 2),
            in_specs=[token_block] * 4
            + weights.specs(2, lambda i, j, s: (i, 0), width)
            + [pl.BlockSpec(memory_space=pl.ANY)] * len(extra),
            out_specs=pl.BlockSpec(
                (3, hidden // 2, cols), lambda i, j, s: (0, i, 2 * group + j)
            ),
        ),
        out_shape=jax.ShapeDtypeStruct((3, hidden, 4 * cols), jnp.bfloat16),
        input_output_aliases={} if held is None else {8: 0},
        compiler_params=pltpu.CompilerParams(vmem_limit_bytes=VMEM),
        cost_estimate=FREE,
        name="units",
    )(core, *tokens, *cots, *weights.arrays, *extra)


class OwnWeights:
    def __init__(self, shards):
        self.arrays = tuple(shards)
        self.hidden = shards[0].shape[0] // 2

    def specs(self, cuts, place, width):
        def index(*grid):
            row, col = place(*grid)
            return (grid[-1][0] * cuts + row, col)

        return [pl.BlockSpec((self.hidden // cuts, width), index)] * len(self.arrays)


class FarWeights:
    def __init__(self, gathered):
        parts, count, rows, width = gathered.shape
        self.hidden = parts * rows
        if rows % 16:
            gathered = gathered.reshape(2, parts // 2, count, rows, width)
            gathered = gathered.transpose(0, 2, 1, 3, 4).reshape(2, count, -1, width)
        self.arrays = (gathered,) * count

    def specs(self, cuts, place, width):
        parts, count, rows, _ = self.arrays[0].shape

        def spec(which):
            def index(*grid):
                row, col = place(*grid)
                return (row, which, 0, col)

            return pl.BlockSpec((parts // cuts, 1, rows, width), index)

        return [spec(which) for which in range(count)]


def sums_kernel(core_ref, *refs, count):
    total = 0.0
    for act_ref, weight_ref in zip(refs[:count], refs[count : 2 * count], strict=True):
        total = total + tn(act_ref[0], flat(weight_ref))
    refs[-1][...] = total.astype(jnp.bfloat16)


def sums(acts, weights, core, group, which, block=None, deps=()):
    all_tokens = acts[0].shape[2]
    width = weights[0].arrays[0].shape[-1]
    rows = all_tokens // 4
    blocks = 2 if block is None else 1
    cols = 512 if width % 512 == 0 else width // 2
    first = 2 * group + (block or 0)

    def act_spec(act, kind):
        return pl.BlockSpec((1, act.shape[1], rows), lambda n, t, s: (kind, 0, first + t))

    act_specs, weight_specs, act_args, weight_args = [], [], [], []
    for act, weight in zip(acts, weights, strict=True):
        specs = weight.specs(1, lambda n, t, s: (0, n), cols)
        for kind in which:
            act_specs.append(act_spec(act, kind))
            act_args.append(act)
            weight_specs.append(specs[kind])
            weight_args.append(weight.arrays[kind])
    return pl.pallas_call(
        lambda *refs: sums_kernel(*refs, count=len(act_args)),
        grid_spec=pltpu.PrefetchScalarGridSpec(
            num_scalar_prefetch=1,
            grid=(width // cols, blocks),
            in_specs=act_specs + weight_specs + [pl.BlockSpec(memory_space=pl.ANY)] * len(deps),
            out_specs=pl.BlockSpec((rows, cols), lambda n, t, s: (t, n)),
        ),
        out_shape=jax.ShapeDtypeStruct((blocks * rows, width), jnp.bfloat16),
        compiler_params=pltpu.CompilerParams(vmem_limit_bytes=VMEM),
        cost_estimate=FREE,
        name="sums",
    )(core, *act_args, *weight_args, *deps)


def grams_kernel(acts_ref, *refs, sets):
    out_ref = refs[-1]

    def one(rights):
        step = rights[0].shape[0]
        total = 0.0
        for i, right_ref in enumerate(rights):
            total = total + jnp.dot(
                acts_ref[0, :, i * step : (i + 1) * step], right_ref[...],
                preferred_element_type=jnp.float32,
            )
        out_ref[0] = total.astype(jnp.bfloat16)

    if sets == 1:
        one(refs[0:4])
    else:
        pl.when(pl.program_id(0) < 2)(lambda: one(refs[0:4]))
        pl.when(pl.program_id(0) == 2)(lambda: one(refs[4:8]))


def grams(acts, tokens, cots, pairs, kinds, deps=()):
    _, hidden, all_tokens = acts.shape
    step, width = tokens[0].shape
    cols = width // pairs
    first, count = kinds[0], len(kinds)
    if cols % 128:
        parts = []
        for kind in kinds:
            whole = sum(
                product(acts[kind, :, i * step : (i + 1) * step], right)
                for i, right in enumerate(cots if kind == 2 else tokens)
            )
            parts.append(whole.astype(jnp.bfloat16))
        return jnp.concatenate(parts, 0).reshape(count * hidden, pairs, cols).transpose(1, 0, 2)
    if count == 3:
        specs = [pl.BlockSpec((step, cols), lambda k, p: (0, jnp.where(k < 2, p, pairs - 1)))] * 4
        specs = specs + [pl.BlockSpec((step, cols), lambda k, p: (0, jnp.where(k < 2, 0, p)))] * 4
        rights = tuple(tokens) + tuple(cots)
    else:
        specs = [pl.BlockSpec((step, cols), lambda k, p: (0, p))] * 4
        rights = tuple(cots) if first == 2 else tuple(tokens)
    return pl.pallas_call(
        lambda *refs: grams_kernel(*refs, sets=len(rights) // 4),
        grid=(count, pairs),
        in_specs=[pl.BlockSpec((1, hidden, all_tokens), lambda k, p: (first + k, 0, 0))]
        + specs
        + [pl.BlockSpec(memory_space=pl.ANY)] * len(deps),
        out_specs=pl.BlockSpec((1, hidden, cols), lambda k, p: (p, k, 0)),
        out_shape=jax.ShapeDtypeStruct((pairs, count * hidden, cols), jnp.bfloat16),
        compiler_params=pltpu.CompilerParams(vmem_limit_bytes=VMEM),
        cost_estimate=FREE,
        name="grams",
    )(acts, *rights, *deps)


class Gathered:
    def __init__(self, own, others, shard):
        count, _, rows, width = others.shape
        if rows % 16:
            others = others.transpose(1, 0, 2, 3).reshape(1, -1, count * rows, width)
        self.own, self.others = own, others
        self.shard = shard.reshape(1).astype(jnp.int32)
        self.shards = others.shape[1] + 1

    def place(self, step, shard_ref):
        return lax.rem(shard_ref[0] + self.shards - step, self.shards)

    def specs(self):
        count, _, rows, width = self.others.shape
        return [
            pl.BlockSpec(self.own.shape, lambda r, s: (0, 0)),
            pl.BlockSpec((count, 1, rows, width), lambda r, s: (0, jnp.maximum(r - 1, 0), 0, 0)),
        ]


def by_shard(own_ref, others_ref, use):
    pl.when(pl.program_id(0) == 0)(lambda: use(own_ref[...]))
    pl.when(pl.program_id(0) > 0)(lambda: use(flat(others_ref)))


def spread_kernel(shard_ref, left_ref, own_ref, others_ref, *refs):
    out_ref = refs[-1]

    def use(weight):
        out_ref[...] = nt(left_ref[...], weight).astype(out_ref.dtype)

    by_shard(own_ref, others_ref, use)


def spread(left, weight, dtype, deps=()):
    tokens, width = left.shape
    rows = weight.own.shape[0]
    return pl.pallas_call(
        spread_kernel,
        grid_spec=pltpu.PrefetchScalarGridSpec(
            num_scalar_prefetch=1,
            grid=(weight.shards,),
            in_specs=[pl.BlockSpec((tokens, width), lambda r, s: (0, 0))]
            + weight.specs()
            + [pl.BlockSpec(memory_space=pl.ANY)] * len(deps),
            out_specs=pl.BlockSpec((tokens, rows), lambda r, s: (0, weight.place(r, s))),
        ),
        out_shape=jax.ShapeDtypeStruct((tokens, weight.shards * rows), dtype),
        compiler_params=pltpu.CompilerParams(vmem_limit_bytes=VMEM),
        cost_estimate=FREE,
        name="spread",
    )(weight.shard, left, weight.own, weight.others, *deps)


def collect_kernel(shard_ref, left_ref, own_ref, others_ref, start_ref, gain_ref, *refs, outs):
    refs = refs[-outs:]
    total_ref = refs[0]

    @pl.when(pl.program_id(0) == 0)
    def _():
        total_ref[...] = start_ref[...].astype(jnp.float32)

    def use(weight):
        total_ref[...] += jnp.dot(left_ref[...], weight, preferred_element_type=jnp.float32)

    by_shard(own_ref, others_ref, use)
    if outs > 1:

        @pl.when(pl.program_id(0) == pl.num_programs(0) - 1)
        def _():
            rows = min(128, total_ref.shape[0])

            def norm(i, carry):
                here = pl.ds(pl.multiple_of(i * rows, rows), rows)
                total = total_ref[here, :]
                scale = norm_scale(total)
                refs[1][here, :] = (total * scale * gain_ref[...]).astype(jnp.bfloat16)
                refs[2][here, :] = jnp.broadcast_to(scale, (rows, 128))
                return carry

            lax.fori_loop(0, total_ref.shape[0] // rows, norm, 0)


def collect(left, weight, start, gain=None, deps=()):
    tokens = left.shape[0]
    rows, width = weight.own.shape
    whole = pl.BlockSpec((tokens, width), lambda r, s: (0, 0))
    shapes, specs = [jax.ShapeDtypeStruct((tokens, width), jnp.float32)], [whole]
    if gain is not None:
        shapes.append(jax.ShapeDtypeStruct((tokens, width), jnp.bfloat16))
        shapes.append(jax.ShapeDtypeStruct((tokens, 128), jnp.float32))
        specs.extend([whole, pl.BlockSpec((tokens, 128), lambda r, s: (0, 0))])
    gain_row = jnp.zeros((1, width), jnp.float32) if gain is None else gain.reshape(1, width)
    return pl.pallas_call(
        lambda *refs: collect_kernel(*refs, outs=len(specs)),
        grid_spec=pltpu.PrefetchScalarGridSpec(
            num_scalar_prefetch=1,
            grid=(weight.shards,),
            in_specs=[pl.BlockSpec((tokens, rows), lambda r, s: (0, weight.place(r, s)))]
            + weight.specs()
            + [whole, pl.BlockSpec((1, width), lambda r, s: (0, 0))]
            + [pl.BlockSpec(memory_space=pl.ANY)] * len(deps),
            out_specs=specs,
        ),
        out_shape=shapes,
        compiler_params=pltpu.CompilerParams(vmem_limit_bytes=VMEM),
        cost_estimate=FREE,
        name="collect",
    )(weight.shard, left, weight.own, weight.others, start, gain_row, *deps)


def cross_kernel(core_ref, *refs, lefts, gained, added):
    right_ref, out_ref = refs[lefts], refs[-1]
    first = 0

    def put(part, rows):
        here = (0, slice(None), slice(first, first + rows))
        if added:
            part = part + refs[lefts + 1 + gained][here].astype(jnp.float32)
        out_ref[here] = part.astype(jnp.bfloat16)

    for left_ref in refs[:lefts]:
        shards, _, rows, tokens = left_ref.shape
        left = left_ref[...].reshape(shards * rows, tokens)
        part = jnp.dot(left, right_ref[...], preferred_element_type=jnp.float32)
        put(part.reshape(shards, rows, -1), rows)
        first = first + rows
    if gained:
        gains = refs[lefts + 1][...].astype(jnp.float32)
        put(jnp.broadcast_to(gains[None], (out_ref.shape[1],) + gains.shape), gains.shape[0])


def cross(lefts, right, core, shards, pairs, gains=None, add=None, deps=(), first=0, of=None, into=None):
    tokens, width = right.shape
    cols = width // pairs
    views = [left.reshape(shards, 2, -1, tokens) for left in lefts]
    rows = [view.shape[2] for view in views]
    total = sum(rows) + (0 if gains is None else gains.shape[0])
    if cols % 128:
        picked = jnp.concatenate(
            [lax.dynamic_index_in_dim(view, core[0], 1, keepdims=False) for view in views], 1
        )
        whole = product(picked.reshape(-1, tokens), right).reshape(shards, sum(rows), width)
        if gains is not None:
            extra = jnp.broadcast_to(gains.astype(jnp.float32)[None], (shards,) + gains.shape)
            whole = jnp.concatenate([whole, extra], 1)
        whole = whole.reshape(shards, total, pairs, cols).transpose(2, 0, 1, 3)
        if add is not None:
            whole = whole + add[:, :, first : first + total].astype(jnp.float32)
        whole = whole.astype(jnp.bfloat16)
        if of is None:
            return whole
        if into is None:
            into = jnp.zeros((pairs, shards, of, cols), jnp.bfloat16)
        return lax.dynamic_update_slice(into, whole, (0, 0, first, 0))
    block = pl.BlockSpec((1, shards, total, cols), lambda p, s: (p, 0, first // total, 0))
    kept = () if into is None else (into,)
    specs = [
        pl.BlockSpec((shards, 1, count, tokens), lambda p, s: (0, s[0], 0, 0)) for count in rows
    ]
    specs.append(pl.BlockSpec((tokens, cols), lambda p, s: (0, p)))
    args = [*views, right]
    if gains is not None:
        specs.append(pl.BlockSpec((gains.shape[0], cols), lambda p, s: (0, p)))
        args.append(gains)
    if add is not None:
        specs.append(block)
        args.append(add)
    return pl.pallas_call(
        lambda *refs: cross_kernel(
            *refs, lefts=len(views), gained=gains is not None, added=add is not None
        ),
        grid_spec=pltpu.PrefetchScalarGridSpec(
            num_scalar_prefetch=1,
            grid=(pairs,),
            in_specs=specs + [pl.BlockSpec(memory_space=pl.ANY)] * (len(kept) + len(deps)),
            out_specs=block,
        ),
        out_shape=jax.ShapeDtypeStruct((pairs, shards, of or total, cols), jnp.bfloat16),
        input_output_aliases={1 + len(args): 0} if kept else {},
        compiler_params=pltpu.CompilerParams(vmem_limit_bytes=VMEM),
        cost_estimate=FREE,
        name="cross",
    )(core, *args, *kept, *deps)


def swap(value, axis, bit):
    return lax.ppermute(value, axis, [(i, i ^ bit) for i in range(lax.axis_size(axis))])


def after(value, *others):
    return lax.optimization_barrier((value, *others))[0]


def same_core():
    count = lax.axis_size("ctx")
    return [list(range(0, count, 2)), list(range(1, count, 2))]


def own_part(shard, place):
    part = shard.shape[0] // lax.axis_size("ctx")
    return lax.dynamic_slice_in_dim(shard, place * part, part, 0)


def together(*values):
    return lax.optimization_barrier(values)


def halving_scatter(blocks, axis, place):
    held, bit = blocks, 1
    while held.shape[0] > 1:
        both = held.reshape((held.shape[0] // 2, 2) + held.shape[1:])
        mine = (place // bit) % 2
        keep = lax.dynamic_index_in_dim(both, mine, 1, keepdims=False)
        give = lax.dynamic_index_in_dim(both, 1 - mine, 1, keepdims=False)
        total = keep.astype(jnp.float32) + swap(give, axis, bit).astype(jnp.float32)
        held = total.astype(jnp.bfloat16)
        bit = 2 * bit
    return total[0]


def step_ring(value, axis):
    count = lax.axis_size(axis)
    return lax.ppermute(value, axis, [(i, (i + 1) % count) for i in range(count)])


def ring(value, axis):
    arrived = []
    for _ in range(lax.axis_size(axis) - 1):
        value = step_ring(value, axis)
        arrived.append(value)
    return arrived


def exchanges(axis):
    bits, bit = [], 2
    while bit < lax.axis_size(axis):
        bits.append(bit)
        bit = 2 * bit
    return bits + [1]


def pairs_gather(value):
    pairs = lax.axis_size("ctx") // 2
    if pairs == 4:
        half = value.shape[0] // 2
        x_all, y_all = swap(value, "ctx", 2), swap(value, "ctx", 4)
        low = swap(y_all[:half], "ctx", 2)
        high = swap(x_all[half:], "ctx", 4)
        return [(0, [value]), (2, [x_all]), (4, [y_all]), (6, [low, high])]
    held, bit = [(0, value)], 2
    while bit < 2 * pairs:
        held = held + [(bits ^ bit, swap(item, "ctx", bit)) for bits, item in held]
        bit = 2 * bit
    return [(bits, [item]) for bits, item in held]


def window_gather(value, reach, place):
    rows = value.shape[0]
    out = jnp.zeros(((reach + 2) * rows,) + value.shape[1:], value.dtype)
    parts = [(bits, part, i) for bits, held in pairs_gather(value) for i, part in enumerate(held)]
    for bits, part, i in parts:
        both = ((bits, part), (bits ^ 1, swap(part, "ctx", 1)))
        for other, block in both:
            spot = (place ^ other) - place + reach
            spot = jnp.where((spot < 0) | (spot > reach), reach + 1, spot)
            start = spot * rows + (i * block.shape[0])
            out = lax.dynamic_update_slice_in_dim(out, block, start, 0)
    return out


def place_block(out, block, place):
    return lax.dynamic_update_index_in_dim(out, block, place, 0)


def in_places(own, arrived, place):
    count = len(arrived) + 1
    out = jnp.zeros((count,) + own.shape, own.dtype)
    for step, value in enumerate([own, *arrived]):
        out = lax.dynamic_update_index_in_dim(out, value, lax.rem(place + count - step, count), 0)
    return out


def in_order(gathered, first, part):
    mine = gathered[:, :, first : first + part].transpose(1, 0, 2, 3)
    return mine.reshape(-1, gathered.shape[-1])


def body(
    inputs,
    norm_gains,
    q_weight,
    kv_weight,
    o_weight,
    gate_weight,
    up_weight,
    down_weight,
    cotangent,
    doc_lengths,
):
    x_rows = inputs[0].astype(jnp.float32)
    grad_out = cotangent[0]
    tok_rows, width = x_rows.shape
    place = lax.axis_index("ctx")
    ctx_count = lax.axis_size("ctx")
    pairs = ctx_count // 2
    core = place % 2
    pair = place // 2
    own_core = core.reshape(1).astype(jnp.int32)
    shard = lax.axis_index("fsdp")
    shards = lax.axis_size("fsdp")
    reach = min(ctx_count - 1, (WINDOW + tok_rows - 2) // tok_rows)
    key_count = (reach + 1) * tok_rows
    first_token = place * tok_rows
    token_ids, segment, positions = doc_info(doc_lengths[0], first_token, tok_rows)
    low = jnp.maximum(token_ids - positions, token_ids - (WINDOW - 1)) - (
        first_token - reach * tok_rows
    )
    cosine, sine = rope_angles(positions)
    gain_attn = norm_gains[0]
    gain_mlp = norm_gains[1]

    q_part, kv_part, o_part = (own_part(w, place) for w in (q_weight, kv_weight, o_weight))
    kv_z = in_places(kv_part, ring(kv_part, "fsdp"), shard)
    moving = after(q_part, kv_z)
    held, origins = kv_z[None], [place]
    q_arrived = []
    for bit in exchanges("ctx"):
        if len(q_arrived) < shards - 1:
            moving = step_ring(moving, "fsdp")
            q_arrived.append(moving)
        held = jnp.concatenate([held, swap(held, "ctx", bit)], 0)
        origins = origins + [origin ^ bit for origin in origins]
        held, moving = together(held, moving)
    while len(q_arrived) < shards - 1:
        moving = step_ring(moving, "fsdp")
        q_arrived.append(moving)
    kv_all = jnp.zeros_like(held)
    for step, origin in enumerate(origins):
        kv_all = place_block(kv_all, held[step], origin)
    q_ring = jnp.stack(q_arrived, 0)
    q_ring, kv_all = together(q_ring, kv_all)
    q_all = lax.all_gather(q_ring, "ctx", axis=0)

    half_rows = gate_weight.shape[0] // 2
    part_rows = half_rows // pairs
    cut = (part_rows * 7 // 15 + 15) // 16 * 16
    far_rows, last_rows = cut // 4, part_rows - cut
    mine = jnp.stack(
        [
            lax.dynamic_slice_in_dim(w, core * half_rows + pair * part_rows, part_rows, 0)
            for w in (gate_weight, up_weight, down_weight)
        ],
        0,
    )
    mine, _ = together(mine, q_ring)
    own_weights = OwnWeights((gate_weight, up_weight, down_weight))

    scale_one = norm_scale(x_rows)
    normed_one = (x_rows * scale_one * gain_attn).astype(jnp.bfloat16)
    kv_full = in_order(kv_all, 0, kv_part.shape[0])
    kv_pre = times_rows(normed_one, kv_full)
    key_rot = rotate(kv_pre[:, :HEAD], cosine, sine).astype(jnp.bfloat16)
    kv_local = jnp.concatenate([key_rot, kv_pre[:, HEAD:].astype(jnp.bfloat16)], 1)
    kv_local, moving = together(kv_local, o_part)
    kv_window = window_gather(kv_local, reach, place)
    o_arrived = ring(moving, "fsdp")
    cot_rows = tok_rows // 8
    cot_first = swap(after(grad_out[:cot_rows], o_arrived[-1]), "fsdp", 1)
    far_first = swap(after(mine[:, :far_rows], o_arrived[-1]), "fsdp", 2)
    o_ring = jnp.stack(o_arrived, 0)
    q_all, o_ring, far_first, cot_first, kv_window, normed_one, cosine_t, sine_t = together(
        q_all, o_ring, far_first, cot_first, kv_window, normed_one, cosine.T, sine.T
    )
    o_all = lax.all_gather(o_ring, "ctx", axis=0)
    q_full = Gathered(q_weight, q_all, shard)
    o_full = Gathered(o_weight, o_all, shard)
    far_second = swap(after(mine[:, far_rows : part_rows - last_rows], o_ring), "fsdp", 2)
    cot_second = swap(after(grad_out[cot_rows:], o_ring), "fsdp", 1)
    query_pre = spread(normed_one, q_full, jnp.float32)
    attn_rows, attn_rows_t, query_rot, log_total = attend(
        query_pre, cosine, sine, low, kv_window
    )
    far_last = mine[:, part_rows - last_rows :]
    log_total, cot_second, far_second, far_last = together(
        log_total, cot_second, far_second, far_last
    )
    far_third = swap(far_last, "fsdp", 2)
    near_cots = (grad_out, swap(grad_out, "ctx", 1))
    cot_across = jnp.concatenate([cot_first, cot_second], 0)
    cots = [near_cots, (cot_across, swap(cot_across, "ctx", 1))]

    def over_plane(part):
        return lax.all_gather(part, "ctx", axis=0, axis_index_groups=same_core())

    far_a = FarWeights(
        over_plane(jnp.concatenate([far_first, far_second], 1))
    )
    hidden_one, normed_two, scale_two = collect(attn_rows, o_full, inputs[0], gain_mlp)
    scale_two = scale_two[:, :1]

    near = (normed_two, swap(normed_two, "ctx", 1))
    across = swap(normed_two, "fsdp", 1)
    own_acts = units(near, near_cots, own_weights, own_core, 0, None)
    a_acts = units(near, near_cots, far_a, own_core, 0, None, (own_acts, cots[1][1]))
    across, a_acts, far_third = together(across, a_acts, far_third)
    far = (across, swap(across, "ctx", 1))
    far_b = FarWeights(over_plane(far_third))
    own_acts = units(far, cots[1], own_weights, own_core, 1, own_acts, (a_acts,))
    a_acts = units(far, cots[1], far_a, own_core, 1, a_acts, (own_acts,))
    near_far, cot_rows = near + far, cots[0] + cots[1]

    def over_pairs(blocks):
        mine = lax.psum_scatter(
            blocks, "ctx", scatter_dimension=0, tiled=False, axis_index_groups=same_core()
        )
        return lax.optimization_barrier(mine)

    a_grams = grams(a_acts, near_far, cot_rows, pairs, (0, 1, 2))
    b_acts = units(near, cots[0], far_b, own_core, 0, None, (a_grams,))
    b_acts = units(far, cots[1], far_b, own_core, 1, b_acts)
    b_grams = grams(b_acts, near_far, cot_rows, pairs, (0, 1, 2))
    a_sums, b_sums = over_pairs(a_grams), over_pairs(b_grams)
    acts, weights = (own_acts, a_acts, b_acts), (own_weights, far_a, far_b)

    def group_sums(group, which, block, deps):
        return sums(acts, weights, own_core, group, which, block, deps)

    own_gate_up = grams(own_acts, near_far, cot_rows, pairs, (0, 1), (b_grams,))
    give = group_sums(1, (0, 1), 1, (own_gate_up,))
    own_gate_up = over_pairs(own_gate_up)
    got = swap(give, "ctx", 1)
    near_give = group_sums(0, (0, 1), 1, (give,))
    near_got = swap(near_give, "ctx", 1)
    keep = group_sums(1, (0, 1), 0, (near_give, a_sums))
    total = add16(keep, got)
    moved = swap(total, "fsdp", 1)
    own_down = grams(own_acts, near_far, cot_rows, pairs, (2,), (total, near_got))
    near_keep = group_sums(0, (0, 1), 0, (own_down,))
    out_give = group_sums(1, (2,), 1, (near_keep,))
    out_got = swap(out_give, "ctx", 1)
    out_keep = group_sums(1, (2,), 0, (out_give,))
    moved, own_down, near_keep, out_keep, a_sums = together(
        moved, own_down, near_keep, out_keep, a_sums
    )
    own_down = over_pairs(own_down)
    grad_normed_two = (
        near_keep.astype(jnp.float32) + near_got.astype(jnp.float32) + moved.astype(jnp.float32)
    )
    grad_hidden = grad_out.astype(jnp.float32) + norm_back(
        grad_normed_two, hidden_one, scale_two, gain_mlp
    )
    gain_mlp_grad = jnp.sum(grad_normed_two * hidden_one * scale_two, 0)
    grad_branch = grad_hidden.astype(jnp.bfloat16)
    grad_attended = spread(grad_branch, o_full, jnp.bfloat16, (b_sums,))

    gate_rows = b_sums.shape[0] // 3
    a_all = swap(a_sums, "fsdp", 2)
    grad_query_pre, grad_query_pre_t, grad_kv = attend_back(
        query_rot, grad_attended, attn_rows, log_total, cosine_t, sine_t, low, kv_window,
        (out_keep,),
    )
    grad_stack = grad_kv.reshape(reach + 1, tok_rows, 2 * HEAD)
    moved_kv = [shifted(grad_stack[reach - hop], "ctx", -hop) for hop in range(1, reach + 1)]
    out_moved = swap(add16(out_keep, out_got), "fsdp", 1)
    q_give = cross(
        [grad_query_pre_t], normed_one, 1 - own_core, shards, pairs,
        deps=(grad_kv, a_all, own_gate_up, out_moved),
    )
    q_got = swap(q_give, "ctx", 1)
    q_half, kv_half = q_weight.shape[0] // 2, kv_weight.shape[0] // 2
    okv_rows = q_half + kv_half + 16
    okv_give = cross(
        [attn_rows_t], grad_branch, 1 - own_core, shards, pairs, deps=(q_give,), of=okv_rows
    )
    q_sums = cross(
        [grad_query_pre_t], normed_one, own_core, shards, pairs, None, q_got, (okv_give,)
    )
    moved_kv, q_sums, b_sums = together(moved_kv, q_sums, b_sums)
    b_gate = swap(b_sums[:gate_rows], "fsdp", 2)
    b_up = swap(after(b_sums[gate_rows : 2 * gate_rows], b_gate), "fsdp", 2)
    b_down = swap(after(b_sums[2 * gate_rows :], b_up), "fsdp", 2)
    q_pairs = over_pairs(q_sums)
    own_kv_grad = grad_stack[reach].astype(jnp.float32)
    for block in moved_kv:
        own_kv_grad = own_kv_grad + block.astype(jnp.float32)
    grad_kv_pre = jnp.concatenate(
        [rotate_back(own_kv_grad[:, :HEAD], cosine, sine), own_kv_grad[:, HEAD:]], 1
    ).astype(jnp.bfloat16)
    (grad_normed_one,) = collect(
        grad_query_pre, q_full, product(grad_kv_pre, kv_full)
    )
    gain_attn_grad = jnp.sum(grad_normed_one * x_rows * scale_one, 0)
    gains = jnp.stack([gain_attn_grad, gain_mlp_grad], 0).astype(jnp.bfloat16)
    gains = jnp.concatenate([gains, jnp.zeros((14, width), jnp.bfloat16)], 0)
    kv_left = [grad_kv_pre.T]
    okv_give = cross(
        kv_left, normed_one, 1 - own_core, shards, pairs, gains, None, (b_gate,), q_half,
        okv_rows, okv_give,
    )
    okv_got = swap(okv_give, "ctx", 1)
    near_out = sums(acts, weights, own_core, 0, (2,), None, (okv_give,))
    near_out_got = swap(near_out[tok_rows:], "ctx", 1)
    okv_sums = cross(
        [attn_rows_t], grad_branch, own_core, shards, pairs, None, okv_got, (near_out, b_up),
        of=okv_rows,
    )
    okv_sums = cross(
        kv_left, normed_one, own_core, shards, pairs, gains, okv_got, (own_down, q_pairs), q_half, okv_rows,
        okv_sums,
    )
    grad_inputs = grad_hidden + norm_back(grad_normed_one, x_rows, scale_one, gain_attn)

    out_cols = width // ctx_count

    def both_halves(mine):
        keep = lax.dynamic_slice_in_dim(mine, core * out_cols, out_cols, 1)
        give = lax.dynamic_slice_in_dim(mine, (1 - core) * out_cols, out_cols, 1)
        got = swap(give.astype(jnp.bfloat16), "ctx", 1).astype(jnp.float32)
        lower = jnp.where(core == 0, keep, got)
        upper = jnp.where(core == 0, got, keep)
        return jnp.concatenate([lower, upper], 0)

    okv_pairs = over_pairs(okv_sums)
    q_mine = halving_scatter(q_pairs, "fsdp", shard)
    result = hidden_one + (
        near_out[:tok_rows].astype(jnp.float32)
        + near_out_got.astype(jnp.float32)
        + out_moved.astype(jnp.float32)
    )
    q_grad = both_halves(q_mine)
    okv_mine = halving_scatter(okv_pairs, "fsdp", shard)
    o_grad = both_halves(okv_mine[:q_half])
    kv_grad = both_halves(okv_mine[q_half : q_half + kv_half])
    gain_total = lax.dynamic_slice_in_dim(
        okv_mine[q_half + kv_half : q_half + kv_half + 2], core * out_cols, out_cols, 1
    )

    a_all = a_all.reshape(3, pairs, cut, -1)
    b_all = jnp.concatenate([b_gate, b_up, b_down], 0).reshape(3, pairs, part_rows - cut, -1)
    own_all = (own_gate_up[:half_rows], own_gate_up[half_rows:], own_down)
    mlp_grads = []
    for kind in range(3):
        others = jnp.concatenate([a_all[kind], b_all[kind]], 1).reshape(half_rows, -1)
        mlp_grads.append(
            both_halves(own_all[kind].astype(jnp.float32) + others.astype(jnp.float32))
        )

    return (
        result.astype(jnp.bfloat16)[None],
        grad_inputs.astype(jnp.bfloat16)[None],
        gain_total,
        q_grad,
        kv_grad,
        o_grad,
        mlp_grads[0],
        mlp_grads[1],
        mlp_grads[2],
    )


def solution(mesh):
    in_specs = (
        P("fsdp", "ctx", None),
        P(),
        P("fsdp", None),
        P("fsdp", None),
        P("fsdp", None),
        P("fsdp", None),
        P("fsdp", None),
        P("fsdp", None),
        P("fsdp", "ctx", None),
        P("fsdp", None),
    )
    out_specs = (
        P("fsdp", "ctx", None),
        P("fsdp", "ctx", None),
        P(None, "ctx"),
        P("fsdp", "ctx"),
        P("fsdp", "ctx"),
        P("fsdp", "ctx"),
        P("fsdp", "ctx"),
        P("fsdp", "ctx"),
        P("fsdp", "ctx"),
    )
    return jax.shard_map(body, mesh=mesh, in_specs=in_specs, out_specs=out_specs, check_vma=False)
```

```python
import jax
import jax.numpy as jnp
from jax import lax
from jax.experimental import pallas as pl
from jax.experimental.pallas import tpu as pltpu
from jax.sharding import PartitionSpec as P

HEADS = 10
HEAD = 256
WINDOW = 2048


EPSILON = 1e-06
MASKED = -1e30
LOWEST = -1e29
VMEM = 56 * 1024 * 1024
FREE = pl.CostEstimate(flops=0, bytes_accessed=0, transcendentals=0)


def shifted(value, axis, steps):
    count = lax.axis_size(axis)
    initial, last = (max(0, -steps), min(count, count - steps))
    return lax.ppermute(value, axis, [(source, source + steps) for source in range(initial, last)])


def swap(value, axis, bit):
    return lax.ppermute(value, axis, [(i, i ^ bit) for i in range(lax.axis_size(axis))])


def add16(left, right):
    return (left.astype(jnp.float32) + right.astype(jnp.float32)).astype(jnp.bfloat16)


def times_rows(left, right):
    return lax.dot_general(
        left, right, (((1,), (1,)), ((), ())), preferred_element_type=jnp.float32
    )


def gram_rows(left, right):
    return lax.dot_general(
        left, right, (((0,), (0,)), ((), ())), preferred_element_type=jnp.float32
    )


def product(left, right):
    return jnp.dot(left, right, preferred_element_type=jnp.float32)


def doc_info(doc_lengths, first_token, token_count):
    doc_ends = jnp.cumsum(doc_lengths)
    doc_starts = doc_ends - doc_lengths
    token_ids = first_token + jnp.arange(token_count, dtype=jnp.int32)
    segment = jnp.sum((doc_ends[None, :] <= token_ids[:, None]).astype(jnp.int32), 1)
    begins = jnp.max(
        jnp.where(doc_starts[None, :] <= token_ids[:, None], doc_starts[None, :], 0), 1
    )
    return (token_ids, segment, token_ids - begins)


def rope_angles(positions):
    half_width = HEAD // 2
    column = jnp.arange(half_width, dtype=jnp.float32)
    inverse = jnp.power(10000.0, -column / half_width)
    angles = positions.astype(jnp.float32)[:, None] * inverse[None, :]
    return (jnp.cos(angles), jnp.sin(angles))


def rotate(values, cosine, sine):
    half_width = values.shape[-1] // 2
    first_half = values[..., :half_width]
    second_half = values[..., half_width:]
    return jnp.concatenate(
        [first_half * cosine - second_half * sine, second_half * cosine + first_half * sine], -1
    )


def rotate_back(grad_in, cosine, sine):
    half_width = grad_in.shape[-1] // 2
    first_half = grad_in[..., :half_width]
    second_half = grad_in[..., half_width:]
    return jnp.concatenate(
        [first_half * cosine + second_half * sine, second_half * cosine - first_half * sine], -1
    )


def norm_scale(values):
    return lax.rsqrt(jnp.mean(values * values, -1, keepdims=True) + EPSILON)


def norm_back(grad_in, values, scale, gain):
    weighted = grad_in * gain
    return scale * weighted - values * scale * scale * scale * jnp.mean(
        weighted * values, -1, keepdims=True
    )


def head_rows(block, count):
    return jnp.concatenate([block[:, h * HEAD : (h + 1) * HEAD] for h in range(count)], 0)


def row_bounds(low_ref, first_key, tokens, count):
    high = first_key + lax.broadcasted_iota(jnp.int32, (1, tokens), 1)
    low = low_ref[0]
    return jnp.concatenate([low] * count, 1), jnp.concatenate([high] * count, 1)


def seen(start, shape, low, high):
    key = start + lax.broadcasted_iota(jnp.int32, shape, 0)
    return (key >= low) & (key <= high)


def turn(from_ref, to_ref, chunk):
    def step(j, carry):
        here = pl.ds(pl.multiple_of(j * chunk, chunk), chunk)
        to_ref[:, here] = from_ref[here, :].astype(jnp.float32).T.astype(jnp.bfloat16)
        return carry

    lax.fori_loop(0, from_ref.shape[0] // chunk, step, 0)


def attend_kernel(
    span_ref, pre_ref, cos_ref, sin_ref, low_ref, key_ref, value_ref, *refs, base, chunk
):
    out_ref, out_t_ref, rot_ref, log_ref, acc, value_t_ref = refs[-6:]

    @pl.when((pl.program_id(0) == 0) & (pl.program_id(1) == 0))
    def _():
        turn(value_ref, value_t_ref, chunk)

    tile = pl.program_id(0)
    tokens = pre_ref.shape[0]
    count = pre_ref.shape[1] // HEAD
    cosine, sine = cos_ref[...], sin_ref[...]
    half = HEAD // 2
    for h in range(count):
        first = pre_ref[:, h * HEAD : h * HEAD + half]
        second = pre_ref[:, h * HEAD + half : (h + 1) * HEAD]
        rot_ref[:, h * HEAD : h * HEAD + half] = (
            (first * cosine - second * sine) * HEAD ** (-0.5)
        ).astype(jnp.bfloat16)
        rot_ref[:, h * HEAD + half : (h + 1) * HEAD] = (
            (second * cosine + first * sine) * HEAD ** (-0.5)
        ).astype(jnp.bfloat16)
    query = head_rows(rot_ref[...], count)
    low, high = row_bounds(low_ref, base + tile * tokens, tokens, count)
    rows = count * tokens

    acc[...] = jnp.zeros_like(acc)

    def step(j, carry):
        top, total = carry
        start = pl.multiple_of(j * chunk, chunk)
        scores = lax.dot_general(
            key_ref[pl.ds(start, chunk), :], query, (((1,), (1,)), ((), ())),
            preferred_element_type=jnp.float32,
        )
        scores = jnp.where(seen(start, scores.shape, low, high), scores, MASKED)
        higher = jnp.maximum(top, jnp.max(scores, 0, keepdims=True))
        part = jnp.exp(scores - higher)
        shrink = jnp.exp(top - higher)
        acc[...] = acc[...] * shrink + lax.dot_general(
            value_t_ref[:, pl.ds(start, chunk)], part.astype(jnp.bfloat16), (((1,), (0,)), ((), ())),
            preferred_element_type=jnp.float32,
        )
        return higher, total * shrink + jnp.sum(part, 0, keepdims=True)

    top, total = lax.fori_loop(
        span_ref[0, tile], span_ref[1, tile], step,
        (jnp.full((1, rows), LOWEST, jnp.float32), jnp.zeros((1, rows), jnp.float32)),
    )
    log_ref[0, 0] = top + jnp.log(total)
    outs_t = acc[...] * (1.0 / total)
    outs = outs_t.T.astype(jnp.bfloat16)
    outs_t = outs_t.astype(jnp.bfloat16)
    for h in range(count):
        out_t_ref[h * HEAD : (h + 1) * HEAD, :] = outs_t[:, h * tokens : (h + 1) * tokens]
        out_ref[:, h * HEAD : (h + 1) * HEAD] = outs[h * tokens : (h + 1) * tokens]


def attend_back_kernel(
    span_ref, rot_ref, grad_ref, out_ref, log_ref, cos_ref, sin_ref, low_ref, key_ref, value_ref,
    *refs, base, chunk
):
    pre_ref, pre_t_ref, grad_kv_ref, grad_key_ref, grad_value_ref, acc, key_t_ref = refs[-7:]
    tile = pl.program_id(0)
    tokens = rot_ref.shape[0]
    count = rot_ref.shape[1] // HEAD

    @pl.when((tile == 0) & (pl.program_id(1) == 0))
    def _():
        turn(key_ref, key_t_ref, chunk)
        grad_key_ref[...] = jnp.zeros_like(grad_key_ref)
        grad_value_ref[...] = jnp.zeros_like(grad_value_ref)

    query = head_rows(rot_ref[...], count)
    grad = head_rows(grad_ref[...], count)
    outs = head_rows(out_ref[...], count)
    delta = jnp.sum((grad.astype(jnp.float32) * outs.astype(jnp.float32)).T, 0, keepdims=True)
    log_total = log_ref[0, 0]
    low, high = row_bounds(low_ref, base + tile * tokens, tokens, count)
    acc[...] = jnp.zeros_like(acc)

    def step(j, carry):
        start = pl.multiple_of(j * chunk, chunk)
        here = pl.ds(start, chunk)
        scores = lax.dot_general(
            key_ref[here, :], query, (((1,), (1,)), ((), ())), preferred_element_type=jnp.float32
        )
        grad_probs = lax.dot_general(
            value_ref[here, :], grad, (((1,), (1,)), ((), ())), preferred_element_type=jnp.float32
        )
        probs = jnp.where(seen(start, scores.shape, low, high), jnp.exp(scores - log_total), 0.0)
        grad_scores = (probs * (grad_probs - delta)).astype(jnp.bfloat16)
        grad_value_ref[here, :] += jnp.dot(
            probs.astype(jnp.bfloat16), grad, preferred_element_type=jnp.float32
        )
        grad_key_ref[here, :] += jnp.dot(grad_scores, query, preferred_element_type=jnp.float32)
        acc[...] += lax.dot_general(
            key_t_ref[:, here], grad_scores, (((1,), (0,)), ((), ())),
            preferred_element_type=jnp.float32,
        )
        return carry

    lax.fori_loop(span_ref[0, tile], span_ref[1, tile], step, 0)
    cosine, sine = cos_ref[...], sin_ref[...]
    half = HEAD // 2
    for h in range(count):
        own = acc[:, h * tokens : (h + 1) * tokens] * HEAD ** (-0.5)
        first, second = own[:half], own[half:]
        own = jnp.concatenate(
            [first * cosine + second * sine, second * cosine - first * sine], 0
        )
        pre_t_ref[h * HEAD : (h + 1) * HEAD, :] = own.astype(jnp.bfloat16)
        pre_ref[:, h * HEAD : (h + 1) * HEAD] = own.T.astype(jnp.bfloat16)

    @pl.when((tile == pl.num_programs(0) - 1) & (pl.program_id(1) == pl.num_programs(1) - 1))
    def _():
        grad_kv_ref[:, :HEAD] = grad_key_ref[...].astype(jnp.bfloat16)
        grad_kv_ref[:, HEAD:] = grad_value_ref[...].astype(jnp.bfloat16)


def attention_plan(tok_rows, key_count, low):
    tile = min(128, tok_rows)
    chunk = 256 if key_count % 256 == 0 else 128
    base = key_count - tok_rows
    tiles = tok_rows // tile
    begin = low[::tile] // chunk
    end = (base + (jnp.arange(tiles, dtype=jnp.int32) + 1) * tile + chunk - 1) // chunk
    return tile, chunk, base, jnp.stack([begin, end], 0).astype(jnp.int32)


GROUP = 10


def attend(query_pre, cosine, sine, low, window, deps=()):
    tok_rows = query_pre.shape[0]
    key_count = window.shape[0] - tok_rows
    tile, chunk, base, span = attention_plan(tok_rows, key_count, low)
    tiles = tok_rows // tile
    groups = HEADS // GROUP
    wide = GROUP * HEAD
    block = pl.BlockSpec((tile, wide), lambda i, g, s: (i, g))
    angle = pl.BlockSpec((tile, HEAD // 2), lambda i, g, s: (i, 0))
    return pl.pallas_call(
        lambda *refs: attend_kernel(*refs, base=base, chunk=chunk),
        grid_spec=pltpu.PrefetchScalarGridSpec(
            num_scalar_prefetch=1,
            grid=(tiles, groups),
            in_specs=[
                block,
                angle,
                angle,
                pl.BlockSpec((1, 1, tile), lambda i, g, s: (i, 0, 0)),
                pl.BlockSpec((key_count, HEAD), lambda i, g, s: (0, 0)),
                pl.BlockSpec((key_count, HEAD), lambda i, g, s: (0, 1)),
            ]
            + [pl.BlockSpec(memory_space=pl.ANY)] * len(deps),
            out_specs=[
                block,
                pl.BlockSpec((wide, tile), lambda i, g, s: (g, i)),
                block,
                pl.BlockSpec((1, 1, 1, GROUP * tile), lambda i, g, s: (i, g, 0, 0)),
            ],
            scratch_shapes=[
                pltpu.VMEM((HEAD, GROUP * tile), jnp.float32),
                pltpu.VMEM((HEAD, key_count), jnp.bfloat16),
            ],
        ),
        out_shape=[
            jax.ShapeDtypeStruct(query_pre.shape, jnp.bfloat16),
            jax.ShapeDtypeStruct(query_pre.shape[::-1], jnp.bfloat16),
            jax.ShapeDtypeStruct(query_pre.shape, jnp.bfloat16),
            jax.ShapeDtypeStruct((tiles, groups, 1, GROUP * tile), jnp.float32),
        ],
        compiler_params=pltpu.CompilerParams(vmem_limit_bytes=VMEM),
        cost_estimate=FREE,
        name="attend",
    )(span, query_pre, cosine, sine, low.reshape(tiles, 1, tile), window, window, *deps)


def attend_back(query_rot, grad_rows, attn_rows, log_total, cosine_t, sine_t, low, window, deps):
    tok_rows = query_rot.shape[0]
    key_count = window.shape[0] - tok_rows
    tile, chunk, base, span = attention_plan(tok_rows, key_count, low)
    tiles = tok_rows // tile
    groups = HEADS // GROUP
    wide = GROUP * HEAD
    block = pl.BlockSpec((tile, wide), lambda i, g, s: (i, g))
    angle = pl.BlockSpec((HEAD // 2, tile), lambda i, g, s: (0, i))
    return pl.pallas_call(
        lambda *refs: attend_back_kernel(*refs, base=base, chunk=chunk),
        grid_spec=pltpu.PrefetchScalarGridSpec(
            num_scalar_prefetch=1,
            grid=(tiles, groups),
            in_specs=[
                block,
                block,
                block,
                pl.BlockSpec((1, 1, 1, GROUP * tile), lambda i, g, s: (i, g, 0, 0)),
                angle,
                angle,
                pl.BlockSpec((1, 1, tile), lambda i, g, s: (i, 0, 0)),
                pl.BlockSpec((key_count, HEAD), lambda i, g, s: (0, 0)),
                pl.BlockSpec((key_count, HEAD), lambda i, g, s: (0, 1)),
            ]
            + [pl.BlockSpec(memory_space=pl.ANY)] * len(deps),
            out_specs=[
                block,
                pl.BlockSpec((wide, tile), lambda i, g, s: (g, i)),
                pl.BlockSpec((key_count, 2 * HEAD), lambda i, g, s: (0, 0)),
            ],
            scratch_shapes=[
                pltpu.VMEM((key_count, HEAD), jnp.float32),
                pltpu.VMEM((key_count, HEAD), jnp.float32),
                pltpu.VMEM((HEAD, GROUP * tile), jnp.float32),
                pltpu.VMEM((HEAD, key_count), jnp.bfloat16),
            ],
        ),
        out_shape=[
            jax.ShapeDtypeStruct(query_rot.shape, jnp.bfloat16),
            jax.ShapeDtypeStruct(query_rot.shape[::-1], jnp.bfloat16),
            jax.ShapeDtypeStruct((key_count, 2 * HEAD), jnp.bfloat16),
        ],
        compiler_params=pltpu.CompilerParams(vmem_limit_bytes=VMEM),
        cost_estimate=FREE,
        name="attend_back",
    )(
        span, query_rot, grad_rows, attn_rows, log_total, cosine_t, sine_t, low.reshape(tiles, 1, tile),
        window, window, *deps,
    )


def nt(left, right):
    return lax.dot_general(
        left, right, (((1,), (1,)), ((), ())), preferred_element_type=jnp.float32
    )


def tn(left, right):
    return lax.dot_general(
        left, right, (((0,), (0,)), ((), ())), preferred_element_type=jnp.float32
    )


def flat(ref):
    block = ref[...]
    return block.reshape(-1, block.shape[-1])


def units_kernel(core_ref, *refs):
    tokens, cots = refs[0:2], refs[2:4]
    gate_ref, up_ref, down_ref = refs[4:7]
    out_ref = refs[-1]
    gate_rows, up_rows, down_rows = flat(gate_ref), flat(up_ref), flat(down_ref)

    def one(token_ref, cot_ref):
        gate = nt(gate_rows, token_ref[...])
        up = nt(up_rows, token_ref[...])
        grad_mixed = nt(down_rows, cot_ref[...])
        root = (2.0 / jnp.pi) ** 0.5
        square = gate * gate
        curve = jnp.tanh(root * (gate + 0.044715 * (square * gate)))
        upper = 0.5 * (1.0 + curve)
        activated = gate * upper
        slope = upper + 0.5 * gate * (1.0 - curve * curve) * (root * (1.0 + 0.134145 * square))
        out_ref[0] = (grad_mixed * up * slope).astype(jnp.bfloat16)
        out_ref[1] = (grad_mixed * activated).astype(jnp.bfloat16)
        out_ref[2] = (activated * up).astype(jnp.bfloat16)

    for j in (0, 1):
        pl.when(pl.program_id(1) == j)(lambda j=j: one(tokens[j], cots[j]))


def units(tokens, cots, weights, core, group, held, deps=()):
    cols, width = tokens[0].shape
    hidden = weights.hidden
    token_block = pl.BlockSpec((cols, width), lambda i, j, s: (0, 0))
    extra = (() if held is None else (held,)) + tuple(deps)
    return pl.pallas_call(
        units_kernel,
        grid_spec=pltpu.PrefetchScalarGridSpec(
            num_scalar_prefetch=1,
            grid=(2, 2),
            in_specs=[token_block] * 4
            + weights.specs(2, lambda i, j, s: (i, 0), width)
            + [pl.BlockSpec(memory_space=pl.ANY)] * len(extra),
            out_specs=pl.BlockSpec(
                (3, hidden // 2, cols), lambda i, j, s: (0, i, 2 * group + j)
            ),
        ),
        out_shape=jax.ShapeDtypeStruct((3, hidden, 4 * cols), jnp.bfloat16),
        input_output_aliases={} if held is None else {8: 0},
        compiler_params=pltpu.CompilerParams(vmem_limit_bytes=VMEM),
        cost_estimate=FREE,
        name="units",
    )(core, *tokens, *cots, *weights.arrays, *extra)


class OwnWeights:
    def __init__(self, shards):
        self.arrays = tuple(shards)
        self.hidden = shards[0].shape[0] // 2

    def specs(self, cuts, place, width):
        def index(*grid):
            row, col = place(*grid)
            return (grid[-1][0] * cuts + row, col)

        return [pl.BlockSpec((self.hidden // cuts, width), index)] * len(self.arrays)


class FarWeights:
    def __init__(self, gathered):
        parts, count, rows, width = gathered.shape
        self.hidden = parts * rows
        if rows % 16:
            gathered = gathered.reshape(2, parts // 2, count, rows, width)
            gathered = gathered.transpose(0, 2, 1, 3, 4).reshape(2, count, -1, width)
        self.arrays = (gathered,) * count

    def specs(self, cuts, place, width):
        parts, count, rows, _ = self.arrays[0].shape

        def spec(which):
            def index(*grid):
                row, col = place(*grid)
                return (row, which, 0, col)

            return pl.BlockSpec((parts // cuts, 1, rows, width), index)

        return [spec(which) for which in range(count)]


def sums_kernel(core_ref, *refs, count):
    total = 0.0
    for act_ref, weight_ref in zip(refs[:count], refs[count : 2 * count], strict=True):
        total = total + tn(act_ref[0], flat(weight_ref))
    refs[-1][...] = total.astype(jnp.bfloat16)


def sums(acts, weights, core, group, which, block=None, deps=()):
    all_tokens = acts[0].shape[2]
    width = weights[0].arrays[0].shape[-1]
    rows = all_tokens // 4
    blocks = 2 if block is None else 1
    cols = 512 if width % 512 == 0 else width // 2
    first = 2 * group + (block or 0)

    def act_spec(act, kind):
        return pl.BlockSpec((1, act.shape[1], rows), lambda n, t, s: (kind, 0, first + t))

    act_specs, weight_specs, act_args, weight_args = [], [], [], []
    for act, weight in zip(acts, weights, strict=True):
        specs = weight.specs(1, lambda n, t, s: (0, n), cols)
        for kind in which:
            act_specs.append(act_spec(act, kind))
            act_args.append(act)
            weight_specs.append(specs[kind])
            weight_args.append(weight.arrays[kind])
    return pl.pallas_call(
        lambda *refs: sums_kernel(*refs, count=len(act_args)),
        grid_spec=pltpu.PrefetchScalarGridSpec(
            num_scalar_prefetch=1,
            grid=(width // cols, blocks),
            in_specs=act_specs + weight_specs + [pl.BlockSpec(memory_space=pl.ANY)] * len(deps),
            out_specs=pl.BlockSpec((rows, cols), lambda n, t, s: (t, n)),
        ),
        out_shape=jax.ShapeDtypeStruct((blocks * rows, width), jnp.bfloat16),
        compiler_params=pltpu.CompilerParams(vmem_limit_bytes=VMEM),
        cost_estimate=FREE,
        name="sums",
    )(core, *act_args, *weight_args, *deps)


def grams_kernel(acts_ref, *refs, sets):
    out_ref = refs[-1]

    def one(rights):
        step = rights[0].shape[0]
        total = 0.0
        for i, right_ref in enumerate(rights):
            total = total + jnp.dot(
                acts_ref[0, :, i * step : (i + 1) * step], right_ref[...],
                preferred_element_type=jnp.float32,
            )
        out_ref[0] = total.astype(jnp.bfloat16)

    if sets == 1:
        one(refs[0:4])
    else:
        pl.when(pl.program_id(0) < 2)(lambda: one(refs[0:4]))
        pl.when(pl.program_id(0) == 2)(lambda: one(refs[4:8]))


def grams(acts, tokens, cots, pairs, kinds, deps=()):
    _, hidden, all_tokens = acts.shape
    step, width = tokens[0].shape
    cols = width // pairs
    first, count = kinds[0], len(kinds)
    if cols % 128:
        parts = []
        for kind in kinds:
            whole = sum(
                product(acts[kind, :, i * step : (i + 1) * step], right)
                for i, right in enumerate(cots if kind == 2 else tokens)
            )
            parts.append(whole.astype(jnp.bfloat16))
        return jnp.concatenate(parts, 0).reshape(count * hidden, pairs, cols).transpose(1, 0, 2)
    if count == 3:
        specs = [pl.BlockSpec((step, cols), lambda k, p: (0, jnp.where(k < 2, p, pairs - 1)))] * 4
        specs = specs + [pl.BlockSpec((step, cols), lambda k, p: (0, jnp.where(k < 2, 0, p)))] * 4
        rights = tuple(tokens) + tuple(cots)
    else:
        specs = [pl.BlockSpec((step, cols), lambda k, p: (0, p))] * 4
        rights = tuple(cots) if first == 2 else tuple(tokens)
    return pl.pallas_call(
        lambda *refs: grams_kernel(*refs, sets=len(rights) // 4),
        grid=(count, pairs),
        in_specs=[pl.BlockSpec((1, hidden, all_tokens), lambda k, p: (first + k, 0, 0))]
        + specs
        + [pl.BlockSpec(memory_space=pl.ANY)] * len(deps),
        out_specs=pl.BlockSpec((1, hidden, cols), lambda k, p: (p, k, 0)),
        out_shape=jax.ShapeDtypeStruct((pairs, count * hidden, cols), jnp.bfloat16),
        compiler_params=pltpu.CompilerParams(vmem_limit_bytes=VMEM),
        cost_estimate=FREE,
        name="grams",
    )(acts, *rights, *deps)


class Gathered:
    def __init__(self, own, others, shard):
        count, _, rows, width = others.shape
        if rows % 16:
            others = others.transpose(1, 0, 2, 3).reshape(1, -1, count * rows, width)
        self.own, self.others = own, others
        self.shard = shard.reshape(1).astype(jnp.int32)
        self.shards = others.shape[1] + 1

    def place(self, step, shard_ref):
        return lax.rem(shard_ref[0] + self.shards - step, self.shards)

    def specs(self):
        count, _, rows, width = self.others.shape
        return [
            pl.BlockSpec(self.own.shape, lambda r, s: (0, 0)),
            pl.BlockSpec((count, 1, rows, width), lambda r, s: (0, jnp.maximum(r - 1, 0), 0, 0)),
        ]


def by_shard(own_ref, others_ref, use):
    pl.when(pl.program_id(0) == 0)(lambda: use(own_ref[...]))
    pl.when(pl.program_id(0) > 0)(lambda: use(flat(others_ref)))


def spread_kernel(shard_ref, left_ref, own_ref, others_ref, *refs):
    out_ref = refs[-1]

    def use(weight):
        out_ref[...] = nt(left_ref[...], weight).astype(out_ref.dtype)

    by_shard(own_ref, others_ref, use)


def spread(left, weight, dtype, deps=()):
    tokens, width = left.shape
    rows = weight.own.shape[0]
    return pl.pallas_call(
        spread_kernel,
        grid_spec=pltpu.PrefetchScalarGridSpec(
            num_scalar_prefetch=1,
            grid=(weight.shards,),
            in_specs=[pl.BlockSpec((tokens, width), lambda r, s: (0, 0))]
            + weight.specs()
            + [pl.BlockSpec(memory_space=pl.ANY)] * len(deps),
            out_specs=pl.BlockSpec((tokens, rows), lambda r, s: (0, weight.place(r, s))),
        ),
        out_shape=jax.ShapeDtypeStruct((tokens, weight.shards * rows), dtype),
        compiler_params=pltpu.CompilerParams(vmem_limit_bytes=VMEM),
        cost_estimate=FREE,
        name="spread",
    )(weight.shard, left, weight.own, weight.others, *deps)


def collect_kernel(shard_ref, left_ref, own_ref, others_ref, start_ref, gain_ref, *refs, outs):
    refs = refs[-outs:]
    total_ref = refs[0]

    @pl.when(pl.program_id(0) == 0)
    def _():
        total_ref[...] = start_ref[...].astype(jnp.float32)

    def use(weight):
        total_ref[...] += jnp.dot(left_ref[...], weight, preferred_element_type=jnp.float32)

    by_shard(own_ref, others_ref, use)
    if outs > 1:

        @pl.when(pl.program_id(0) == pl.num_programs(0) - 1)
        def _():
            rows = min(128, total_ref.shape[0])

            def norm(i, carry):
                here = pl.ds(pl.multiple_of(i * rows, rows), rows)
                total = total_ref[here, :]
                scale = norm_scale(total)
                refs[1][here, :] = (total * scale * gain_ref[...]).astype(jnp.bfloat16)
                refs[2][here, :] = jnp.broadcast_to(scale, (rows, 128))
                return carry

            lax.fori_loop(0, total_ref.shape[0] // rows, norm, 0)


def collect(left, weight, start, gain=None, deps=()):
    tokens = left.shape[0]
    rows, width = weight.own.shape
    whole = pl.BlockSpec((tokens, width), lambda r, s: (0, 0))
    shapes, specs = [jax.ShapeDtypeStruct((tokens, width), jnp.float32)], [whole]
    if gain is not None:
        shapes.append(jax.ShapeDtypeStruct((tokens, width), jnp.bfloat16))
        shapes.append(jax.ShapeDtypeStruct((tokens, 128), jnp.float32))
        specs.extend([whole, pl.BlockSpec((tokens, 128), lambda r, s: (0, 0))])
    gain_row = jnp.zeros((1, width), jnp.float32) if gain is None else gain.reshape(1, width)
    return pl.pallas_call(
        lambda *refs: collect_kernel(*refs, outs=len(specs)),
        grid_spec=pltpu.PrefetchScalarGridSpec(
            num_scalar_prefetch=1,
            grid=(weight.shards,),
            in_specs=[pl.BlockSpec((tokens, rows), lambda r, s: (0, weight.place(r, s)))]
            + weight.specs()
            + [whole, pl.BlockSpec((1, width), lambda r, s: (0, 0))]
            + [pl.BlockSpec(memory_space=pl.ANY)] * len(deps),
            out_specs=specs,
        ),
        out_shape=shapes,
        compiler_params=pltpu.CompilerParams(vmem_limit_bytes=VMEM),
        cost_estimate=FREE,
        name="collect",
    )(weight.shard, left, weight.own, weight.others, start, gain_row, *deps)


def cross_kernel(core_ref, *refs, lefts, gained, added):
    right_ref, out_ref = refs[lefts], refs[-1]
    first = 0

    def put(part, rows):
        here = (0, slice(None), slice(first, first + rows))
        if added:
            part = part + refs[lefts + 1 + gained][here].astype(jnp.float32)
        out_ref[here] = part.astype(jnp.bfloat16)

    for left_ref in refs[:lefts]:
        shards, _, rows, tokens = left_ref.shape
        left = left_ref[...].reshape(shards * rows, tokens)
        part = jnp.dot(left, right_ref[...], preferred_element_type=jnp.float32)
        put(part.reshape(shards, rows, -1), rows)
        first = first + rows
    if gained:
        gains = refs[lefts + 1][...].astype(jnp.float32)
        put(jnp.broadcast_to(gains[None], (out_ref.shape[1],) + gains.shape), gains.shape[0])


def cross(lefts, right, core, shards, pairs, gains=None, add=None, deps=(), first=0, of=None, into=None):
    tokens, width = right.shape
    cols = width // pairs
    views = [left.reshape(shards, 2, -1, tokens) for left in lefts]
    rows = [view.shape[2] for view in views]
    total = sum(rows) + (0 if gains is None else gains.shape[0])
    if cols % 128:
        picked = jnp.concatenate(
            [lax.dynamic_index_in_dim(view, core[0], 1, keepdims=False) for view in views], 1
        )
        whole = product(picked.reshape(-1, tokens), right).reshape(shards, sum(rows), width)
        if gains is not None:
            extra = jnp.broadcast_to(gains.astype(jnp.float32)[None], (shards,) + gains.shape)
            whole = jnp.concatenate([whole, extra], 1)
        whole = whole.reshape(shards, total, pairs, cols).transpose(2, 0, 1, 3)
        if add is not None:
            whole = whole + add[:, :, first : first + total].astype(jnp.float32)
        whole = whole.astype(jnp.bfloat16)
        if of is None:
            return whole
        if into is None:
            into = jnp.zeros((pairs, shards, of, cols), jnp.bfloat16)
        return lax.dynamic_update_slice(into, whole, (0, 0, first, 0))
    block = pl.BlockSpec((1, shards, total, cols), lambda p, s: (p, 0, first // total, 0))
    kept = () if into is None else (into,)
    specs = [
        pl.BlockSpec((shards, 1, count, tokens), lambda p, s: (0, s[0], 0, 0)) for count in rows
    ]
    specs.append(pl.BlockSpec((tokens, cols), lambda p, s: (0, p)))
    args = [*views, right]
    if gains is not None:
        specs.append(pl.BlockSpec((gains.shape[0], cols), lambda p, s: (0, p)))
        args.append(gains)
    if add is not None:
        specs.append(block)
        args.append(add)
    return pl.pallas_call(
        lambda *refs: cross_kernel(
            *refs, lefts=len(views), gained=gains is not None, added=add is not None
        ),
        grid_spec=pltpu.PrefetchScalarGridSpec(
            num_scalar_prefetch=1,
            grid=(pairs,),
            in_specs=specs + [pl.BlockSpec(memory_space=pl.ANY)] * (len(kept) + len(deps)),
            out_specs=block,
        ),
        out_shape=jax.ShapeDtypeStruct((pairs, shards, of or total, cols), jnp.bfloat16),
        input_output_aliases={1 + len(args): 0} if kept else {},
        compiler_params=pltpu.CompilerParams(vmem_limit_bytes=VMEM),
        cost_estimate=FREE,
        name="cross",
    )(core, *args, *kept, *deps)


def swap(value, axis, bit):
    return lax.ppermute(value, axis, [(i, i ^ bit) for i in range(lax.axis_size(axis))])


def after(value, *others):
    return lax.optimization_barrier((value, *others))[0]


def same_core():
    count = lax.axis_size("ctx")
    return [list(range(0, count, 2)), list(range(1, count, 2))]


def own_part(shard, place):
    part = shard.shape[0] // lax.axis_size("ctx")
    return lax.dynamic_slice_in_dim(shard, place * part, part, 0)


def together(*values):
    return lax.optimization_barrier(values)


def halving_scatter(blocks, axis, place):
    held, bit = blocks, 1
    while held.shape[0] > 1:
        both = held.reshape((held.shape[0] // 2, 2) + held.shape[1:])
        mine = (place // bit) % 2
        keep = lax.dynamic_index_in_dim(both, mine, 1, keepdims=False)
        give = lax.dynamic_index_in_dim(both, 1 - mine, 1, keepdims=False)
        total = keep.astype(jnp.float32) + swap(give, axis, bit).astype(jnp.float32)
        held = total.astype(jnp.bfloat16)
        bit = 2 * bit
    return total[0]


def step_ring(value, axis):
    count = lax.axis_size(axis)
    return lax.ppermute(value, axis, [(i, (i + 1) % count) for i in range(count)])


def ring(value, axis):
    arrived = []
    for _ in range(lax.axis_size(axis) - 1):
        value = step_ring(value, axis)
        arrived.append(value)
    return arrived


def exchanges(axis):
    bits, bit = [], 2
    while bit < lax.axis_size(axis):
        bits.append(bit)
        bit = 2 * bit
    return bits + [1]


def pairs_gather(value):
    pairs = lax.axis_size("ctx") // 2
    if pairs == 4:
        half = value.shape[0] // 2
        x_all, y_all = swap(value, "ctx", 2), swap(value, "ctx", 4)
        low = swap(y_all[:half], "ctx", 2)
        high = swap(x_all[half:], "ctx", 4)
        return [(0, [value]), (2, [x_all]), (4, [y_all]), (6, [low, high])]
    held, bit = [(0, value)], 2
    while bit < 2 * pairs:
        held = held + [(bits ^ bit, swap(item, "ctx", bit)) for bits, item in held]
        bit = 2 * bit
    return [(bits, [item]) for bits, item in held]


def window_gather(value, reach, place):
    rows = value.shape[0]
    out = jnp.zeros(((reach + 2) * rows,) + value.shape[1:], value.dtype)
    parts = [(bits, part, i) for bits, held in pairs_gather(value) for i, part in enumerate(held)]
    for bits, part, i in parts:
        both = ((bits, part), (bits ^ 1, swap(part, "ctx", 1)))
        for other, block in both:
            spot = (place ^ other) - place + reach
            spot = jnp.where((spot < 0) | (spot > reach), reach + 1, spot)
            start = spot * rows + (i * block.shape[0])
            out = lax.dynamic_update_slice_in_dim(out, block, start, 0)
    return out


def place_block(out, block, place):
    return lax.dynamic_update_index_in_dim(out, block, place, 0)


def in_places(own, arrived, place):
    count = len(arrived) + 1
    out = jnp.zeros((count,) + own.shape, own.dtype)
    for step, value in enumerate([own, *arrived]):
        out = lax.dynamic_update_index_in_dim(out, value, lax.rem(place + count - step, count), 0)
    return out


def in_order(gathered, first, part):
    mine = gathered[:, :, first : first + part].transpose(1, 0, 2, 3)
    return mine.reshape(-1, gathered.shape[-1])


def body(
    inputs,
    norm_gains,
    q_weight,
    kv_weight,
    o_weight,
    gate_weight,
    up_weight,
    down_weight,
    cotangent,
    doc_lengths,
):
    x_rows = inputs[0].astype(jnp.float32)
    grad_out = cotangent[0]
    tok_rows, width = x_rows.shape
    place = lax.axis_index("ctx")
    ctx_count = lax.axis_size("ctx")
    pairs = ctx_count // 2
    core = place % 2
    pair = place // 2
    own_core = core.reshape(1).astype(jnp.int32)
    shard = lax.axis_index("fsdp")
    shards = lax.axis_size("fsdp")
    reach = min(ctx_count - 1, (WINDOW + tok_rows - 2) // tok_rows)
    key_count = (reach + 1) * tok_rows
    first_token = place * tok_rows
    token_ids, segment, positions = doc_info(doc_lengths[0], first_token, tok_rows)
    low = jnp.maximum(token_ids - positions, token_ids - (WINDOW - 1)) - (
        first_token - reach * tok_rows
    )
    cosine, sine = rope_angles(positions)
    gain_attn = norm_gains[0]
    gain_mlp = norm_gains[1]

    q_part, kv_part, o_part = (own_part(w, place) for w in (q_weight, kv_weight, o_weight))
    kv_z = in_places(kv_part, ring(kv_part, "fsdp"), shard)
    moving = after(q_part, kv_z)
    held, origins = kv_z[None], [place]
    q_arrived = []
    for bit in exchanges("ctx"):
        if len(q_arrived) < shards - 1:
            moving = step_ring(moving, "fsdp")
            q_arrived.append(moving)
        held = jnp.concatenate([held, swap(held, "ctx", bit)], 0)
        origins = origins + [origin ^ bit for origin in origins]
        held, moving = together(held, moving)
    while len(q_arrived) < shards - 1:
        moving = step_ring(moving, "fsdp")
        q_arrived.append(moving)
    kv_all = jnp.zeros_like(held)
    for step, origin in enumerate(origins):
        kv_all = place_block(kv_all, held[step], origin)
    q_ring = jnp.stack(q_arrived, 0)
    q_ring, kv_all = together(q_ring, kv_all)
    q_all = lax.all_gather(q_ring, "ctx", axis=0)

    half_rows = gate_weight.shape[0] // 2
    part_rows = half_rows // pairs
    cut = (part_rows * 7 // 15 + 15) // 16 * 16
    far_rows, last_rows = cut // 4, part_rows - cut
    mine = jnp.stack(
        [
            lax.dynamic_slice_in_dim(w, core * half_rows + pair * part_rows, part_rows, 0)
            for w in (gate_weight, up_weight, down_weight)
        ],
        0,
    )
    mine, _ = together(mine, q_ring)
    own_weights = OwnWeights((gate_weight, up_weight, down_weight))

    scale_one = norm_scale(x_rows)
    normed_one = (x_rows * scale_one * gain_attn).astype(jnp.bfloat16)
    kv_full = in_order(kv_all, 0, kv_part.shape[0])
    kv_pre = times_rows(normed_one, kv_full)
    key_rot = rotate(kv_pre[:, :HEAD], cosine, sine).astype(jnp.bfloat16)
    kv_local = jnp.concatenate([key_rot, kv_pre[:, HEAD:].astype(jnp.bfloat16)], 1)
    kv_local, moving = together(kv_local, o_part)
    kv_window = window_gather(kv_local, reach, place)
    o_arrived = ring(moving, "fsdp")
    cot_rows = tok_rows // 8
    cot_first = swap(after(grad_out[:cot_rows], o_arrived[-1]), "fsdp", 1)
    far_first = swap(after(mine[:, :far_rows], o_arrived[-1]), "fsdp", 2)
    o_ring = jnp.stack(o_arrived, 0)
    q_all, o_ring, far_first, cot_first, kv_window, normed_one, cosine_t, sine_t = together(
        q_all, o_ring, far_first, cot_first, kv_window, normed_one, cosine.T, sine.T
    )
    o_all = lax.all_gather(o_ring, "ctx", axis=0)
    q_full = Gathered(q_weight, q_all, shard)
    o_full = Gathered(o_weight, o_all, shard)
    far_second = swap(after(mine[:, far_rows : part_rows - last_rows], o_ring), "fsdp", 2)
    cot_second = swap(after(grad_out[cot_rows:], o_ring), "fsdp", 1)
    query_pre = spread(normed_one, q_full, jnp.float32)
    attn_rows, attn_rows_t, query_rot, log_total = attend(
        query_pre, cosine, sine, low, kv_window
    )
    far_last = mine[:, part_rows - last_rows :]
    log_total, cot_second, far_second, far_last = together(
        log_total, cot_second, far_second, far_last
    )
    far_third = swap(far_last, "fsdp", 2)
    near_cots = (grad_out, swap(grad_out, "ctx", 1))
    cot_across = jnp.concatenate([cot_first, cot_second], 0)
    cots = [near_cots, (cot_across, swap(cot_across, "ctx", 1))]

    def over_plane(part):
        return lax.all_gather(part, "ctx", axis=0, axis_index_groups=same_core())

    far_a = FarWeights(
        over_plane(jnp.concatenate([far_first, far_second], 1))
    )
    hidden_one, normed_two, scale_two = collect(attn_rows, o_full, inputs[0], gain_mlp)
    scale_two = scale_two[:, :1]

    near = (normed_two, swap(normed_two, "ctx", 1))
    across = swap(normed_two, "fsdp", 1)
    own_acts = units(near, near_cots, own_weights, own_core, 0, None)
    a_acts = units(near, near_cots, far_a, own_core, 0, None, (own_acts, cots[1][1]))
    across, a_acts, far_third = together(across, a_acts, far_third)
    far = (across, swap(across, "ctx", 1))
    far_b = FarWeights(over_plane(far_third))
    own_acts = units(far, cots[1], own_weights, own_core, 1, own_acts, (a_acts,))
    a_acts = units(far, cots[1], far_a, own_core, 1, a_acts, (own_acts,))
    near_far, cot_rows = near + far, cots[0] + cots[1]

    def over_pairs(blocks):
        mine = lax.psum_scatter(
            blocks, "ctx", scatter_dimension=0, tiled=False, axis_index_groups=same_core()
        )
        return lax.optimization_barrier(mine)

    a_grams = grams(a_acts, near_far, cot_rows, pairs, (0, 1, 2))
    b_acts = units(near, cots[0], far_b, own_core, 0, None, (a_grams,))
    b_acts = units(far, cots[1], far_b, own_core, 1, b_acts)
    b_grams = grams(b_acts, near_far, cot_rows, pairs, (0, 1, 2))
    a_sums, b_sums = over_pairs(a_grams), over_pairs(b_grams)
    acts, weights = (own_acts, a_acts, b_acts), (own_weights, far_a, far_b)

    def group_sums(group, which, block, deps):
        return sums(acts, weights, own_core, group, which, block, deps)

    own_gate_up = grams(own_acts, near_far, cot_rows, pairs, (0, 1), (b_grams,))
    give = group_sums(1, (0, 1), 1, (own_gate_up,))
    own_gate_up = over_pairs(own_gate_up)
    got = swap(give, "ctx", 1)
    near_give = group_sums(0, (0, 1), 1, (give,))
    near_got = swap(near_give, "ctx", 1)
    keep = group_sums(1, (0, 1), 0, (near_give, a_sums))
    total = add16(keep, got)
    moved = swap(total, "fsdp", 1)
    own_down = grams(own_acts, near_far, cot_rows, pairs, (2,), (total, near_got))
    near_keep = group_sums(0, (0, 1), 0, (own_down,))
    out_give = group_sums(1, (2,), 1, (near_keep,))
    out_got = swap(out_give, "ctx", 1)
    out_keep = group_sums(1, (2,), 0, (out_give,))
    moved, own_down, near_keep, out_keep, a_sums = together(
        moved, own_down, near_keep, out_keep, a_sums
    )
    own_down = over_pairs(own_down)
    grad_normed_two = (
        near_keep.astype(jnp.float32) + near_got.astype(jnp.float32) + moved.astype(jnp.float32)
    )
    grad_hidden = grad_out.astype(jnp.float32) + norm_back(
        grad_normed_two, hidden_one, scale_two, gain_mlp
    )
    gain_mlp_grad = jnp.sum(grad_normed_two * hidden_one * scale_two, 0)
    grad_branch = grad_hidden.astype(jnp.bfloat16)
    grad_attended = spread(grad_branch, o_full, jnp.bfloat16, (b_sums,))

    gate_rows = b_sums.shape[0] // 3
    a_all = swap(a_sums, "fsdp", 2)
    grad_query_pre, grad_query_pre_t, grad_kv = attend_back(
        query_rot, grad_attended, attn_rows, log_total, cosine_t, sine_t, low, kv_window,
        (out_keep,),
    )
    grad_stack = grad_kv.reshape(reach + 1, tok_rows, 2 * HEAD)
    moved_kv = [shifted(grad_stack[reach - hop], "ctx", -hop) for hop in range(1, reach + 1)]
    out_moved = swap(add16(out_keep, out_got), "fsdp", 1)
    q_give = cross(
        [grad_query_pre_t], normed_one, 1 - own_core, shards, pairs,
        deps=(grad_kv, a_all, own_gate_up, out_moved),
    )
    q_got = swap(q_give, "ctx", 1)
    q_half, kv_half = q_weight.shape[0] // 2, kv_weight.shape[0] // 2
    okv_rows = q_half + kv_half + 16
    okv_give = cross(
        [attn_rows_t], grad_branch, 1 - own_core, shards, pairs, deps=(q_give,), of=okv_rows
    )
    q_sums = cross(
        [grad_query_pre_t], normed_one, own_core, shards, pairs, None, q_got, (okv_give,)
    )
    moved_kv, q_sums, b_sums = together(moved_kv, q_sums, b_sums)
    b_gate = swap(b_sums[:gate_rows], "fsdp", 2)
    b_up = swap(after(b_sums[gate_rows : 2 * gate_rows], b_gate), "fsdp", 2)
    b_down = swap(after(b_sums[2 * gate_rows :], b_up), "fsdp", 2)
    q_pairs = over_pairs(q_sums)
    own_kv_grad = grad_stack[reach].astype(jnp.float32)
    for block in moved_kv:
        own_kv_grad = own_kv_grad + block.astype(jnp.float32)
    grad_kv_pre = jnp.concatenate(
        [rotate_back(own_kv_grad[:, :HEAD], cosine, sine), own_kv_grad[:, HEAD:]], 1
    ).astype(jnp.bfloat16)
    (grad_normed_one,) = collect(
        grad_query_pre, q_full, product(grad_kv_pre, kv_full)
    )
    gain_attn_grad = jnp.sum(grad_normed_one * x_rows * scale_one, 0)
    gains = jnp.stack([gain_attn_grad, gain_mlp_grad], 0).astype(jnp.bfloat16)
    gains = jnp.concatenate([gains, jnp.zeros((14, width), jnp.bfloat16)], 0)
    kv_left = [grad_kv_pre.T]
    okv_give = cross(
        kv_left, normed_one, 1 - own_core, shards, pairs, gains, None, (b_gate,), q_half,
        okv_rows, okv_give,
    )
    okv_got = swap(okv_give, "ctx", 1)
    near_out = sums(acts, weights, own_core, 0, (2,), None, (okv_give,))
    near_out_got = swap(near_out[tok_rows:], "ctx", 1)
    okv_sums = cross(
        [attn_rows_t], grad_branch, own_core, shards, pairs, None, okv_got, (near_out, b_up),
        of=okv_rows,
    )
    okv_sums = cross(
        kv_left, normed_one, own_core, shards, pairs, gains, okv_got, (own_down, q_pairs), q_half, okv_rows,
        okv_sums,
    )
    grad_inputs = grad_hidden + norm_back(grad_normed_one, x_rows, scale_one, gain_attn)

    out_cols = width // ctx_count

    def both_halves(mine):
        keep = lax.dynamic_slice_in_dim(mine, core * out_cols, out_cols, 1)
        give = lax.dynamic_slice_in_dim(mine, (1 - core) * out_cols, out_cols, 1)
        got = swap(give.astype(jnp.bfloat16), "ctx", 1).astype(jnp.float32)
        lower = jnp.where(core == 0, keep, got)
        upper = jnp.where(core == 0, got, keep)
        return jnp.concatenate([lower, upper], 0)

    okv_pairs = over_pairs(okv_sums)
    q_mine = halving_scatter(q_pairs, "fsdp", shard)
    b_down, q_mine = together(b_down, q_mine)
    result = hidden_one + (
        near_out[:tok_rows].astype(jnp.float32)
        + near_out_got.astype(jnp.float32)
        + out_moved.astype(jnp.float32)
    )
    q_grad = both_halves(q_mine)
    okv_mine = halving_scatter(okv_pairs, "fsdp", shard)
    o_grad = both_halves(okv_mine[:q_half])
    kv_grad = both_halves(okv_mine[q_half : q_half + kv_half])
    gain_total = lax.dynamic_slice_in_dim(
        okv_mine[q_half + kv_half : q_half + kv_half + 2], core * out_cols, out_cols, 1
    )

    a_all = a_all.reshape(3, pairs, cut, -1)
    b_all = jnp.concatenate([b_gate, b_up, b_down], 0).reshape(3, pairs, part_rows - cut, -1)
    own_all = (own_gate_up[:half_rows], own_gate_up[half_rows:], own_down)
    mlp_grads = []
    for kind in range(3):
        others = jnp.concatenate([a_all[kind], b_all[kind]], 1).reshape(half_rows, -1)
        mlp_grads.append(
            both_halves(own_all[kind].astype(jnp.float32) + others.astype(jnp.float32))
        )

    return (
        result.astype(jnp.bfloat16)[None],
        grad_inputs.astype(jnp.bfloat16)[None],
        gain_total,
        q_grad,
        kv_grad,
        o_grad,
        mlp_grads[0],
        mlp_grads[1],
        mlp_grads[2],
    )


def solution(mesh):
    in_specs = (
        P("fsdp", "ctx", None),
        P(),
        P("fsdp", None),
        P("fsdp", None),
        P("fsdp", None),
        P("fsdp", None),
        P("fsdp", None),
        P("fsdp", None),
        P("fsdp", "ctx", None),
        P("fsdp", None),
    )
    out_specs = (
        P("fsdp", "ctx", None),
        P("fsdp", "ctx", None),
        P(None, "ctx"),
        P("fsdp", "ctx"),
        P("fsdp", "ctx"),
        P("fsdp", "ctx"),
        P("fsdp", "ctx"),
        P("fsdp", "ctx"),
        P("fsdp", "ctx"),
    )
    return jax.shard_map(body, mesh=mesh, in_specs=in_specs, out_specs=out_specs, check_vma=False)
```

```python
import jax
import jax.numpy as jnp
from jax import lax
from jax.experimental import pallas as pl
from jax.experimental.pallas import tpu as pltpu
from jax.sharding import PartitionSpec as P

HEADS = 10
HEAD = 256
WINDOW = 2048


EPSILON = 1e-06
MASKED = -1e30
LOWEST = -1e29
VMEM = 56 * 1024 * 1024
FREE = pl.CostEstimate(flops=0, bytes_accessed=0, transcendentals=0)


def shifted(value, axis, steps):
    count = lax.axis_size(axis)
    initial, last = (max(0, -steps), min(count, count - steps))
    return lax.ppermute(value, axis, [(source, source + steps) for source in range(initial, last)])


def swap(value, axis, bit):
    return lax.ppermute(value, axis, [(i, i ^ bit) for i in range(lax.axis_size(axis))])


def add16(left, right):
    return (left.astype(jnp.float32) + right.astype(jnp.float32)).astype(jnp.bfloat16)


def times_rows(left, right):
    return lax.dot_general(
        left, right, (((1,), (1,)), ((), ())), preferred_element_type=jnp.float32
    )


def gram_rows(left, right):
    return lax.dot_general(
        left, right, (((0,), (0,)), ((), ())), preferred_element_type=jnp.float32
    )


def product(left, right):
    return jnp.dot(left, right, preferred_element_type=jnp.float32)


def doc_info(doc_lengths, first_token, token_count):
    doc_ends = jnp.cumsum(doc_lengths)
    doc_starts = doc_ends - doc_lengths
    token_ids = first_token + jnp.arange(token_count, dtype=jnp.int32)
    segment = jnp.sum((doc_ends[None, :] <= token_ids[:, None]).astype(jnp.int32), 1)
    begins = jnp.max(
        jnp.where(doc_starts[None, :] <= token_ids[:, None], doc_starts[None, :], 0), 1
    )
    return (token_ids, segment, token_ids - begins)


def rope_angles(positions):
    half_width = HEAD // 2
    column = jnp.arange(half_width, dtype=jnp.float32)
    inverse = jnp.power(10000.0, -column / half_width)
    angles = positions.astype(jnp.float32)[:, None] * inverse[None, :]
    return (jnp.cos(angles), jnp.sin(angles))


def rotate(values, cosine, sine):
    half_width = values.shape[-1] // 2
    first_half = values[..., :half_width]
    second_half = values[..., half_width:]
    return jnp.concatenate(
        [first_half * cosine - second_half * sine, second_half * cosine + first_half * sine], -1
    )


def rotate_back(grad_in, cosine, sine):
    half_width = grad_in.shape[-1] // 2
    first_half = grad_in[..., :half_width]
    second_half = grad_in[..., half_width:]
    return jnp.concatenate(
        [first_half * cosine + second_half * sine, second_half * cosine - first_half * sine], -1
    )


def norm_scale(values):
    return lax.rsqrt(jnp.mean(values * values, -1, keepdims=True) + EPSILON)


def norm_back(grad_in, values, scale, gain):
    weighted = grad_in * gain
    return scale * weighted - values * scale * scale * scale * jnp.mean(
        weighted * values, -1, keepdims=True
    )


def head_rows(block, count):
    return jnp.concatenate([block[:, h * HEAD : (h + 1) * HEAD] for h in range(count)], 0)


def row_bounds(low_ref, first_key, tokens, count):
    high = first_key + lax.broadcasted_iota(jnp.int32, (1, tokens), 1)
    low = low_ref[0]
    return jnp.concatenate([low] * count, 1), jnp.concatenate([high] * count, 1)


def seen(start, shape, low, high):
    key = start + lax.broadcasted_iota(jnp.int32, shape, 0)
    return (key >= low) & (key <= high)


def turn(from_ref, to_ref, chunk):
    def step(j, carry):
        here = pl.ds(pl.multiple_of(j * chunk, chunk), chunk)
        to_ref[:, here] = from_ref[here, :].astype(jnp.float32).T.astype(jnp.bfloat16)
        return carry

    lax.fori_loop(0, from_ref.shape[0] // chunk, step, 0)


def attend_kernel(
    span_ref, pre_ref, cos_ref, sin_ref, low_ref, key_ref, value_ref, *refs, base, chunk
):
    out_ref, out_t_ref, rot_ref, log_ref, acc, value_t_ref = refs[-6:]

    @pl.when((pl.program_id(0) == 0) & (pl.program_id(1) == 0))
    def _():
        turn(value_ref, value_t_ref, chunk)

    tile = pl.program_id(0)
    tokens = pre_ref.shape[0]
    count = pre_ref.shape[1] // HEAD
    cosine, sine = cos_ref[...], sin_ref[...]
    half = HEAD // 2
    for h in range(count):
        first = pre_ref[:, h * HEAD : h * HEAD + half]
        second = pre_ref[:, h * HEAD + half : (h + 1) * HEAD]
        rot_ref[:, h * HEAD : h * HEAD + half] = (
            (first * cosine - second * sine) * HEAD ** (-0.5)
        ).astype(jnp.bfloat16)
        rot_ref[:, h * HEAD + half : (h + 1) * HEAD] = (
            (second * cosine + first * sine) * HEAD ** (-0.5)
        ).astype(jnp.bfloat16)
    query = head_rows(rot_ref[...], count)
    low, high = row_bounds(low_ref, base + tile * tokens, tokens, count)
    rows = count * tokens

    acc[...] = jnp.zeros_like(acc)

    def step(j, carry):
        top, total = carry
        start = pl.multiple_of(j * chunk, chunk)
        scores = lax.dot_general(
            key_ref[pl.ds(start, chunk), :], query, (((1,), (1,)), ((), ())),
            preferred_element_type=jnp.float32,
        )
        scores = jnp.where(seen(start, scores.shape, low, high), scores, MASKED)
        higher = jnp.maximum(top, jnp.max(scores, 0, keepdims=True))
        part = jnp.exp(scores - higher)
        shrink = jnp.exp(top - higher)
        acc[...] = acc[...] * shrink + lax.dot_general(
            value_t_ref[:, pl.ds(start, chunk)], part.astype(jnp.bfloat16), (((1,), (0,)), ((), ())),
            preferred_element_type=jnp.float32,
        )
        return higher, total * shrink + jnp.sum(part, 0, keepdims=True)

    top, total = lax.fori_loop(
        span_ref[0, tile], span_ref[1, tile], step,
        (jnp.full((1, rows), LOWEST, jnp.float32), jnp.zeros((1, rows), jnp.float32)),
    )
    log_ref[0, 0] = top + jnp.log(total)
    outs_t = acc[...] * (1.0 / total)
    outs = outs_t.T.astype(jnp.bfloat16)
    outs_t = outs_t.astype(jnp.bfloat16)
    for h in range(count):
        out_t_ref[h * HEAD : (h + 1) * HEAD, :] = outs_t[:, h * tokens : (h + 1) * tokens]
        out_ref[:, h * HEAD : (h + 1) * HEAD] = outs[h * tokens : (h + 1) * tokens]


def attend_back_kernel(
    span_ref, rot_ref, grad_ref, out_ref, log_ref, cos_ref, sin_ref, low_ref, key_ref, value_ref,
    *refs, base, chunk
):
    pre_ref, pre_t_ref, grad_kv_ref, grad_key_ref, grad_value_ref, acc, key_t_ref = refs[-7:]
    tile = pl.program_id(0)
    tokens = rot_ref.shape[0]
    count = rot_ref.shape[1] // HEAD

    @pl.when((tile == 0) & (pl.program_id(1) == 0))
    def _():
        turn(key_ref, key_t_ref, chunk)
        grad_key_ref[...] = jnp.zeros_like(grad_key_ref)
        grad_value_ref[...] = jnp.zeros_like(grad_value_ref)

    query = head_rows(rot_ref[...], count)
    grad = head_rows(grad_ref[...], count)
    outs = head_rows(out_ref[...], count)
    delta = jnp.sum((grad.astype(jnp.float32) * outs.astype(jnp.float32)).T, 0, keepdims=True)
    log_total = log_ref[0, 0]
    low, high = row_bounds(low_ref, base + tile * tokens, tokens, count)
    acc[...] = jnp.zeros_like(acc)

    def step(j, carry):
        start = pl.multiple_of(j * chunk, chunk)
        here = pl.ds(start, chunk)
        scores = lax.dot_general(
            key_ref[here, :], query, (((1,), (1,)), ((), ())), preferred_element_type=jnp.float32
        )
        grad_probs = lax.dot_general(
            value_ref[here, :], grad, (((1,), (1,)), ((), ())), preferred_element_type=jnp.float32
        )
        probs = jnp.where(seen(start, scores.shape, low, high), jnp.exp(scores - log_total), 0.0)
        grad_scores = (probs * (grad_probs - delta)).astype(jnp.bfloat16)
        grad_value_ref[here, :] += jnp.dot(
            probs.astype(jnp.bfloat16), grad, preferred_element_type=jnp.float32
        )
        grad_key_ref[here, :] += jnp.dot(grad_scores, query, preferred_element_type=jnp.float32)
        acc[...] += lax.dot_general(
            key_t_ref[:, here], grad_scores, (((1,), (0,)), ((), ())),
            preferred_element_type=jnp.float32,
        )
        return carry

    lax.fori_loop(span_ref[0, tile], span_ref[1, tile], step, 0)
    cosine, sine = cos_ref[...], sin_ref[...]
    half = HEAD // 2
    for h in range(count):
        own = acc[:, h * tokens : (h + 1) * tokens] * HEAD ** (-0.5)
        first, second = own[:half], own[half:]
        own = jnp.concatenate(
            [first * cosine + second * sine, second * cosine - first * sine], 0
        )
        pre_t_ref[h * HEAD : (h + 1) * HEAD, :] = own.astype(jnp.bfloat16)
        pre_ref[:, h * HEAD : (h + 1) * HEAD] = own.T.astype(jnp.bfloat16)

    @pl.when((tile == pl.num_programs(0) - 1) & (pl.program_id(1) == pl.num_programs(1) - 1))
    def _():
        grad_kv_ref[:, :HEAD] = grad_key_ref[...].astype(jnp.bfloat16)
        grad_kv_ref[:, HEAD:] = grad_value_ref[...].astype(jnp.bfloat16)


def attention_plan(tok_rows, key_count, low):
    tile = min(128, tok_rows)
    chunk = 256 if key_count % 256 == 0 else 128
    base = key_count - tok_rows
    tiles = tok_rows // tile
    begin = low[::tile] // chunk
    end = (base + (jnp.arange(tiles, dtype=jnp.int32) + 1) * tile + chunk - 1) // chunk
    return tile, chunk, base, jnp.stack([begin, end], 0).astype(jnp.int32)


GROUP = 10


def attend(query_pre, cosine, sine, low, window, deps=()):
    tok_rows = query_pre.shape[0]
    key_count = window.shape[0] - tok_rows
    tile, chunk, base, span = attention_plan(tok_rows, key_count, low)
    tiles = tok_rows // tile
    groups = HEADS // GROUP
    wide = GROUP * HEAD
    block = pl.BlockSpec((tile, wide), lambda i, g, s: (i, g))
    angle = pl.BlockSpec((tile, HEAD // 2), lambda i, g, s: (i, 0))
    return pl.pallas_call(
        lambda *refs: attend_kernel(*refs, base=base, chunk=chunk),
        grid_spec=pltpu.PrefetchScalarGridSpec(
            num_scalar_prefetch=1,
            grid=(tiles, groups),
            in_specs=[
                block,
                angle,
                angle,
                pl.BlockSpec((1, 1, tile), lambda i, g, s: (i, 0, 0)),
                pl.BlockSpec((key_count, HEAD), lambda i, g, s: (0, 0)),
                pl.BlockSpec((key_count, HEAD), lambda i, g, s: (0, 1)),
            ]
            + [pl.BlockSpec(memory_space=pl.ANY)] * len(deps),
            out_specs=[
                block,
                pl.BlockSpec((wide, tile), lambda i, g, s: (g, i)),
                block,
                pl.BlockSpec((1, 1, 1, GROUP * tile), lambda i, g, s: (i, g, 0, 0)),
            ],
            scratch_shapes=[
                pltpu.VMEM((HEAD, GROUP * tile), jnp.float32),
                pltpu.VMEM((HEAD, key_count), jnp.bfloat16),
            ],
        ),
        out_shape=[
            jax.ShapeDtypeStruct(query_pre.shape, jnp.bfloat16),
            jax.ShapeDtypeStruct(query_pre.shape[::-1], jnp.bfloat16),
            jax.ShapeDtypeStruct(query_pre.shape, jnp.bfloat16),
            jax.ShapeDtypeStruct((tiles, groups, 1, GROUP * tile), jnp.float32),
        ],
        compiler_params=pltpu.CompilerParams(vmem_limit_bytes=VMEM),
        cost_estimate=FREE,
        name="attend",
    )(span, query_pre, cosine, sine, low.reshape(tiles, 1, tile), window, window, *deps)


def attend_back(query_rot, grad_rows, attn_rows, log_total, cosine_t, sine_t, low, window, deps):
    tok_rows = query_rot.shape[0]
    key_count = window.shape[0] - tok_rows
    tile, chunk, base, span = attention_plan(tok_rows, key_count, low)
    tiles = tok_rows // tile
    groups = HEADS // GROUP
    wide = GROUP * HEAD
    block = pl.BlockSpec((tile, wide), lambda i, g, s: (i, g))
    angle = pl.BlockSpec((HEAD // 2, tile), lambda i, g, s: (0, i))
    return pl.pallas_call(
        lambda *refs: attend_back_kernel(*refs, base=base, chunk=chunk),
        grid_spec=pltpu.PrefetchScalarGridSpec(
            num_scalar_prefetch=1,
            grid=(tiles, groups),
            in_specs=[
                block,
                block,
                block,
                pl.BlockSpec((1, 1, 1, GROUP * tile), lambda i, g, s: (i, g, 0, 0)),
                angle,
                angle,
                pl.BlockSpec((1, 1, tile), lambda i, g, s: (i, 0, 0)),
                pl.BlockSpec((key_count, HEAD), lambda i, g, s: (0, 0)),
                pl.BlockSpec((key_count, HEAD), lambda i, g, s: (0, 1)),
            ]
            + [pl.BlockSpec(memory_space=pl.ANY)] * len(deps),
            out_specs=[
                block,
                pl.BlockSpec((wide, tile), lambda i, g, s: (g, i)),
                pl.BlockSpec((key_count, 2 * HEAD), lambda i, g, s: (0, 0)),
            ],
            scratch_shapes=[
                pltpu.VMEM((key_count, HEAD), jnp.float32),
                pltpu.VMEM((key_count, HEAD), jnp.float32),
                pltpu.VMEM((HEAD, GROUP * tile), jnp.float32),
                pltpu.VMEM((HEAD, key_count), jnp.bfloat16),
            ],
        ),
        out_shape=[
            jax.ShapeDtypeStruct(query_rot.shape, jnp.bfloat16),
            jax.ShapeDtypeStruct(query_rot.shape[::-1], jnp.bfloat16),
            jax.ShapeDtypeStruct((key_count, 2 * HEAD), jnp.bfloat16),
        ],
        compiler_params=pltpu.CompilerParams(vmem_limit_bytes=VMEM),
        cost_estimate=FREE,
        name="attend_back",
    )(
        span, query_rot, grad_rows, attn_rows, log_total, cosine_t, sine_t, low.reshape(tiles, 1, tile),
        window, window, *deps,
    )


def nt(left, right):
    return lax.dot_general(
        left, right, (((1,), (1,)), ((), ())), preferred_element_type=jnp.float32
    )


def tn(left, right):
    return lax.dot_general(
        left, right, (((0,), (0,)), ((), ())), preferred_element_type=jnp.float32
    )


def flat(ref):
    block = ref[...]
    return block.reshape(-1, block.shape[-1])


def units_kernel(core_ref, *refs):
    tokens, cots = refs[0:2], refs[2:4]
    gate_ref, up_ref, down_ref = refs[4:7]
    out_ref = refs[-1]
    gate_rows, up_rows, down_rows = flat(gate_ref), flat(up_ref), flat(down_ref)

    def one(token_ref, cot_ref):
        gate = nt(gate_rows, token_ref[...])
        up = nt(up_rows, token_ref[...])
        grad_mixed = nt(down_rows, cot_ref[...])
        root = (2.0 / jnp.pi) ** 0.5
        square = gate * gate
        curve = jnp.tanh(root * (gate + 0.044715 * (square * gate)))
        upper = 0.5 * (1.0 + curve)
        activated = gate * upper
        slope = upper + 0.5 * gate * (1.0 - curve * curve) * (root * (1.0 + 0.134145 * square))
        out_ref[0] = (grad_mixed * up * slope).astype(jnp.bfloat16)
        out_ref[1] = (grad_mixed * activated).astype(jnp.bfloat16)
        out_ref[2] = (activated * up).astype(jnp.bfloat16)

    for j in (0, 1):
        pl.when(pl.program_id(1) == j)(lambda j=j: one(tokens[j], cots[j]))


def units(tokens, cots, weights, core, group, held, deps=()):
    cols, width = tokens[0].shape
    hidden = weights.hidden
    token_block = pl.BlockSpec((cols, width), lambda i, j, s: (0, 0))
    extra = (() if held is None else (held,)) + tuple(deps)
    return pl.pallas_call(
        units_kernel,
        grid_spec=pltpu.PrefetchScalarGridSpec(
            num_scalar_prefetch=1,
            grid=(2, 2),
            in_specs=[token_block] * 4
            + weights.specs(2, lambda i, j, s: (i, 0), width)
            + [pl.BlockSpec(memory_space=pl.ANY)] * len(extra),
            out_specs=pl.BlockSpec(
                (3, hidden // 2, cols), lambda i, j, s: (0, i, 2 * group + j)
            ),
        ),
        out_shape=jax.ShapeDtypeStruct((3, hidden, 4 * cols), jnp.bfloat16),
        input_output_aliases={} if held is None else {8: 0},
        compiler_params=pltpu.CompilerParams(vmem_limit_bytes=VMEM),
        cost_estimate=FREE,
        name="units",
    )(core, *tokens, *cots, *weights.arrays, *extra)


class OwnWeights:
    def __init__(self, shards):
        self.arrays = tuple(shards)
        self.hidden = shards[0].shape[0] // 2

    def specs(self, cuts, place, width):
        def index(*grid):
            row, col = place(*grid)
            return (grid[-1][0] * cuts + row, col)

        return [pl.BlockSpec((self.hidden // cuts, width), index)] * len(self.arrays)


class FarWeights:
    def __init__(self, gathered):
        parts, count, rows, width = gathered.shape
        self.hidden = parts * rows
        if rows % 16:
            gathered = gathered.reshape(2, parts // 2, count, rows, width)
            gathered = gathered.transpose(0, 2, 1, 3, 4).reshape(2, count, -1, width)
        self.arrays = (gathered,) * count

    def specs(self, cuts, place, width):
        parts, count, rows, _ = self.arrays[0].shape

        def spec(which):
            def index(*grid):
                row, col = place(*grid)
                return (row, which, 0, col)

            return pl.BlockSpec((parts // cuts, 1, rows, width), index)

        return [spec(which) for which in range(count)]


def sums_kernel(core_ref, *refs, count):
    total = 0.0
    for act_ref, weight_ref in zip(refs[:count], refs[count : 2 * count], strict=True):
        total = total + tn(act_ref[0], flat(weight_ref))
    refs[-1][...] = total.astype(jnp.bfloat16)


def sums(acts, weights, core, group, which, block=None, deps=()):
    all_tokens = acts[0].shape[2]
    width = weights[0].arrays[0].shape[-1]
    rows = all_tokens // 4
    blocks = 2 if block is None else 1
    cols = 512 if width % 512 == 0 else width // 2
    first = 2 * group + (block or 0)

    def act_spec(act, kind):
        return pl.BlockSpec((1, act.shape[1], rows), lambda n, t, s: (kind, 0, first + t))

    act_specs, weight_specs, act_args, weight_args = [], [], [], []
    for act, weight in zip(acts, weights, strict=True):
        specs = weight.specs(1, lambda n, t, s: (0, n), cols)
        for kind in which:
            act_specs.append(act_spec(act, kind))
            act_args.append(act)
            weight_specs.append(specs[kind])
            weight_args.append(weight.arrays[kind])
    return pl.pallas_call(
        lambda *refs: sums_kernel(*refs, count=len(act_args)),
        grid_spec=pltpu.PrefetchScalarGridSpec(
            num_scalar_prefetch=1,
            grid=(width // cols, blocks),
            in_specs=act_specs + weight_specs + [pl.BlockSpec(memory_space=pl.ANY)] * len(deps),
            out_specs=pl.BlockSpec((rows, cols), lambda n, t, s: (t, n)),
        ),
        out_shape=jax.ShapeDtypeStruct((blocks * rows, width), jnp.bfloat16),
        compiler_params=pltpu.CompilerParams(vmem_limit_bytes=VMEM),
        cost_estimate=FREE,
        name="sums",
    )(core, *act_args, *weight_args, *deps)


def grams_kernel(acts_ref, *refs, sets):
    out_ref = refs[-1]

    def one(rights):
        step = rights[0].shape[0]
        total = 0.0
        for i, right_ref in enumerate(rights):
            total = total + jnp.dot(
                acts_ref[0, :, i * step : (i + 1) * step], right_ref[...],
                preferred_element_type=jnp.float32,
            )
        out_ref[0] = total.astype(jnp.bfloat16)

    if sets == 1:
        one(refs[0:4])
    else:
        pl.when(pl.program_id(0) < 2)(lambda: one(refs[0:4]))
        pl.when(pl.program_id(0) == 2)(lambda: one(refs[4:8]))


def grams(acts, tokens, cots, pairs, kinds, deps=()):
    _, hidden, all_tokens = acts.shape
    step, width = tokens[0].shape
    cols = width // pairs
    first, count = kinds[0], len(kinds)
    if cols % 128:
        parts = []
        for kind in kinds:
            whole = sum(
                product(acts[kind, :, i * step : (i + 1) * step], right)
                for i, right in enumerate(cots if kind == 2 else tokens)
            )
            parts.append(whole.astype(jnp.bfloat16))
        return jnp.concatenate(parts, 0).reshape(count * hidden, pairs, cols).transpose(1, 0, 2)
    if count == 3:
        specs = [pl.BlockSpec((step, cols), lambda k, p: (0, jnp.where(k < 2, p, pairs - 1)))] * 4
        specs = specs + [pl.BlockSpec((step, cols), lambda k, p: (0, jnp.where(k < 2, 0, p)))] * 4
        rights = tuple(tokens) + tuple(cots)
    else:
        specs = [pl.BlockSpec((step, cols), lambda k, p: (0, p))] * 4
        rights = tuple(cots) if first == 2 else tuple(tokens)
    return pl.pallas_call(
        lambda *refs: grams_kernel(*refs, sets=len(rights) // 4),
        grid=(count, pairs),
        in_specs=[pl.BlockSpec((1, hidden, all_tokens), lambda k, p: (first + k, 0, 0))]
        + specs
        + [pl.BlockSpec(memory_space=pl.ANY)] * len(deps),
        out_specs=pl.BlockSpec((1, hidden, cols), lambda k, p: (p, k, 0)),
        out_shape=jax.ShapeDtypeStruct((pairs, count * hidden, cols), jnp.bfloat16),
        compiler_params=pltpu.CompilerParams(vmem_limit_bytes=VMEM),
        cost_estimate=FREE,
        name="grams",
    )(acts, *rights, *deps)


class Gathered:
    def __init__(self, own, others, shard):
        count, _, rows, width = others.shape
        if rows % 16:
            others = others.transpose(1, 0, 2, 3).reshape(1, -1, count * rows, width)
        self.own, self.others = own, others
        self.shard = shard.reshape(1).astype(jnp.int32)
        self.shards = others.shape[1] + 1

    def place(self, step, shard_ref):
        return lax.rem(shard_ref[0] + self.shards - step, self.shards)

    def specs(self):
        count, _, rows, width = self.others.shape
        return [
            pl.BlockSpec(self.own.shape, lambda r, s: (0, 0)),
            pl.BlockSpec((count, 1, rows, width), lambda r, s: (0, jnp.maximum(r - 1, 0), 0, 0)),
        ]


def by_shard(own_ref, others_ref, use):
    pl.when(pl.program_id(0) == 0)(lambda: use(own_ref[...]))
    pl.when(pl.program_id(0) > 0)(lambda: use(flat(others_ref)))


def spread_kernel(shard_ref, left_ref, own_ref, others_ref, *refs):
    out_ref = refs[-1]

    def use(weight):
        out_ref[...] = nt(left_ref[...], weight).astype(out_ref.dtype)

    by_shard(own_ref, others_ref, use)


def spread(left, weight, dtype, deps=()):
    tokens, width = left.shape
    rows = weight.own.shape[0]
    return pl.pallas_call(
        spread_kernel,
        grid_spec=pltpu.PrefetchScalarGridSpec(
            num_scalar_prefetch=1,
            grid=(weight.shards,),
            in_specs=[pl.BlockSpec((tokens, width), lambda r, s: (0, 0))]
            + weight.specs()
            + [pl.BlockSpec(memory_space=pl.ANY)] * len(deps),
            out_specs=pl.BlockSpec((tokens, rows), lambda r, s: (0, weight.place(r, s))),
        ),
        out_shape=jax.ShapeDtypeStruct((tokens, weight.shards * rows), dtype),
        compiler_params=pltpu.CompilerParams(vmem_limit_bytes=VMEM),
        cost_estimate=FREE,
        name="spread",
    )(weight.shard, left, weight.own, weight.others, *deps)


def collect_kernel(shard_ref, left_ref, own_ref, others_ref, start_ref, gain_ref, *refs, outs):
    refs = refs[-outs:]
    total_ref = refs[0]

    @pl.when(pl.program_id(0) == 0)
    def _():
        total_ref[...] = start_ref[...].astype(jnp.float32)

    def use(weight):
        total_ref[...] += jnp.dot(left_ref[...], weight, preferred_element_type=jnp.float32)

    by_shard(own_ref, others_ref, use)
    if outs > 1:

        @pl.when(pl.program_id(0) == pl.num_programs(0) - 1)
        def _():
            rows = min(128, total_ref.shape[0])

            def norm(i, carry):
                here = pl.ds(pl.multiple_of(i * rows, rows), rows)
                total = total_ref[here, :]
                scale = norm_scale(total)
                refs[1][here, :] = (total * scale * gain_ref[...]).astype(jnp.bfloat16)
                refs[2][here, :] = jnp.broadcast_to(scale, (rows, 128))
                return carry

            lax.fori_loop(0, total_ref.shape[0] // rows, norm, 0)


def collect(left, weight, start, gain=None, deps=()):
    tokens = left.shape[0]
    rows, width = weight.own.shape
    whole = pl.BlockSpec((tokens, width), lambda r, s: (0, 0))
    shapes, specs = [jax.ShapeDtypeStruct((tokens, width), jnp.float32)], [whole]
    if gain is not None:
        shapes.append(jax.ShapeDtypeStruct((tokens, width), jnp.bfloat16))
        shapes.append(jax.ShapeDtypeStruct((tokens, 128), jnp.float32))
        specs.extend([whole, pl.BlockSpec((tokens, 128), lambda r, s: (0, 0))])
    gain_row = jnp.zeros((1, width), jnp.float32) if gain is None else gain.reshape(1, width)
    return pl.pallas_call(
        lambda *refs: collect_kernel(*refs, outs=len(specs)),
        grid_spec=pltpu.PrefetchScalarGridSpec(
            num_scalar_prefetch=1,
            grid=(weight.shards,),
            in_specs=[pl.BlockSpec((tokens, rows), lambda r, s: (0, weight.place(r, s)))]
            + weight.specs()
            + [whole, pl.BlockSpec((1, width), lambda r, s: (0, 0))]
            + [pl.BlockSpec(memory_space=pl.ANY)] * len(deps),
            out_specs=specs,
        ),
        out_shape=shapes,
        compiler_params=pltpu.CompilerParams(vmem_limit_bytes=VMEM),
        cost_estimate=FREE,
        name="collect",
    )(weight.shard, left, weight.own, weight.others, start, gain_row, *deps)


def cross_kernel(core_ref, *refs, lefts, gained, added):
    right_ref, out_ref = refs[lefts], refs[-1]
    first = 0

    def put(part, rows):
        here = (0, slice(None), slice(first, first + rows))
        if added:
            part = part + refs[lefts + 1 + gained][here].astype(jnp.float32)
        out_ref[here] = part.astype(jnp.bfloat16)

    for left_ref in refs[:lefts]:
        shards, _, rows, tokens = left_ref.shape
        left = left_ref[...].reshape(shards * rows, tokens)
        part = jnp.dot(left, right_ref[...], preferred_element_type=jnp.float32)
        put(part.reshape(shards, rows, -1), rows)
        first = first + rows
    if gained:
        gains = refs[lefts + 1][...].astype(jnp.float32)
        put(jnp.broadcast_to(gains[None], (out_ref.shape[1],) + gains.shape), gains.shape[0])


def cross(lefts, right, core, shards, pairs, gains=None, add=None, deps=(), first=0, of=None, into=None):
    tokens, width = right.shape
    cols = width // pairs
    views = [left.reshape(shards, 2, -1, tokens) for left in lefts]
    rows = [view.shape[2] for view in views]
    total = sum(rows) + (0 if gains is None else gains.shape[0])
    if cols % 128:
        picked = jnp.concatenate(
            [lax.dynamic_index_in_dim(view, core[0], 1, keepdims=False) for view in views], 1
        )
        whole = product(picked.reshape(-1, tokens), right).reshape(shards, sum(rows), width)
        if gains is not None:
            extra = jnp.broadcast_to(gains.astype(jnp.float32)[None], (shards,) + gains.shape)
            whole = jnp.concatenate([whole, extra], 1)
        whole = whole.reshape(shards, total, pairs, cols).transpose(2, 0, 1, 3)
        if add is not None:
            whole = whole + add[:, :, first : first + total].astype(jnp.float32)
        whole = whole.astype(jnp.bfloat16)
        if of is None:
            return whole
        if into is None:
            into = jnp.zeros((pairs, shards, of, cols), jnp.bfloat16)
        return lax.dynamic_update_slice(into, whole, (0, 0, first, 0))
    block = pl.BlockSpec((1, shards, total, cols), lambda p, s: (p, 0, first // total, 0))
    kept = () if into is None else (into,)
    specs = [
        pl.BlockSpec((shards, 1, count, tokens), lambda p, s: (0, s[0], 0, 0)) for count in rows
    ]
    specs.append(pl.BlockSpec((tokens, cols), lambda p, s: (0, p)))
    args = [*views, right]
    if gains is not None:
        specs.append(pl.BlockSpec((gains.shape[0], cols), lambda p, s: (0, p)))
        args.append(gains)
    if add is not None:
        specs.append(block)
        args.append(add)
    return pl.pallas_call(
        lambda *refs: cross_kernel(
            *refs, lefts=len(views), gained=gains is not None, added=add is not None
        ),
        grid_spec=pltpu.PrefetchScalarGridSpec(
            num_scalar_prefetch=1,
            grid=(pairs,),
            in_specs=specs + [pl.BlockSpec(memory_space=pl.ANY)] * (len(kept) + len(deps)),
            out_specs=block,
        ),
        out_shape=jax.ShapeDtypeStruct((pairs, shards, of or total, cols), jnp.bfloat16),
        input_output_aliases={1 + len(args): 0} if kept else {},
        compiler_params=pltpu.CompilerParams(vmem_limit_bytes=VMEM),
        cost_estimate=FREE,
        name="cross",
    )(core, *args, *kept, *deps)


def swap(value, axis, bit):
    return lax.ppermute(value, axis, [(i, i ^ bit) for i in range(lax.axis_size(axis))])


def after(value, *others):
    return lax.optimization_barrier((value, *others))[0]


def same_core():
    count = lax.axis_size("ctx")
    return [list(range(0, count, 2)), list(range(1, count, 2))]


def own_part(shard, place):
    part = shard.shape[0] // lax.axis_size("ctx")
    return lax.dynamic_slice_in_dim(shard, place * part, part, 0)


def together(*values):
    return lax.optimization_barrier(values)


def halving_scatter(blocks, axis, place):
    held, bit = blocks, 1
    while held.shape[0] > 1:
        both = held.reshape((held.shape[0] // 2, 2) + held.shape[1:])
        mine = (place // bit) % 2
        keep = lax.dynamic_index_in_dim(both, mine, 1, keepdims=False)
        give = lax.dynamic_index_in_dim(both, 1 - mine, 1, keepdims=False)
        total = keep.astype(jnp.float32) + swap(give, axis, bit).astype(jnp.float32)
        held = total.astype(jnp.bfloat16)
        bit = 2 * bit
    return total[0]


def step_ring(value, axis):
    count = lax.axis_size(axis)
    return lax.ppermute(value, axis, [(i, (i + 1) % count) for i in range(count)])


def ring(value, axis):
    arrived = []
    for _ in range(lax.axis_size(axis) - 1):
        value = step_ring(value, axis)
        arrived.append(value)
    return arrived


def exchanges(axis):
    bits, bit = [], 2
    while bit < lax.axis_size(axis):
        bits.append(bit)
        bit = 2 * bit
    return bits + [1]


def pairs_gather(value):
    pairs = lax.axis_size("ctx") // 2
    if pairs == 4:
        half = value.shape[0] // 2
        x_all, y_all = swap(value, "ctx", 2), swap(value, "ctx", 4)
        low = swap(y_all[:half], "ctx", 2)
        high = swap(x_all[half:], "ctx", 4)
        return [(0, [value]), (2, [x_all]), (4, [y_all]), (6, [low, high])]
    held, bit = [(0, value)], 2
    while bit < 2 * pairs:
        held = held + [(bits ^ bit, swap(item, "ctx", bit)) for bits, item in held]
        bit = 2 * bit
    return [(bits, [item]) for bits, item in held]


def window_gather(value, reach, place):
    rows = value.shape[0]
    out = jnp.zeros(((reach + 2) * rows,) + value.shape[1:], value.dtype)
    parts = [(bits, part, i) for bits, held in pairs_gather(value) for i, part in enumerate(held)]
    for bits, part, i in parts:
        both = ((bits, part), (bits ^ 1, swap(part, "ctx", 1)))
        for other, block in both:
            spot = (place ^ other) - place + reach
            spot = jnp.where((spot < 0) | (spot > reach), reach + 1, spot)
            start = spot * rows + (i * block.shape[0])
            out = lax.dynamic_update_slice_in_dim(out, block, start, 0)
    return out


def place_block(out, block, place):
    return lax.dynamic_update_index_in_dim(out, block, place, 0)


def in_places(own, arrived, place):
    count = len(arrived) + 1
    out = jnp.zeros((count,) + own.shape, own.dtype)
    for step, value in enumerate([own, *arrived]):
        out = lax.dynamic_update_index_in_dim(out, value, lax.rem(place + count - step, count), 0)
    return out


def in_order(gathered, first, part):
    mine = gathered[:, :, first : first + part].transpose(1, 0, 2, 3)
    return mine.reshape(-1, gathered.shape[-1])


def body(
    inputs,
    norm_gains,
    q_weight,
    kv_weight,
    o_weight,
    gate_weight,
    up_weight,
    down_weight,
    cotangent,
    doc_lengths,
):
    x_rows = inputs[0].astype(jnp.float32)
    grad_out = cotangent[0]
    tok_rows, width = x_rows.shape
    place = lax.axis_index("ctx")
    ctx_count = lax.axis_size("ctx")
    pairs = ctx_count // 2
    core = place % 2
    pair = place // 2
    own_core = core.reshape(1).astype(jnp.int32)
    shard = lax.axis_index("fsdp")
    shards = lax.axis_size("fsdp")
    reach = min(ctx_count - 1, (WINDOW + tok_rows - 2) // tok_rows)
    key_count = (reach + 1) * tok_rows
    first_token = place * tok_rows
    token_ids, segment, positions = doc_info(doc_lengths[0], first_token, tok_rows)
    low = jnp.maximum(token_ids - positions, token_ids - (WINDOW - 1)) - (
        first_token - reach * tok_rows
    )
    cosine, sine = rope_angles(positions)
    gain_attn = norm_gains[0]
    gain_mlp = norm_gains[1]

    q_part, kv_part, o_part = (own_part(w, place) for w in (q_weight, kv_weight, o_weight))
    kv_z = in_places(kv_part, ring(kv_part, "fsdp"), shard)
    moving = after(q_part, kv_z)
    held, origins = kv_z[None], [place]
    q_arrived = []
    for bit in exchanges("ctx"):
        if len(q_arrived) < shards - 1:
            moving = step_ring(moving, "fsdp")
            q_arrived.append(moving)
        held = jnp.concatenate([held, swap(held, "ctx", bit)], 0)
        origins = origins + [origin ^ bit for origin in origins]
        held, moving = together(held, moving)
    while len(q_arrived) < shards - 1:
        moving = step_ring(moving, "fsdp")
        q_arrived.append(moving)
    kv_all = jnp.zeros_like(held)
    for step, origin in enumerate(origins):
        kv_all = place_block(kv_all, held[step], origin)
    q_ring = jnp.stack(q_arrived, 0)
    q_ring, kv_all = together(q_ring, kv_all)
    q_all = lax.all_gather(q_ring, "ctx", axis=0)

    half_rows = gate_weight.shape[0] // 2
    part_rows = half_rows // pairs
    cut = (part_rows * 7 // 15 + 15) // 16 * 16
    far_rows, last_rows = cut // 4, part_rows - cut
    mine = jnp.stack(
        [
            lax.dynamic_slice_in_dim(w, core * half_rows + pair * part_rows, part_rows, 0)
            for w in (gate_weight, up_weight, down_weight)
        ],
        0,
    )
    mine, _ = together(mine, q_ring)
    own_weights = OwnWeights((gate_weight, up_weight, down_weight))

    scale_one = norm_scale(x_rows)
    normed_one = (x_rows * scale_one * gain_attn).astype(jnp.bfloat16)
    kv_full = in_order(kv_all, 0, kv_part.shape[0])
    kv_pre = times_rows(normed_one, kv_full)
    key_rot = rotate(kv_pre[:, :HEAD], cosine, sine).astype(jnp.bfloat16)
    kv_local = jnp.concatenate([key_rot, kv_pre[:, HEAD:].astype(jnp.bfloat16)], 1)
    kv_local, moving = together(kv_local, o_part)
    kv_window = window_gather(kv_local, reach, place)
    o_arrived = ring(moving, "fsdp")
    cot_rows = tok_rows // 8
    cot_first = swap(after(grad_out[:cot_rows], o_arrived[-1]), "fsdp", 1)
    far_first = swap(after(mine[:, :far_rows], o_arrived[-1]), "fsdp", 2)
    o_ring = jnp.stack(o_arrived, 0)
    q_all, o_ring, far_first, cot_first, kv_window, normed_one, cosine_t, sine_t = together(
        q_all, o_ring, far_first, cot_first, kv_window, normed_one, cosine.T, sine.T
    )
    o_all = lax.all_gather(o_ring, "ctx", axis=0)
    q_full = Gathered(q_weight, q_all, shard)
    o_full = Gathered(o_weight, o_all, shard)
    far_second = swap(after(mine[:, far_rows : part_rows - last_rows], o_ring), "fsdp", 2)
    cot_second = swap(after(grad_out[cot_rows:], o_ring), "fsdp", 1)
    query_pre = spread(normed_one, q_full, jnp.float32)
    attn_rows, attn_rows_t, query_rot, log_total = attend(
        query_pre, cosine, sine, low, kv_window
    )
    far_last = mine[:, part_rows - last_rows :]
    log_total, cot_second, far_second, far_last = together(
        log_total, cot_second, far_second, far_last
    )
    far_third = swap(far_last, "fsdp", 2)
    near_cots = (grad_out, swap(grad_out, "ctx", 1))
    cot_across = jnp.concatenate([cot_first, cot_second], 0)
    cots = [near_cots, (cot_across, swap(cot_across, "ctx", 1))]

    def over_plane(part):
        return lax.all_gather(part, "ctx", axis=0, axis_index_groups=same_core())

    far_a = FarWeights(
        over_plane(jnp.concatenate([far_first, far_second], 1))
    )
    hidden_one, normed_two, scale_two = collect(attn_rows, o_full, inputs[0], gain_mlp)
    scale_two = scale_two[:, :1]

    near = (normed_two, swap(normed_two, "ctx", 1))
    across = swap(normed_two, "fsdp", 1)
    own_acts = units(near, near_cots, own_weights, own_core, 0, None)
    a_acts = units(near, near_cots, far_a, own_core, 0, None, (own_acts, cots[1][1]))
    across, a_acts, far_third = together(across, a_acts, far_third)
    far = (across, swap(across, "ctx", 1))
    far_b = FarWeights(over_plane(far_third))
    own_acts = units(far, cots[1], own_weights, own_core, 1, own_acts, (a_acts,))
    a_acts = units(far, cots[1], far_a, own_core, 1, a_acts, (own_acts,))
    near_far, cot_rows = near + far, cots[0] + cots[1]

    def over_pairs(blocks):
        mine = lax.psum_scatter(
            blocks, "ctx", scatter_dimension=0, tiled=False, axis_index_groups=same_core()
        )
        return lax.optimization_barrier(mine)

    a_grams = grams(a_acts, near_far, cot_rows, pairs, (0, 1, 2))
    b_acts = units(near, cots[0], far_b, own_core, 0, None, (a_grams,))
    b_acts = units(far, cots[1], far_b, own_core, 1, b_acts)
    b_grams = grams(b_acts, near_far, cot_rows, pairs, (0, 1, 2))
    a_sums, b_sums = over_pairs(a_grams), over_pairs(b_grams)
    acts, weights = (own_acts, a_acts, b_acts), (own_weights, far_a, far_b)

    def group_sums(group, which, block, deps):
        return sums(acts, weights, own_core, group, which, block, deps)

    own_gate_up = grams(own_acts, near_far, cot_rows, pairs, (0, 1), (b_grams,))
    give = group_sums(1, (0, 1), 1, (own_gate_up,))
    own_gate_up = over_pairs(own_gate_up)
    got = swap(give, "ctx", 1)
    near_give = group_sums(0, (0, 1), 1, (give,))
    near_got = swap(near_give, "ctx", 1)
    keep = group_sums(1, (0, 1), 0, (near_give, a_sums))
    total = add16(keep, got)
    moved = swap(total, "fsdp", 1)
    own_down = grams(own_acts, near_far, cot_rows, pairs, (2,), (total, near_got))
    near_keep = group_sums(0, (0, 1), 0, (own_down,))
    out_give = group_sums(1, (2,), 1, (near_keep,))
    out_got = swap(out_give, "ctx", 1)
    out_keep = group_sums(1, (2,), 0, (out_give,))
    moved, own_down, near_keep, out_keep, a_sums = together(
        moved, own_down, near_keep, out_keep, a_sums
    )
    own_down = over_pairs(own_down)
    grad_normed_two = (
        near_keep.astype(jnp.float32) + near_got.astype(jnp.float32) + moved.astype(jnp.float32)
    )
    grad_hidden = grad_out.astype(jnp.float32) + norm_back(
        grad_normed_two, hidden_one, scale_two, gain_mlp
    )
    gain_mlp_grad = jnp.sum(grad_normed_two * hidden_one * scale_two, 0)
    grad_branch = grad_hidden.astype(jnp.bfloat16)
    grad_attended = spread(grad_branch, o_full, jnp.bfloat16, (b_sums,))

    gate_rows = b_sums.shape[0] // 3
    a_all = swap(a_sums, "fsdp", 2)
    grad_query_pre, grad_query_pre_t, grad_kv = attend_back(
        query_rot, grad_attended, attn_rows, log_total, cosine_t, sine_t, low, kv_window,
        (out_keep,),
    )
    grad_stack = grad_kv.reshape(reach + 1, tok_rows, 2 * HEAD)
    moved_kv = [shifted(grad_stack[reach - hop], "ctx", -hop) for hop in range(1, reach + 1)]
    out_moved = swap(add16(out_keep, out_got), "fsdp", 1)
    q_give = cross(
        [grad_query_pre_t], normed_one, 1 - own_core, shards, pairs,
        deps=(grad_kv, a_all, own_gate_up, out_moved),
    )
    q_got = swap(q_give, "ctx", 1)
    q_half, kv_half = q_weight.shape[0] // 2, kv_weight.shape[0] // 2
    okv_rows = q_half + kv_half + 16
    q_sums = cross(
        [grad_query_pre_t], normed_one, own_core, shards, pairs, None, q_got
    )
    q_pairs = over_pairs(q_sums)
    okv_give = cross(
        [attn_rows_t], grad_branch, 1 - own_core, shards, pairs, deps=(q_sums,), of=okv_rows
    )
    moved_kv, okv_give, b_sums = together(moved_kv, okv_give, b_sums)
    b_gate = swap(b_sums[:gate_rows], "fsdp", 2)
    b_up = swap(after(b_sums[gate_rows : 2 * gate_rows], b_gate), "fsdp", 2)
    b_down = swap(after(b_sums[2 * gate_rows :], b_up), "fsdp", 2)
    own_kv_grad = grad_stack[reach].astype(jnp.float32)
    for block in moved_kv:
        own_kv_grad = own_kv_grad + block.astype(jnp.float32)
    grad_kv_pre = jnp.concatenate(
        [rotate_back(own_kv_grad[:, :HEAD], cosine, sine), own_kv_grad[:, HEAD:]], 1
    ).astype(jnp.bfloat16)
    (grad_normed_one,) = collect(
        grad_query_pre, q_full, product(grad_kv_pre, kv_full)
    )
    gain_attn_grad = jnp.sum(grad_normed_one * x_rows * scale_one, 0)
    gains = jnp.stack([gain_attn_grad, gain_mlp_grad], 0).astype(jnp.bfloat16)
    gains = jnp.concatenate([gains, jnp.zeros((14, width), jnp.bfloat16)], 0)
    kv_left = [grad_kv_pre.T]
    okv_give = cross(
        kv_left, normed_one, 1 - own_core, shards, pairs, gains, None, (b_gate,), q_half,
        okv_rows, okv_give,
    )
    okv_got = swap(okv_give, "ctx", 1)
    near_out = sums(acts, weights, own_core, 0, (2,), None, (okv_give,))
    near_out_got = swap(near_out[tok_rows:], "ctx", 1)
    okv_sums = cross(
        [attn_rows_t], grad_branch, own_core, shards, pairs, None, okv_got, (near_out, b_up),
        of=okv_rows,
    )
    okv_sums = cross(
        kv_left, normed_one, own_core, shards, pairs, gains, okv_got, (own_down, q_pairs), q_half, okv_rows,
        okv_sums,
    )
    grad_inputs = grad_hidden + norm_back(grad_normed_one, x_rows, scale_one, gain_attn)

    out_cols = width // ctx_count

    def both_halves(mine):
        keep = lax.dynamic_slice_in_dim(mine, core * out_cols, out_cols, 1)
        give = lax.dynamic_slice_in_dim(mine, (1 - core) * out_cols, out_cols, 1)
        got = swap(give.astype(jnp.bfloat16), "ctx", 1).astype(jnp.float32)
        lower = jnp.where(core == 0, keep, got)
        upper = jnp.where(core == 0, got, keep)
        return jnp.concatenate([lower, upper], 0)

    okv_pairs = over_pairs(okv_sums)
    q_mine = halving_scatter(q_pairs, "fsdp", shard)
    b_down, q_mine = together(b_down, q_mine)
    result = hidden_one + (
        near_out[:tok_rows].astype(jnp.float32)
        + near_out_got.astype(jnp.float32)
        + out_moved.astype(jnp.float32)
    )
    q_grad = both_halves(q_mine)
    okv_mine = halving_scatter(okv_pairs, "fsdp", shard)
    o_grad = both_halves(okv_mine[:q_half])
    kv_grad = both_halves(okv_mine[q_half : q_half + kv_half])
    gain_total = lax.dynamic_slice_in_dim(
        okv_mine[q_half + kv_half : q_half + kv_half + 2], core * out_cols, out_cols, 1
    )

    a_all = a_all.reshape(3, pairs, cut, -1)
    b_all = jnp.concatenate([b_gate, b_up, b_down], 0).reshape(3, pairs, part_rows - cut, -1)
    own_all = (own_gate_up[:half_rows], own_gate_up[half_rows:], own_down)
    mlp_grads = []
    for kind in range(3):
        others = jnp.concatenate([a_all[kind], b_all[kind]], 1).reshape(half_rows, -1)
        mlp_grads.append(
            both_halves(own_all[kind].astype(jnp.float32) + others.astype(jnp.float32))
        )

    return (
        result.astype(jnp.bfloat16)[None],
        grad_inputs.astype(jnp.bfloat16)[None],
        gain_total,
        q_grad,
        kv_grad,
        o_grad,
        mlp_grads[0],
        mlp_grads[1],
        mlp_grads[2],
    )


def solution(mesh):
    in_specs = (
        P("fsdp", "ctx", None),
        P(),
        P("fsdp", None),
        P("fsdp", None),
        P("fsdp", None),
        P("fsdp", None),
        P("fsdp", None),
        P("fsdp", None),
        P("fsdp", "ctx", None),
        P("fsdp", None),
    )
    out_specs = (
        P("fsdp", "ctx", None),
        P("fsdp", "ctx", None),
        P(None, "ctx"),
        P("fsdp", "ctx"),
        P("fsdp", "ctx"),
        P("fsdp", "ctx"),
        P("fsdp", "ctx"),
        P("fsdp", "ctx"),
        P("fsdp", "ctx"),
    )
    return jax.shard_map(body, mesh=mesh, in_specs=in_specs, out_specs=out_specs, check_vma=False)
```
